32 devices in a mesh: fsdp: 32 (over z, y, x, core).
Axes of the slice: x: 2, y: 2, z: 4, core: 2. Of those that a mesh axis runs over, the one named last changes fastest.
Arguments:
- block_input: bfloat16 [4096, 1024], P('fsdp'), may hold values from -6 to 6
- seq_lengths: int32 [48], replicated, may hold values from 32 to 64, as said below
- seq_devices: int32 [48], replicated, may hold values from 0 to 31, as said below
- expert_ids: int32 [4096, 8], P('fsdp'), may hold values from 0 to 31, all different within a row; in each aligned block of 128 rows (0 to 127, 128 to 255, ...) at most 40 rows name the same one
- attn_gain: bfloat16 [1024], P('fsdp'), may hold values from 0.5 to 1.5
- query_weight: bfloat16 [1024, 1024], P('fsdp'), may hold values from -0.1875 to 0.1875
- keyvalue_weight: bfloat16 [1024, 1024], P('fsdp'), may hold values from -0.1875 to 0.1875
- output_weight: bfloat16 [1024, 1024], P('fsdp'), may hold values from -1 to 1
- moe_gain: bfloat16 [1024], P('fsdp'), may hold values from 0.5 to 1.5
- router_weight: bfloat16 [1024, 32], P('fsdp'), may hold values from -0.09375 to 0.09375
- gate_weight: bfloat16 [16384, 1024], P('fsdp'), may hold values from -0.1875 to 0.1875
- up_weight: bfloat16 [16384, 1024], P('fsdp'), may hold values from -0.1875 to 0.1875
- down_weight: bfloat16 [16384, 1024], P('fsdp'), may hold values from -0.75 to 0.75
- output_grad: bfloat16 [4096, 1024], P('fsdp'), may hold values from -6 to 6
Outputs:
- block_output: bfloat16 [4096, 1024], P('fsdp')
- input_grad: float32 [4096, 1024], P('fsdp')
- attn_gain_grad: float32 [1024], P('fsdp')
- query_grad: float32 [1024, 1024], P('fsdp')
- keyvalue_grad: float32 [1024, 1024], P('fsdp')
- output_weight_grad: float32 [1024, 1024], P('fsdp')
- moe_gain_grad: float32 [1024], P('fsdp')
- router_grad: float32 [1024, 32], P('fsdp')
- gate_grad: float32 [16384, 1024], P('fsdp')
- up_grad: float32 [16384, 1024], P('fsdp')
- down_grad: float32 [16384, 1024], P('fsdp')
The draws below stay inside these ranges and needn't reach their ends.
Inputs may be any that keep to these rules, and one draw needn't show every extreme that they name: `seq_lengths`: no device holds more than 2 sequences, so one device's lengths sum to 128 or less; in every draw one device holds 2 sequences of 64 rows. `seq_devices`: no device index is named more than 2 times; one is named exactly 2 times. `expert_ids`: each row names 8 different experts. Within the rows of one device no expert is named by more than 40 rows, and in some device's rows one expert is named by exactly 40.
All inputs are finite; a program needn't handle non-finite values.
Results may differ from the reference program's by a relative error of at most 0.013.
The reference program's roundings to bfloat16 on the way count: a program that leaves them out, or rounds other values in their place, can miss the bound.
Values may be sent and summed in bfloat16 or wider, within the bound.
No kernel may reach another device: no remote copies, remote signals or barrier semaphores. Data moves between devices by JAX's collectives and lax.ppermute only.
A program may use at most 640 MiB of HBM per device.

```python
import math
from functools import partial
import jax
import jax.numpy as jnp
import numpy as np
from jax import lax

MODEL_DIMENSION = 1024
QUERY_HEADS = 16
KEY_VALUE_HEADS = 8
HEAD_WIDTH = 64
EXPERT_COUNT = 32
EXPERT_HIDDEN = 512
TOPK = 8
SEQ_CAP = 2
TOK_DEV = 128
LEN_MAX = 64
CAP = 40
NSEQ = 48
TOKENS = 4096
N_FSDP = 32


def sequence_plan(key):
    slot_count = N_FSDP * SEQ_CAP
    order = jax.random.permutation(jax.random.fold_in(key, 31), slot_count).astype(jnp.int32)
    chosen = order[0] // SEQ_CAP
    later = (order // SEQ_CAP != chosen).astype(jnp.int32)
    ranked = order[jnp.argsort(later, stable=True)]
    devices_of = (ranked[:NSEQ] // SEQ_CAP).astype(jnp.int32)
    lengths = jax.random.randint(jax.random.fold_in(key, 37), (NSEQ,), LEN_MAX // 2, LEN_MAX + 1).astype(jnp.int32)
    lengths = jnp.where(devices_of == chosen, LEN_MAX, lengths)
    lengths = lengths.at[NSEQ - 1].set(LEN_MAX // 2)
    return (lengths.astype(jnp.int32), devices_of)


def draw_seq_lengths(key, part):
    return sequence_plan(key)[0]


def draw_seq_devices(key, part):
    return sequence_plan(key)[1]


def level_of(stream_key, dims, pieces, low, largest):
    gain = 1.0
    for dim, shards_of in pieces:
        heights = jax.random.uniform(jax.random.fold_in(jax.random.fold_in(stream_key, 6), dim), (shards_of,), jnp.float32, low / len(pieces), largest / len(pieces))
        gain = gain * jnp.repeat(jnp.exp(heights), dims[dim] // shards_of).reshape((-1,) + (1,) * (len(dims) - 1 - dim))
    return gain


def shared_out(stream_key, own, number, rows, amount, top, most, slope):
    order = jax.random.permutation(stream_key, amount)
    crowded, common = shares(amount, rows * top, most, slope, True), shares(amount, rows * top, most, slope, False)
    places = jnp.arange(amount)

    def named(tallies, rotation):
        used = int((tallies > 0).sum())
        fixed = max(1, used // 4)
        moved = fixed + (places - fixed + rotation * (used - fixed)) % max(1, amount - fixed)
        return jnp.zeros((amount,), jnp.int32).at[order[jnp.where(places < fixed, places, moved)]].set(jnp.asarray(tallies, jnp.int32))

    tallies = jnp.where(number % 4 == 0, named(crowded, number // 4), named(common, number - number // 4 - 1))
    mixed = jax.random.permutation(jax.random.fold_in(own, 3), amount)
    source_of, receiver = mixed[0:amount // 2 * 2:2], mixed[1:amount // 2 * 2:2]
    room = jnp.minimum(tallies[source_of] - 1, most - tallies[receiver]) // 2
    room = jnp.where((source_of == order[0]) | (receiver == order[0]) | (tallies[receiver] == 0), 0, jnp.maximum(room, 0))
    moved = jax.random.randint(jax.random.fold_in(own, 4), (amount // 2,), 0, 1 << 20) % (room + 1)
    tallies = tallies.at[source_of].add(-moved).at[receiver].add(moved)
    labels = jnp.searchsorted(jnp.cumsum(tallies), jnp.arange(rows * top), side="right").astype(jnp.int32)
    listing = labels.reshape(top, rows).T
    listing = listing[jax.random.permutation(jax.random.fold_in(own, 1), rows)]
    rotation = jax.random.randint(jax.random.fold_in(own, 2), (rows, 1), 0, top)
    return jnp.take_along_axis(listing, (jnp.arange(top)[None, :] + rotation) % top, axis=1)


def shares(amount, total, most, slope, full):
    weights = [(1 << 20) // math.isqrt(standing ** slope) + 1 for standing in range(1, amount + 1)]
    largest = most if full else min(most, max(-(-total // amount), total * weights[0] // sum(weights)))
    least = 1 if total - largest >= amount - 1 else 0
    given, surplus = [largest] + [least] * (amount - 1), total - largest - least * (amount - 1)
    while surplus > 0:
        candidates = [i for i in range(1, amount) if given[i] < largest] or [i for i in range(1, amount) if given[i] < most]
        mass, budget = sum([weights[i] for i in candidates]), surplus
        for i in candidates:
            addition = min(most - given[i], max(1, budget * weights[i] // mass), surplus)
            given[i] = given[i] + addition
            surplus = surplus - addition
    return np.array(given)


def scatter_about(own_key, shape, spread, most, cuts=(), held_as=jnp.bfloat16):
    factor_of = level_of(own_key, shape, cuts, -0.22, 0.18) if cuts else 1.0
    entries = jax.random.normal(own_key, shape, jnp.float32) * spread * factor_of
    return jnp.minimum(jnp.maximum(entries, -most), most).astype(held_as)


def setup_inputs(seed: int = 0) -> dict:
    streams_of = jax.random.split(jax.random.key(seed), 15)
    block_input = scatter_about(streams_of[0], (TOKENS, MODEL_DIMENSION), 1.0, 6.0, ((0, 32),))
    seq_lengths = draw_seq_lengths(jax.random.fold_in(streams_of[14], 71), 0)
    seq_devices = draw_seq_devices(jax.random.fold_in(streams_of[14], 71), 0)
    expert_ids_keys = jax.random.split(jax.random.fold_in(streams_of[3], 1), TOKENS // TOK_DEV)
    expert_ids_turns = jax.random.permutation(jax.random.fold_in(streams_of[3], 3), TOKENS // TOK_DEV)
    expert_ids = jax.vmap(lambda own, number: shared_out(jax.random.fold_in(streams_of[3], 2), own, number, TOK_DEV, EXPERT_COUNT, TOPK, CAP, 1))(expert_ids_keys, expert_ids_turns).reshape((TOKENS, TOPK))
    attn_gain = jnp.clip(1.0 + 0.1 * jax.random.normal(streams_of[4], (MODEL_DIMENSION,), jnp.float32), 0.5, 1.5).astype(jnp.bfloat16)
    query_weight = scatter_about(streams_of[5], (MODEL_DIMENSION, QUERY_HEADS * HEAD_WIDTH), MODEL_DIMENSION ** -0.5, 0.1875, ((0, 32),))
    keyvalue_weight = scatter_about(streams_of[6], (MODEL_DIMENSION, 2 * KEY_VALUE_HEADS * HEAD_WIDTH), MODEL_DIMENSION ** -0.5, 0.1875, ((0, 32),))
    output_weight = scatter_about(streams_of[7], (QUERY_HEADS * HEAD_WIDTH, MODEL_DIMENSION), (QUERY_HEADS * HEAD_WIDTH // 32) ** -0.5, 1.0, ((0, 32),))
    moe_gain = jnp.clip(1.0 + 0.1 * jax.random.normal(streams_of[8], (MODEL_DIMENSION,), jnp.float32), 0.5, 1.5).astype(jnp.bfloat16)
    router_weight = scatter_about(streams_of[9], (MODEL_DIMENSION, EXPERT_COUNT), (4 * MODEL_DIMENSION) ** -0.5, 0.09375, ((0, 32),))
    gate_weight = scatter_about(streams_of[10], (EXPERT_COUNT * EXPERT_HIDDEN, MODEL_DIMENSION), MODEL_DIMENSION ** -0.5, 0.1875, ((0, 32),))
    up_weight = scatter_about(streams_of[11], (EXPERT_COUNT * EXPERT_HIDDEN, MODEL_DIMENSION), MODEL_DIMENSION ** -0.5, 0.1875, ((0, 32),))
    down_weight = scatter_about(streams_of[12], (EXPERT_COUNT * EXPERT_HIDDEN, MODEL_DIMENSION), (EXPERT_HIDDEN // 8) ** -0.5, 0.75, ((0, 32),))
    output_grad = scatter_about(streams_of[13], (TOKENS, MODEL_DIMENSION), 1.0, 6.0, ((0, 32),))
    return dict(block_input=block_input, seq_lengths=seq_lengths, seq_devices=seq_devices, expert_ids=expert_ids, attn_gain=attn_gain, query_weight=query_weight, keyvalue_weight=keyvalue_weight, output_weight=output_weight, moe_gain=moe_gain, router_weight=router_weight, gate_weight=gate_weight, up_weight=up_weight, down_weight=down_weight, output_grad=output_grad)


EPS = 1e-06
ROPE_BASE = 10000.0

def layout(seq_lengths, seq_devices, device, count_of_rows):
    on_device = seq_devices == device
    lengths = jnp.where(on_device, seq_lengths, 0).astype(jnp.int32)
    starts = (jnp.cumsum(lengths) - lengths).astype(jnp.int32)
    filled_rows = jnp.sum(lengths).astype(jnp.int32)
    row_slots = jnp.arange(count_of_rows, dtype=jnp.int32)
    inside = (row_slots[:, None] >= starts[None, :]) & (row_slots[:, None] < (starts + lengths)[None, :])
    live_rows = jnp.any(inside, axis=1)
    seq_count = seq_lengths.shape[0]
    numbers = jnp.arange(seq_count, dtype=jnp.int32)
    segment = jnp.where(live_rows, lax.optimization_barrier(jnp.sum(jnp.where(inside, numbers[None, :], 0), axis=1)), seq_count).astype(jnp.int32)
    begins = jnp.where(live_rows, lax.optimization_barrier(jnp.sum(jnp.where(inside, starts[None, :], 0), axis=1)), filled_rows).astype(jnp.int32)
    return (live_rows, segment, (row_slots - begins).astype(jnp.int32))

def rope_tables(position, head_dim):
    half_dim = head_dim // 2
    inverse = ROPE_BASE ** (-(jnp.arange(half_dim, dtype=jnp.float32) * 2.0) / head_dim)
    angles = position.astype(jnp.float32)[:, None] * inverse[None, :]
    return (jnp.cos(angles)[:, None, :], jnp.sin(angles)[:, None, :])

def rotate(values, cosine, sine_part, head_dim):
    count_of_rows = values.shape[0]
    shaped = values.reshape(count_of_rows, -1, head_dim)
    half_dim = head_dim // 2
    first_half = shaped[..., :half_dim]
    second_half = shaped[..., half_dim:]
    turned = jnp.concatenate([first_half * cosine - second_half * sine_part, second_half * cosine + first_half * sine_part], axis=-1)
    return turned.reshape(count_of_rows, -1)

def norm_forward(hidden, gain_vec):
    inv_rms = lax.rsqrt(lax.optimization_barrier(jnp.mean(hidden * hidden, axis=-1, keepdims=True)) + EPS)
    unit_rows = hidden * inv_rms
    return (unit_rows * gain_vec.astype(jnp.float32), unit_rows, inv_rms)

def norm_backward(grad_norm, gain_vec, unit_rows, inv_rms):
    grad_unit = grad_norm * gain_vec.astype(jnp.float32)
    grad_gain = lax.optimization_barrier(jnp.sum(grad_norm * unit_rows, axis=0))
    grad_hidden = inv_rms * (grad_unit - unit_rows * lax.optimization_barrier(jnp.mean(grad_unit * unit_rows, axis=-1, keepdims=True)))
    return (grad_hidden, grad_gain)

def dispatch(expert_ids, experts, capacity):
    count_of_rows, top_count = expert_ids.shape
    flat_ids = expert_ids.reshape(-1)
    one_hot = (flat_ids[:, None] == jnp.arange(experts, dtype=jnp.int32)[None, :]).astype(jnp.int32)
    earlier = (jnp.cumsum(one_hot, axis=0) - one_hot).astype(jnp.int32)
    order_in = lax.optimization_barrier(jnp.sum(earlier * one_hot, axis=1)).astype(jnp.int32)
    pair_slot = (flat_ids * capacity + order_in).astype(jnp.int32)
    pair_token = (jnp.arange(count_of_rows * top_count, dtype=jnp.int32) // top_count).astype(jnp.int32)
    slot_token = jnp.zeros((experts * capacity,), jnp.int32).at[pair_slot].set(pair_token)
    slot_used = jnp.zeros((experts * capacity,), jnp.int32).at[pair_slot].set(1) > 0
    return (pair_slot, slot_token, slot_used)

def head_forward(operands, allowed):
    query_rows, keys_head, values_head = operands
    scale_factor = query_rows.shape[-1] ** (-0.5)
    scores = jnp.einsum('qgd,kd->gqk', query_rows.astype(jnp.float32), keys_head.astype(jnp.float32)) * scale_factor
    scores = jnp.where(allowed[None], scores, -jnp.inf)
    highest = lax.optimization_barrier(jnp.max(scores, axis=-1, keepdims=True))
    totals = lax.optimization_barrier(jnp.sum(jnp.exp(scores - highest), axis=-1, keepdims=True))
    log_total = highest + jnp.log(totals)
    prob_bf = jnp.exp(scores - log_total).astype(jnp.bfloat16)
    mixed_out = jnp.einsum('gqk,kd->qgd', prob_bf.astype(jnp.float32), values_head.astype(jnp.float32)).astype(jnp.bfloat16)
    return (mixed_out, log_total[..., 0])

def head_backward(operands, allowed):
    query_rows, keys_head, values_head, mixed_out, grad_mixed, log_total = operands
    scale_factor = query_rows.shape[-1] ** (-0.5)
    query_f = query_rows.astype(jnp.float32)
    key_f = keys_head.astype(jnp.float32)
    grad_f = grad_mixed.astype(jnp.float32)
    scores = jnp.einsum('qgd,kd->gqk', query_f, key_f) * scale_factor
    prob_full = jnp.where(allowed[None], jnp.exp(scores - log_total[..., None]), 0.0)
    prob_bf = prob_full.astype(jnp.bfloat16)
    grad_values = jnp.einsum('gqk,qgd->kd', prob_bf.astype(jnp.float32), grad_f)
    grad_probs = jnp.einsum('qgd,kd->gqk', grad_f, values_head.astype(jnp.float32))
    inner = lax.optimization_barrier(jnp.sum(grad_f * mixed_out.astype(jnp.float32), axis=-1)).transpose(1, 0)
    grad_scores = (prob_full * (grad_probs - inner[..., None])).astype(jnp.bfloat16).astype(jnp.float32)
    grad_queries = jnp.einsum('gqk,kd->qgd', grad_scores, key_f) * scale_factor
    grad_keys = jnp.einsum('gqk,qgd->kd', grad_scores, query_f) * scale_factor
    return (grad_queries, grad_keys, grad_values)

def device_pass(device, block_rows, cot_rows, id_rows, seq_lengths, seq_devices, dense_params, tables):
    attn_gain, query_weight, keyvalue_weight, output_weight, moe_gain, router_weight = dense_params
    gate_table, up_table, down_table = tables
    count_of_rows, model_width = block_rows.shape
    query_group_width = QUERY_HEADS // KEY_VALUE_HEADS
    key_value_columns = KEY_VALUE_HEADS * HEAD_WIDTH
    live_rows, segment, position = layout(seq_lengths, seq_devices, device, count_of_rows)
    row_slots = jnp.arange(count_of_rows, dtype=jnp.int32)
    allowed = (segment[:, None] == segment[None, :]) & (row_slots[:, None] >= row_slots[None, :])
    cosine, sine_part = rope_tables(position, HEAD_WIDTH)
    input_f = block_rows.astype(jnp.float32)
    attn_norm, attn_unit, attn_rms = norm_forward(input_f, attn_gain)
    attn_in = attn_norm.astype(jnp.bfloat16)
    query_pre = jnp.dot(attn_in, query_weight, preferred_element_type=jnp.float32)
    kv_pre = jnp.dot(attn_in, keyvalue_weight, preferred_element_type=jnp.float32)
    query_rows = rotate(query_pre, cosine, sine_part, HEAD_WIDTH).astype(jnp.bfloat16)
    gathered_keys = rotate(kv_pre[:, :key_value_columns], cosine, sine_part, HEAD_WIDTH).astype(jnp.bfloat16)
    gathered_values = kv_pre[:, key_value_columns:].astype(jnp.bfloat16)
    query_head_rows = query_rows.reshape(count_of_rows, KEY_VALUE_HEADS, query_group_width, HEAD_WIDTH).transpose(1, 0, 2, 3)
    key_head_rows = gathered_keys.reshape(count_of_rows, KEY_VALUE_HEADS, HEAD_WIDTH).transpose(1, 0, 2)
    value_head_rows = gathered_values.reshape(count_of_rows, KEY_VALUE_HEADS, HEAD_WIDTH).transpose(1, 0, 2)
    mixed_heads, log_totals = lax.map(partial(head_forward, allowed=allowed), (query_head_rows, key_head_rows, value_head_rows))
    attn_heads = mixed_heads.transpose(1, 0, 2, 3).reshape(count_of_rows, QUERY_HEADS * HEAD_WIDTH)
    residual = input_f + jnp.dot(attn_heads, output_weight, preferred_element_type=jnp.float32)
    moe_norm, moe_unit, moe_rms = norm_forward(residual, moe_gain)
    moe_in = moe_norm.astype(jnp.bfloat16)
    logits = jnp.dot(moe_in, router_weight, preferred_element_type=jnp.float32)
    picker = id_rows[:, :, None] == jnp.arange(EXPERT_COUNT, dtype=jnp.int32)[None, None, :]
    chosen = lax.optimization_barrier(jnp.sum(jnp.where(picker, logits[:, None, :], 0.0), axis=-1))
    raised = jnp.exp(chosen)
    route_weights = raised / lax.optimization_barrier(jnp.sum(raised, axis=-1, keepdims=True))
    pair_slot, slot_token, slot_used = dispatch(id_rows, EXPERT_COUNT, CAP)
    slot_inputs = jnp.where(slot_used[:, None], moe_in[slot_token], jnp.zeros((), jnp.bfloat16)).reshape(EXPERT_COUNT, CAP, model_width)
    inputs_f = slot_inputs.astype(jnp.float32)
    gate_pre = jnp.einsum('ecd,ehd->ech', inputs_f, gate_table)
    up_pre = jnp.einsum('ecd,ehd->ech', inputs_f, up_table)
    activation = (jax.nn.silu(gate_pre) * up_pre).astype(jnp.bfloat16)
    slot_outputs = jnp.einsum('ech,ehd->ecd', activation.astype(jnp.float32), down_table)
    picked = slot_outputs.reshape(EXPERT_COUNT * CAP, model_width)[pair_slot].reshape(count_of_rows, TOPK, model_width)
    moe_out = lax.optimization_barrier(jnp.sum(route_weights[:, :, None] * picked, axis=1))
    live_col = live_rows[:, None]
    block_output = jnp.where(live_col, residual + moe_out, 0.0).astype(jnp.bfloat16)
    out_cot = jnp.where(live_col, cot_rows.astype(jnp.float32), 0.0)
    route_grad = lax.optimization_barrier(jnp.sum(out_cot[:, None, :] * picked, axis=-1))
    chosen_grad = route_weights * (route_grad - lax.optimization_barrier(jnp.sum(route_weights * route_grad, axis=-1, keepdims=True)))
    logit_grad = lax.optimization_barrier(jnp.sum(jnp.where(picker, chosen_grad[:, :, None], 0.0), axis=1)).astype(jnp.bfloat16)
    slot_weight = jnp.zeros((EXPERT_COUNT * CAP,), jnp.float32).at[pair_slot].set(route_weights.reshape(-1))
    slot_cot = jnp.where(slot_used[:, None], out_cot[slot_token] * slot_weight[:, None], 0.0).astype(jnp.bfloat16).reshape(EXPERT_COUNT, CAP, model_width)
    cot_f = slot_cot.astype(jnp.float32)
    act_grad = jnp.einsum('ecd,ehd->ech', cot_f, down_table)
    sigma = jax.nn.sigmoid(gate_pre)
    gate_pre_grad = (act_grad * up_pre * sigma * (1.0 + gate_pre * (1.0 - sigma))).astype(jnp.bfloat16).astype(jnp.float32)
    up_pre_grad = (act_grad * gate_pre * sigma).astype(jnp.bfloat16).astype(jnp.float32)
    slot_in_grads = jnp.einsum('ech,ehd->ecd', gate_pre_grad, gate_table) + jnp.einsum('ech,ehd->ecd', up_pre_grad, up_table)
    gate_grad = jnp.einsum('ech,ecd->ehd', gate_pre_grad, inputs_f).reshape(EXPERT_COUNT * EXPERT_HIDDEN, model_width)
    up_grad = jnp.einsum('ech,ecd->ehd', up_pre_grad, inputs_f).reshape(EXPERT_COUNT * EXPERT_HIDDEN, model_width)
    down_grad = jnp.einsum('ech,ecd->ehd', activation.astype(jnp.float32), cot_f).reshape(EXPERT_COUNT * EXPERT_HIDDEN, model_width)
    in_grads_flat = slot_in_grads.reshape(EXPERT_COUNT * CAP, model_width)
    moe_in_grad = lax.optimization_barrier(jnp.sum(in_grads_flat[pair_slot].reshape(count_of_rows, TOPK, model_width), axis=1)) + jnp.dot(logit_grad, router_weight.T, preferred_element_type=jnp.float32)
    router_grad = jnp.dot(moe_in.T, logit_grad, preferred_element_type=jnp.float32)
    resid_part, moe_gain_grad = norm_backward(moe_in_grad, moe_gain, moe_unit, moe_rms)
    residual_grad = out_cot + resid_part
    residual_bf = residual_grad.astype(jnp.bfloat16)
    output_weight_grad = jnp.dot(attn_heads.T, residual_bf, preferred_element_type=jnp.float32)
    gradient_per_head = jnp.dot(residual_bf, output_weight.T, preferred_element_type=jnp.float32).astype(jnp.bfloat16)
    head_gradients = gradient_per_head.reshape(count_of_rows, KEY_VALUE_HEADS, query_group_width, HEAD_WIDTH).transpose(1, 0, 2, 3)
    grad_q, grad_k, grad_v = lax.map(partial(head_backward, allowed=allowed), (query_head_rows, key_head_rows, value_head_rows, mixed_heads, head_gradients, log_totals))
    query_rot_grad = grad_q.transpose(1, 0, 2, 3).reshape(count_of_rows, QUERY_HEADS * HEAD_WIDTH)
    key_rot_grad = grad_k.transpose(1, 0, 2).reshape(count_of_rows, key_value_columns)
    value_grad = grad_v.transpose(1, 0, 2).reshape(count_of_rows, key_value_columns)
    query_pre_grad = rotate(query_rot_grad, cosine, -sine_part, HEAD_WIDTH).astype(jnp.bfloat16)
    kv_pre_grad = jnp.concatenate([rotate(key_rot_grad, cosine, -sine_part, HEAD_WIDTH), value_grad], axis=1).astype(jnp.bfloat16)
    query_grad = jnp.dot(attn_in.T, query_pre_grad, preferred_element_type=jnp.float32)
    keyvalue_grad = jnp.dot(attn_in.T, kv_pre_grad, preferred_element_type=jnp.float32)
    attn_in_grad = jnp.dot(query_pre_grad, query_weight.T, preferred_element_type=jnp.float32) + jnp.dot(kv_pre_grad, keyvalue_weight.T, preferred_element_type=jnp.float32)
    input_part, attn_gain_grad = norm_backward(attn_in_grad, attn_gain, attn_unit, attn_rms)
    input_grad = jnp.where(live_col, residual_grad + input_part, 0.0)
    return ((block_output, input_grad), (attn_gain_grad, query_grad, keyvalue_grad, output_weight_grad, moe_gain_grad, router_grad, gate_grad, up_grad, down_grad))

def reference(block_input, seq_lengths, seq_devices, expert_ids, attn_gain, query_weight, keyvalue_weight, output_weight, moe_gain, router_weight, gate_weight, up_weight, down_weight, output_grad):
    tables = (gate_weight.astype(jnp.float32).reshape(EXPERT_COUNT, EXPERT_HIDDEN, MODEL_DIMENSION), up_weight.astype(jnp.float32).reshape(EXPERT_COUNT, EXPERT_HIDDEN, MODEL_DIMENSION), down_weight.astype(jnp.float32).reshape(EXPERT_COUNT, EXPERT_HIDDEN, MODEL_DIMENSION))
    dense_params = (attn_gain, query_weight, keyvalue_weight, output_weight, moe_gain, router_weight)
    inputs = block_input.reshape(N_FSDP, TOK_DEV, MODEL_DIMENSION)
    cot_blocks = output_grad.reshape(N_FSDP, TOK_DEV, MODEL_DIMENSION)
    route_blocks = expert_ids.reshape(N_FSDP, TOK_DEV, TOPK)
    zeroed_gradients = (jnp.zeros((MODEL_DIMENSION,), jnp.float32), jnp.zeros((MODEL_DIMENSION, QUERY_HEADS * HEAD_WIDTH), jnp.float32), jnp.zeros((MODEL_DIMENSION, 2 * KEY_VALUE_HEADS * HEAD_WIDTH), jnp.float32), jnp.zeros((QUERY_HEADS * HEAD_WIDTH, MODEL_DIMENSION), jnp.float32), jnp.zeros((MODEL_DIMENSION,), jnp.float32), jnp.zeros((MODEL_DIMENSION, EXPERT_COUNT), jnp.float32), jnp.zeros((EXPERT_COUNT * EXPERT_HIDDEN, MODEL_DIMENSION), jnp.float32), jnp.zeros((EXPERT_COUNT * EXPERT_HIDDEN, MODEL_DIMENSION), jnp.float32), jnp.zeros((EXPERT_COUNT * EXPERT_HIDDEN, MODEL_DIMENSION), jnp.float32))

    def per_device(running, scan_item):
        device, block_rows, cot_rows, id_rows = scan_item
        outputs, grads = device_pass(device, block_rows, cot_rows, id_rows, seq_lengths, seq_devices, dense_params, tables)
        return (tuple((total_part + grad_part for total_part, grad_part in zip(running, grads))), outputs)
    sums, (block_outs, in_grads) = lax.scan(per_device, zeroed_gradients, (jnp.arange(N_FSDP, dtype=jnp.int32), inputs, cot_blocks, route_blocks))
    return (block_outs.reshape(TOKENS, MODEL_DIMENSION), in_grads.reshape(TOKENS, MODEL_DIMENSION), sums[0], sums[1], sums[2], sums[3], sums[4], sums[5], sums[6], sums[7], sums[8])
```

```python
from functools import partial

import jax
import jax.numpy as jnp
from jax import lax
from jax.sharding import PartitionSpec as P

QUERY_HEADS = 16
KEY_VALUE_HEADS = 8
HEAD_WIDTH = 64
EXPERT_COUNT = 32
EXPERT_HIDDEN = 512
TOPK = 8
CAP = 40


EPS = 1e-06
ROPE_BASE = 10000.0


def layout(seq_lengths, seq_devices, device, count_of_rows):
    on_device = seq_devices == device
    lengths = jnp.where(on_device, seq_lengths, 0)
    starts = jnp.cumsum(lengths) - lengths
    filled_rows = jnp.sum(lengths)
    row_slots = jnp.arange(count_of_rows, dtype=jnp.int32)
    inside = (row_slots[:, None] >= starts[None, :]) & (
        row_slots[:, None] < (starts + lengths)[None, :]
    )
    live_rows = jnp.any(inside, axis=1)
    seq_count = seq_lengths.shape[0]
    numbers = jnp.arange(seq_count, dtype=jnp.int32)
    segment = jnp.where(
        live_rows, jnp.sum(jnp.where(inside, numbers[None, :], 0), axis=1), seq_count
    )
    begins = jnp.where(
        live_rows, jnp.sum(jnp.where(inside, starts[None, :], 0), axis=1), filled_rows
    )
    return (live_rows, segment, row_slots - begins)


def rope_tables(position, head_dim):
    half_dim = head_dim // 2
    inverse = ROPE_BASE ** (-(jnp.arange(half_dim, dtype=jnp.float32) * 2.0) / head_dim)
    angles = position.astype(jnp.float32)[:, None] * inverse[None, :]
    return (jnp.cos(angles)[:, None, :], jnp.sin(angles)[:, None, :])


def rotate(values, cosine, sine_part, head_dim):
    count_of_rows = values.shape[0]
    shaped = values.reshape(count_of_rows, -1, head_dim)
    half_dim = head_dim // 2
    first_half = shaped[..., :half_dim]
    second_half = shaped[..., half_dim:]
    turned = jnp.concatenate(
        [
            first_half * cosine - second_half * sine_part,
            second_half * cosine + first_half * sine_part,
        ],
        axis=-1,
    )
    return turned.reshape(count_of_rows, -1)


def norm_forward(hidden, gain_vec):
    inv_rms = lax.rsqrt(jnp.mean(hidden * hidden, axis=-1, keepdims=True) + EPS)
    unit_rows = hidden * inv_rms
    return (unit_rows * gain_vec.astype(jnp.float32), unit_rows, inv_rms)


def norm_backward(grad_norm, gain_vec, unit_rows, inv_rms):
    grad_unit = grad_norm * gain_vec.astype(jnp.float32)
    grad_gain = jnp.sum(grad_norm * unit_rows, axis=0)
    grad_hidden = inv_rms * (
        grad_unit - unit_rows * jnp.mean(grad_unit * unit_rows, axis=-1, keepdims=True)
    )
    return (grad_hidden, grad_gain)


def head_forward(operands, allowed):
    query_rows, keys_head, values_head = operands
    scale_factor = query_rows.shape[-1] ** (-0.5)
    scores = (
        jnp.einsum("qgd,kd->gqk", query_rows, keys_head, preferred_element_type=jnp.float32)
        * scale_factor
    )
    scores = jnp.where(allowed[None], scores, -jnp.inf)
    highest = jnp.max(scores, axis=-1, keepdims=True)
    totals = jnp.sum(jnp.exp(scores - highest), axis=-1, keepdims=True)
    log_total = highest + jnp.log(totals)
    prob_bf = jnp.exp(scores - log_total).astype(jnp.bfloat16)
    mixed_out = jnp.einsum(
        "gqk,kd->qgd", prob_bf, values_head, preferred_element_type=jnp.float32
    ).astype(jnp.bfloat16)
    return (mixed_out, log_total[..., 0])


def head_backward(operands, allowed):
    query_rows, keys_head, values_head, mixed_out, grad_mixed, log_total = operands
    scale_factor = query_rows.shape[-1] ** (-0.5)
    scores = (
        jnp.einsum("qgd,kd->gqk", query_rows, keys_head, preferred_element_type=jnp.float32)
        * scale_factor
    )
    prob_full = jnp.where(allowed[None], jnp.exp(scores - log_total[..., None]), 0.0)
    prob_bf = prob_full.astype(jnp.bfloat16)
    grad_values = jnp.einsum("gqk,qgd->kd", prob_bf, grad_mixed, preferred_element_type=jnp.float32)
    grad_probs = jnp.einsum(
        "qgd,kd->gqk", grad_mixed, values_head, preferred_element_type=jnp.float32
    )
    inner = jnp.sum(
        grad_mixed.astype(jnp.float32) * mixed_out.astype(jnp.float32), axis=-1
    ).transpose(1, 0)
    grad_scores = (prob_full * (grad_probs - inner[..., None])).astype(jnp.bfloat16)
    grad_queries = (
        jnp.einsum("gqk,kd->qgd", grad_scores, keys_head, preferred_element_type=jnp.float32)
        * scale_factor
    )
    grad_keys = (
        jnp.einsum("gqk,qgd->kd", grad_scores, query_rows, preferred_element_type=jnp.float32)
        * scale_factor
    )
    return (grad_queries, grad_keys, grad_values)


def peer_plan(device, count):
    if count != 32:
        return [device % 2 + 2 * i for i in range(count // 2)]
    core = device % 2
    first = jnp.where(core == 0, 4, 2)
    second = 6 - first
    plan = []
    for plane in range(4):
        base = device ^ (8 * plane)
        plan += [base, base ^ first, base ^ second, base ^ 6]
    return plan


def swap_perm(mask):
    return [(i, i ^ mask) for i in range(32)]


def core_perm(count):
    return [(i, i ^ 1) for i in range(count)]


def first_perm():
    return [(i, i ^ (4 if i % 2 == 0 else 2)) for i in range(32)]


def second_perm():
    return [(i, i ^ (2 if i % 2 == 0 else 4)) for i in range(32)]


def permute(value, perm):
    return lax.ppermute(value, "fsdp", perm)


def parity_groups(count):
    return [list(range(0, count, 2)), list(range(1, count, 2))]


def gather_peers(shard, count):
    if count != 32:
        whole = lax.all_gather(shard, "fsdp", axis=0, axis_index_groups=parity_groups(count))
        return [whole[i] for i in range(count // 2)]
    rows = shard.shape[0]
    base = shard
    first_own = permute(base, first_perm())
    second_own = permute(base, second_perm())
    base_one = permute(base, swap_perm(8))
    base_two = permute(base, swap_perm(16))
    base_three = permute(base, swap_perm(24))
    across_own = permute(first_own, second_perm())
    second_one = permute(base_one, second_perm())
    first_one = permute(first_own, swap_perm(8))
    across_one = permute(across_own, swap_perm(8))
    far = jnp.concatenate([base_two, base_three], axis=0)
    first_far = permute(far, first_perm())
    second_far = permute(far, second_perm())
    across_far = permute(first_far, second_perm())
    return [
        base, first_own, second_own, across_own,
        base_one, first_one, second_one, across_one,
        base_two, first_far[:rows], second_far[:rows], across_far[:rows],
        base_three, first_far[rows:], second_far[rows:], across_far[rows:],
    ]


def add_wide(*terms):
    return sum(t.astype(jnp.float32) for t in terms)


def sum_to_peers(terms, count):
    if count != 32:
        stacked = jnp.concatenate([t.astype(jnp.float32) for t in terms], axis=0)
        return lax.psum_scatter(
            stacked, "fsdp", scatter_dimension=0, tiled=True, axis_index_groups=parity_groups(count)
        )
    bf = jnp.bfloat16
    rows = terms[0].shape[0]
    far = [jnp.concatenate([terms[8 + j], terms[12 + j]], axis=0) for j in range(4)]
    got = permute(far[3], second_perm())
    to_first = add_wide(far[1], got).astype(bf)
    got_first = permute(to_first, first_perm())
    got_second = permute(far[2], second_perm())
    base_far = add_wide(far[0], got_first, got_second).astype(bf)
    back_two = permute(base_far[:rows], swap_perm(16))
    back_three = permute(base_far[rows:], swap_perm(24))
    got_one = permute(terms[6], second_perm())
    base_one = add_wide(terms[4], got_one).astype(bf)
    back_one = permute(base_one, swap_perm(8))
    back_first = permute(terms[5], swap_perm(8))
    back_across = permute(terms[7], swap_perm(8))
    across = add_wide(terms[3], back_across).astype(bf)
    got_across = permute(across, second_perm())
    to_first = add_wide(terms[1], back_first, got_across).astype(bf)
    got_first = permute(to_first, first_perm())
    got_second = permute(terms[2], second_perm())
    return add_wide(terms[0], got_first, got_second, back_one, back_two, back_three)


def gather_dense(shard, device, count):
    if count != 32:
        return lax.all_gather(shard, "fsdp", axis=0, tiled=True)
    mine = jnp.stack(gather_peers(shard, count))
    theirs = permute(mine, core_perm(count))
    order = jnp.stack(peer_plan(device, count) + peer_plan(device ^ 1, count))
    place = jnp.zeros((count,), jnp.int32).at[order].set(jnp.arange(count, dtype=jnp.int32))
    both = jnp.concatenate([mine, theirs], axis=0)
    return both[place].reshape(count * shard.shape[0], -1)


def sum_dense(terms, device, count):
    if count != 32:
        return lax.psum_scatter(terms, "fsdp", scatter_dimension=0, tiled=True)[0]
    mine = terms[jnp.stack(peer_plan(device, count))]
    theirs = terms[jnp.stack(peer_plan(device ^ 1, count))].astype(jnp.bfloat16)
    both = (mine + permute(theirs, core_perm(count))).astype(jnp.bfloat16)
    return sum_to_peers([both[i] for i in range(count // 2)], count)


def expert_set(rows, cots, ids, router, tables, names):
    bf, f32 = jnp.bfloat16, jnp.float32
    dot = partial(jnp.einsum, preferred_element_type=f32)
    count_of_rows = rows.shape[1]
    logits = dot("btd,de->bte", rows, router)
    picker = jnp.any(ids[..., None] == jnp.arange(EXPERT_COUNT, dtype=jnp.int32), axis=2)
    raised = jnp.where(picker, jnp.exp(logits), 0.0)
    weights = raised / jnp.sum(raised, axis=-1, keepdims=True)
    out = jnp.zeros(rows.shape, f32)
    back = jnp.zeros(rows.shape, f32)
    route = jnp.zeros(rows.shape[:2] + (EXPERT_COUNT,), f32)
    grads = []
    for (gate, up, down), name in zip(tables, names):
        hit = jnp.any(ids == name, axis=2)
        rank = jnp.cumsum(hit.astype(jnp.int32), axis=1) - 1
        slots = jnp.arange(CAP, dtype=jnp.int32)
        chosen = hit[:, None, :] & (rank[:, None, :] == slots[None, :, None])
        pick = chosen.astype(bf)
        here = jnp.arange(EXPERT_COUNT, dtype=jnp.int32) == name
        weight = jnp.sum(jnp.where(here, weights, 0.0), axis=-1)
        slot_weight = jnp.sum(jnp.where(chosen, weight[:, None, :], 0.0), axis=-1)[..., None]
        inputs = dot("bst,btd->bsd", pick, rows).astype(bf)
        cot = dot("bst,btd->bsd", pick, cots)
        gate_pre = dot("bsd,hd->bsh", inputs, gate)
        up_pre = dot("bsd,hd->bsh", inputs, up)
        sigma = jax.nn.sigmoid(gate_pre)
        acts = (gate_pre * sigma * up_pre).astype(bf)
        result = dot("bsh,hd->bsd", acts, down)
        slot_route = jnp.sum(cot * result, axis=-1)
        pair_cot = (slot_weight * cot).astype(bf)
        act_grad = dot("bsd,hd->bsh", pair_cot, down)
        gate_pre_grad = (act_grad * up_pre * sigma * (1.0 + gate_pre * (1.0 - sigma))).astype(bf)
        up_pre_grad = (act_grad * gate_pre * sigma).astype(bf)
        in_grad = dot("bsh,hd->bsd", gate_pre_grad, gate) + dot("bsh,hd->bsd", up_pre_grad, up)
        grads.append(
            (
                dot("bsh,bsd->hd", gate_pre_grad, inputs),
                dot("bsh,bsd->hd", up_pre_grad, inputs),
                dot("bsh,bsd->hd", acts, pair_cot),
            )
        )
        out = out + dot("bst,bsd->btd", pick, (slot_weight * result).astype(bf))
        back = back + dot("bst,bsd->btd", pick, in_grad.astype(bf))
        row_route = jnp.sum(jnp.where(chosen, slot_route[..., None], 0.0), axis=1)
        route = route + jnp.where(here, row_route[..., None], 0.0)
    return (out.astype(bf), back.astype(bf), route, grads)


def body(
    block_input,
    seq_lengths,
    seq_devices,
    expert_ids,
    attn_gain,
    query_weight,
    keyvalue_weight,
    output_weight,
    moe_gain,
    router_weight,
    gate_weight,
    up_weight,
    down_weight,
    output_grad,
):
    bf, f32 = jnp.bfloat16, jnp.float32
    count_of_rows, model_width = block_input.shape
    device = lax.axis_index("fsdp").astype(jnp.int32)
    count = lax.axis_size("fsdp")
    shard_rows = gate_weight.shape[0]
    part = query_weight.shape[0]
    query_group_width = QUERY_HEADS // KEY_VALUE_HEADS
    key_value_columns = KEY_VALUE_HEADS * HEAD_WIDTH
    live_rows, segment, position = layout(seq_lengths, seq_devices, device, count_of_rows)
    live_col = live_rows[:, None]
    row_slots = jnp.arange(count_of_rows, dtype=jnp.int32)
    allowed = (segment[:, None] == segment[None, :]) & (row_slots[:, None] >= row_slots[None, :])
    cosine, sine_part = rope_tables(position, HEAD_WIDTH)

    small = jnp.concatenate([router_weight.reshape(-1), attn_gain, moe_gain])
    small_rows = -(-small.shape[0] // (16 * model_width)) * 16
    small = jnp.pad(small, (0, small_rows * model_width - small.shape[0])).reshape(small_rows, model_width)
    dense = gather_dense(jnp.concatenate([query_weight, keyvalue_weight, small], axis=0), device, count)
    dense = dense.reshape(count, -1, model_width)
    full_query = dense[:, :part].reshape(-1, model_width)
    full_kv = dense[:, part : 2 * part].reshape(-1, model_width)
    small = dense[:, 2 * part :].reshape(count, -1)
    full_router = small[:, : part * EXPERT_COUNT].reshape(-1, EXPERT_COUNT)
    full_gain1 = small[:, part * EXPERT_COUNT : part * EXPERT_COUNT + part].reshape(-1)
    full_gain2 = small[:, part * EXPERT_COUNT + part : part * EXPERT_COUNT + 2 * part].reshape(-1)
    full_out = gather_dense(output_weight, device, count)

    own_tables = jnp.stack([gate_weight, up_weight, down_weight])
    sibling_tables = permute(own_tables, core_perm(count))
    own_name = device * shard_rows // EXPERT_HIDDEN
    sibling_name = (device ^ 1) * shard_rows // EXPERT_HIDDEN

    masked_grad = jnp.where(live_col, output_grad, jnp.zeros((), bf))
    id_rows = expert_ids.astype(bf).reshape(-1, model_width)
    id_rows = jnp.pad(id_rows, ((0, -id_rows.shape[0] % 16), (0, 0)))
    cot_blocks = gather_peers(jnp.concatenate([masked_grad, id_rows], axis=0), count)

    input_f = block_input.astype(f32)
    attn_norm, attn_unit, attn_rms = norm_forward(input_f, full_gain1)
    attn_in = attn_norm.astype(bf)
    query_pre = jnp.dot(attn_in, full_query, preferred_element_type=f32)
    kv_pre = jnp.dot(attn_in, full_kv, preferred_element_type=f32)
    query_rows = rotate(query_pre, cosine, sine_part, HEAD_WIDTH).astype(bf)
    gathered_keys = rotate(kv_pre[:, :key_value_columns], cosine, sine_part, HEAD_WIDTH).astype(bf)
    gathered_values = kv_pre[:, key_value_columns:].astype(bf)
    query_head_rows = query_rows.reshape(
        count_of_rows, KEY_VALUE_HEADS, query_group_width, HEAD_WIDTH
    ).transpose(1, 0, 2, 3)
    key_head_rows = gathered_keys.reshape(count_of_rows, KEY_VALUE_HEADS, HEAD_WIDTH).transpose(1, 0, 2)
    value_head_rows = gathered_values.reshape(count_of_rows, KEY_VALUE_HEADS, HEAD_WIDTH).transpose(1, 0, 2)
    mixed_heads, log_totals = jax.vmap(partial(head_forward, allowed=allowed))(
        (query_head_rows, key_head_rows, value_head_rows)
    )
    attn_heads = mixed_heads.transpose(1, 0, 2, 3).reshape(count_of_rows, QUERY_HEADS * HEAD_WIDTH)
    residual = input_f + jnp.dot(attn_heads, full_out, preferred_element_type=f32)
    moe_norm, moe_unit, moe_rms = norm_forward(residual, full_gain2)
    moe_in = moe_norm.astype(bf)

    moe_blocks = gather_peers(moe_in, count)
    outs, backs, sums = [], [], None
    tables = [tuple(own_tables), tuple(sibling_tables)]
    step = len(moe_blocks) // 4
    for first in range(0, len(moe_blocks), step):
        cots = jnp.stack(cot_blocks[first : first + step])
        ids = cots[:, count_of_rows:].reshape(step, -1)[:, : count_of_rows * TOPK]
        ids = ids.reshape(step, count_of_rows, TOPK).astype(jnp.int32)
        out, back, route, grads = expert_set(
            jnp.stack(moe_blocks[first : first + step]),
            cots[:, :count_of_rows],
            ids,
            full_router,
            tables,
            [own_name, sibling_name],
        )
        high = route.astype(bf)
        low = (route - high.astype(f32)).astype(bf)
        packed = jnp.concatenate([high, low], axis=-1).reshape(step, -1, model_width)
        back = jnp.concatenate([back, packed], axis=1)
        outs += [out[i] for i in range(step)]
        backs += [back[i] for i in range(step)]
        sums = grads if sums is None else jax.tree.map(jnp.add, sums, grads)
    from_sibling = permute(jnp.stack(sums[1]), core_perm(count))
    gate_grad, up_grad, down_grad = [a + b for a, b in zip(sums[0], from_sibling)]

    back_sum = sum_to_peers(backs, count)
    slot_in_grad = back_sum[:count_of_rows]
    route = back_sum[count_of_rows:].reshape(count_of_rows, 2, EXPERT_COUNT)
    route_grad = route[:, 0] + route[:, 1]
    logits = jnp.dot(moe_in, full_router, preferred_element_type=f32)
    picker = jnp.any(expert_ids[..., None] == jnp.arange(EXPERT_COUNT, dtype=jnp.int32), axis=1)
    raised = jnp.where(picker, jnp.exp(logits), 0.0)
    route_weights = raised / jnp.sum(raised, axis=-1, keepdims=True)
    logit_grad = route_weights * (route_grad - jnp.sum(route_weights * route_grad, axis=-1, keepdims=True))
    logit_grad = logit_grad.astype(bf)

    moe_out = sum_to_peers(outs, count)
    block_output = jnp.where(live_col, residual + moe_out, 0.0).astype(bf)
    out_cot = masked_grad.astype(f32)
    moe_in_grad = slot_in_grad + jnp.einsum(
        "te,de->td", logit_grad, full_router, preferred_element_type=f32
    )
    router_grad = jnp.einsum("td,te->de", moe_in, logit_grad, preferred_element_type=f32)
    resid_part, moe_gain_grad = norm_backward(moe_in_grad, full_gain2, moe_unit, moe_rms)
    residual_grad = out_cot + resid_part
    residual_bf = residual_grad.astype(bf)
    output_weight_grad = jnp.einsum("tf,td->fd", attn_heads, residual_bf, preferred_element_type=f32)
    gradient_per_head = jnp.einsum(
        "td,fd->tf", residual_bf, full_out, preferred_element_type=f32
    ).astype(bf)
    head_gradients = gradient_per_head.reshape(
        count_of_rows, KEY_VALUE_HEADS, query_group_width, HEAD_WIDTH
    ).transpose(1, 0, 2, 3)
    grad_q, grad_k, grad_v = jax.vmap(partial(head_backward, allowed=allowed))(
        (query_head_rows, key_head_rows, value_head_rows, mixed_heads, head_gradients, log_totals)
    )
    query_rot_grad = grad_q.transpose(1, 0, 2, 3).reshape(count_of_rows, QUERY_HEADS * HEAD_WIDTH)
    key_rot_grad = grad_k.transpose(1, 0, 2).reshape(count_of_rows, key_value_columns)
    value_grad = grad_v.transpose(1, 0, 2).reshape(count_of_rows, key_value_columns)
    query_pre_grad = rotate(query_rot_grad, cosine, -sine_part, HEAD_WIDTH).astype(bf)
    kv_pre_grad = jnp.concatenate(
        [rotate(key_rot_grad, cosine, -sine_part, HEAD_WIDTH), value_grad], axis=1
    ).astype(bf)
    query_grad = jnp.einsum("td,tf->df", attn_in, query_pre_grad, preferred_element_type=f32)
    keyvalue_grad = jnp.einsum("td,tf->df", attn_in, kv_pre_grad, preferred_element_type=f32)
    attn_in_grad = jnp.einsum(
        "tf,df->td", query_pre_grad, full_query, preferred_element_type=f32
    ) + jnp.einsum("tf,df->td", kv_pre_grad, full_kv, preferred_element_type=f32)
    input_part, attn_gain_grad = norm_backward(attn_in_grad, full_gain1, attn_unit, attn_rms)
    input_grad = jnp.where(live_col, residual_grad + input_part, 0.0)

    def per_device(whole):
        return whole.reshape(count, part, -1)

    small_terms = jnp.concatenate(
        [
            router_grad.reshape(count, -1),
            attn_gain_grad.reshape(count, -1),
            moe_gain_grad.reshape(count, -1),
        ],
        axis=1,
    )
    small_terms = jnp.pad(small_terms, ((0, 0), (0, small_rows * model_width - small_terms.shape[1])))
    small_terms = small_terms.reshape(count, small_rows, model_width)
    dense_sum = sum_dense(
        jnp.concatenate(
            [per_device(query_grad), per_device(keyvalue_grad), per_device(output_weight_grad), small_terms],
            axis=1,
        ),
        device,
        count,
    )
    small_sum = dense_sum[3 * part :].reshape(-1)
    routers = part * EXPERT_COUNT
    return (
        block_output,
        input_grad,
        small_sum[routers : routers + part],
        dense_sum[:part],
        dense_sum[part : 2 * part],
        dense_sum[2 * part : 3 * part],
        small_sum[routers + part : routers + 2 * part],
        small_sum[:routers].reshape(part, EXPERT_COUNT),
        gate_grad,
        up_grad,
        down_grad,
    )


def solution(mesh):
    placed = (
        P("fsdp", None),
        P(),
        P(),
        P("fsdp", None),
        P("fsdp"),
        P("fsdp", None),
        P("fsdp", None),
        P("fsdp", None),
        P("fsdp"),
        P("fsdp", None),
        P("fsdp", None),
        P("fsdp", None),
        P("fsdp", None),
        P("fsdp", None),
    )
    return jax.shard_map(
        body,
        mesh=mesh,
        in_specs=placed,
        out_specs=(
            P("fsdp", None),
            P("fsdp", None),
            P("fsdp"),
            P("fsdp", None),
            P("fsdp", None),
            P("fsdp", None),
            P("fsdp"),
            P("fsdp", None),
            P("fsdp", None),
            P("fsdp", None),
            P("fsdp", None),
        ),
        check_vma=False,
    )
```

```python
from functools import partial

import jax
import jax.numpy as jnp
from jax import lax
from jax.experimental import pallas as pl
from jax.experimental.pallas import tpu as pltpu
from jax.sharding import PartitionSpec as P

QUERY_HEADS = 16
KEY_VALUE_HEADS = 8
HEAD_WIDTH = 64
EXPERT_COUNT = 32
EXPERT_HIDDEN = 512
TOPK = 8
CAP = 40

EPS = 1e-06
ROPE_BASE = 10000.0

MODEL = 1024
ROWS = 128
PART = 32
EXTRA = 16
PACK = 3 * PART + EXTRA
BLOCKS = MODEL // PART
WIDE = ROWS + EXTRA
NOT_CHOSEN = 64
VMEM_LIMIT = 60 * 1024 * 1024

BF = jnp.bfloat16
F32 = jnp.float32


def dot(a, b, a_dim, b_dim):
    return lax.dot_general(a, b, (((a_dim,), (b_dim,)), ((), ())), preferred_element_type=F32)


def row_by_col(a, b):
    return dot(a, b, 1, 0)


def row_by_row(a, b):
    return dot(a, b, 1, 1)


def col_by_col(a, b):
    return dot(a, b, 0, 0)


def layout(seq_lengths, seq_devices, device, count_of_rows):
    on_device = seq_devices == device
    lengths = jnp.where(on_device, seq_lengths, 0)
    starts = jnp.cumsum(lengths) - lengths
    filled_rows = jnp.sum(lengths)
    row_slots = jnp.arange(count_of_rows, dtype=jnp.int32)
    inside = (row_slots[:, None] >= starts[None, :]) & (
        row_slots[:, None] < (starts + lengths)[None, :]
    )
    live_rows = jnp.any(inside, axis=1)
    seq_count = seq_lengths.shape[0]
    numbers = jnp.arange(seq_count, dtype=jnp.int32)
    segment = jnp.where(
        live_rows, jnp.sum(jnp.where(inside, numbers[None, :], 0), axis=1), seq_count
    )
    begins = jnp.where(
        live_rows, jnp.sum(jnp.where(inside, starts[None, :], 0), axis=1), filled_rows
    )
    return (live_rows, segment, row_slots - begins)


def rope_tables(position):
    half = HEAD_WIDTH // 2
    lanes = jnp.arange(2 * HEAD_WIDTH, dtype=jnp.int32)
    exponent = (lanes % half).astype(F32) * 2.0 / HEAD_WIDTH
    angles = position.astype(F32)[:, None] * (ROPE_BASE ** (-exponent))[None, :]
    sign = jnp.where(lanes % HEAD_WIDTH < half, -1.0, 1.0)
    return jnp.cos(angles), jnp.sin(angles) * sign[None, :]


def permute(value, perm):
    return lax.ppermute(value, "fsdp", perm)


def swap_perm(mask, count=32):
    return [(i, i ^ mask) for i in range(count)]


def first_perm():
    return [(i, i ^ (4 if i % 2 == 0 else 2)) for i in range(32)]


def second_perm():
    return [(i, i ^ (2 if i % 2 == 0 else 4)) for i in range(32)]


def parity_groups(count):
    return [list(range(0, count, 2)), list(range(1, count, 2))]


def peer_plan(device, count):
    if count != 32:
        return [device % 2 + 2 * i for i in range(count // 2)]
    core = device % 2
    first = jnp.where(core == 0, 4, 2)
    second = 6 - first
    near = [device ^ (8 * z) ^ step for z in (0, 1) for step in (0, first, second, 6)]
    far = [device ^ (8 * z) ^ step for step in (0, first, second, 6) for z in (2, 3)]
    return near + far


def gather_peers(shard, count):
    if count != 32:
        whole = lax.all_gather(shard, "fsdp", axis=0, axis_index_groups=parity_groups(count))
        return [whole[i] for i in range(count // 2)]
    base = shard
    first_own = permute(base, first_perm())
    second_own = permute(base, second_perm())
    base_one = permute(base, swap_perm(8))
    base_two = permute(base, swap_perm(16))
    base_three = permute(base, swap_perm(24))
    across_own = permute(first_own, second_perm())
    second_one = permute(base_one, second_perm())
    first_one = permute(first_own, swap_perm(8))
    across_one = permute(across_own, swap_perm(8))
    far = jnp.concatenate([base_two, base_three], axis=0)
    first_far = permute(far, first_perm())
    second_far = permute(far, second_perm())
    across_far = permute(first_far, second_perm())
    return [
        base, first_own, second_own, across_own, base_one, first_one, second_one, across_one,
        far, first_far, second_far, across_far,
    ]


def add_wide(*terms):
    return sum(t.astype(F32) for t in terms)


def add_round(*terms):
    return add_wide(*terms).astype(BF)


def sum_to_peers(terms, count):
    if count != 32:
        stacked = jnp.concatenate([t.astype(F32) for t in terms], axis=0)
        return [
            lax.psum_scatter(
                stacked, "fsdp", scatter_dimension=0, tiled=True, axis_index_groups=parity_groups(count)
            )
        ]
    own, one, far = terms[:4], terms[4:8], terms[8:]
    rows = own[0].shape[0]
    got = permute(far[3], second_perm())
    got_second = permute(far[2], second_perm())
    got_first = permute(add_round(far[1], got), first_perm())
    got_one = permute(one[2], second_perm())
    back_first = permute(one[1], swap_perm(8))
    back_across = permute(one[3], swap_perm(8))
    back_two = permute(add_round(far[0][:rows], got_first[:rows], got_second[:rows]), swap_perm(16))
    back_three = permute(add_round(far[0][rows:], got_first[rows:], got_second[rows:]), swap_perm(24))
    back_one = permute(add_round(one[0], got_one), swap_perm(8))
    got_across = permute(add_round(own[3], back_across), second_perm())
    got_second = permute(own[2], second_perm())
    got_first = permute(add_round(own[1], back_first, got_across), first_perm())
    return [own[0], got_first, got_second, back_one, back_two, back_three]


def pack_kernel(query, keyvalue, output, small, packed):
    packed[0:PART, :] = query[...]
    packed[PART : 2 * PART, :] = keyvalue[...]
    packed[2 * PART : 3 * PART, :] = output[...]
    packed[3 * PART :, :] = jnp.zeros((EXTRA, MODEL), BF)
    packed[3 * PART :, 0:128] = small[0:EXTRA, :]
    packed[3 * PART :, 128:256] = small[EXTRA:, :]


def start_weights(place, buffers, weights, sems):
    copies = []
    for buffer in buffers:
        for j in range(buffer.shape[0] // PACK):
            i = len(copies)
            copies.append(
                pltpu.make_async_copy(
                    buffer.at[pl.ds(j * PACK, PACK)], weights.at[place[i]], sems.at[i]
                )
            )
            copies[-1].start()
    return copies


def half_swap(chunk):
    lane = lax.broadcasted_iota(jnp.int32, chunk.shape, 1)
    half = HEAD_WIDTH // 2
    return jnp.where(
        lane % HEAD_WIDTH < half, pltpu.roll(chunk, 128 - half, 1), pltpu.roll(chunk, half, 1)
    )


def doubled(chunk, second):
    lane = lax.broadcasted_iota(jnp.int32, chunk.shape, 1)
    turned = pltpu.roll(chunk, HEAD_WIDTH, 1)
    keep = lane >= HEAD_WIDTH if second else lane < HEAD_WIDTH
    return jnp.where(keep, chunk, turned)


def split_pair(chunk):
    lane = lax.broadcasted_iota(jnp.int32, chunk.shape, 1)
    zero = jnp.zeros_like(chunk)
    return jnp.concatenate(
        [jnp.where(lane < HEAD_WIDTH, chunk, zero), jnp.where(lane < HEAD_WIDTH, zero, chunk)], axis=0
    )


def join_pair(stacked):
    lane = lax.broadcasted_iota(jnp.int32, (ROWS, 128), 1)
    return jnp.where(lane < HEAD_WIDTH, stacked[:ROWS], stacked[ROWS:])


def attention_kernel(buffers_count, *refs):
    place, buffers, refs = refs[0], refs[1 : 1 + buffers_count], refs[1 + buffers_count :]
    x_ref, cos_ref, sin_ref, allowed_ref = refs[:4]
    moe_ref, resid_ref, heads_ref, query_ref, kv_ref, probs_ref, small_ref = refs[4:11]
    weights, columns, sems = refs[11:]
    copies = start_weights(place, buffers, weights, sems)
    x = x_ref[...].astype(F32)
    unit = x * lax.rsqrt(jnp.mean(x * x, axis=-1, keepdims=True) + EPS)
    for copy in copies:
        copy.wait()
    for p in range(BLOCKS):
        for j in range(2):
            columns[pl.ds(p * PART + j * EXTRA, EXTRA), :] = weights[
                p, 3 * PART :, 128 * j : 128 * (j + 1)
            ].astype(F32)
    small = columns[...].T
    small_ref[...] = small.astype(BF)
    attn_in = (unit * small[EXPERT_COUNT : EXPERT_COUNT + 1, :]).astype(BF)
    cosine, sine = cos_ref[...], sin_ref[...]

    def weight_columns(which, chunk):
        lanes = slice(256 * chunk, 256 * (chunk + 1))
        return weights[:, PART * which : PART * (which + 1), lanes].reshape(MODEL, 256)

    for chunk in range(4):
        query_pre = row_by_col(attn_in, weight_columns(0, chunk))
        kv_pre = row_by_col(attn_in, weight_columns(1, chunk))
        for j in range(2):
            at = slice(256 * chunk + 128 * j, 256 * chunk + 128 * (j + 1))
            part = query_pre[:, 128 * j : 128 * (j + 1)]
            query_ref[:, at] = (part * cosine + half_swap(part) * sine).astype(BF)
            part = kv_pre[:, 128 * j : 128 * (j + 1)]
            if chunk < 2:
                part = part * cosine + half_swap(part) * sine
            kv_ref[:, at] = part.astype(BF)
    allowed = jnp.concatenate([allowed_ref[...], allowed_ref[...]], axis=0) > 0.0
    scale = HEAD_WIDTH ** (-0.5)
    for head in range(KEY_VALUE_HEADS):
        pair, second = head // 2, head % 2 == 1
        key = doubled(kv_ref[:, 128 * pair : 128 * (pair + 1)].astype(F32), second).astype(BF)
        value = doubled(
            kv_ref[:, 512 + 128 * pair : 512 + 128 * (pair + 1)].astype(F32), second
        ).astype(BF)
        at = slice(128 * head, 128 * (head + 1))
        scores = row_by_row(split_pair(query_ref[:, at]), key) * scale
        scores = jnp.where(allowed, scores, -jnp.inf)
        raised = jnp.exp(scores - jnp.max(scores, axis=-1, keepdims=True))
        probs = raised / jnp.sum(raised, axis=-1, keepdims=True)
        probs_ref[head] = probs
        heads_ref[:, at] = join_pair(row_by_col(probs.astype(BF), value)).astype(BF)
    heads = heads_ref[...]
    for chunk in range(4):
        at = slice(256 * chunk, 256 * (chunk + 1))
        resid_ref[:, at] = x_ref[:, at].astype(F32) + row_by_col(heads, weight_columns(2, chunk))
    residual = resid_ref[...]
    unit = residual * lax.rsqrt(jnp.mean(residual * residual, axis=-1, keepdims=True) + EPS)
    moe_ref[...] = (unit * small[EXPERT_COUNT + 1 : EXPERT_COUNT + 2, :]).astype(BF)


def route_table(extra):
    return jnp.concatenate([extra[:, 0:128], extra[:, 128:256]], axis=0).astype(F32)


def route_weights_of(table, small, rows):
    logits = row_by_row(small, rows)[:EXPERT_COUNT]
    raised = jnp.where(table < NOT_CHOSEN, jnp.exp(logits), 0.0)
    return raised / jnp.sum(raised, axis=0, keepdims=True)


def expert_kernel(layout_of, buffers_count, hidden, *refs):
    names, refs = refs[0], refs[1:]
    x_refs, refs = refs[:buffers_count], refs[buffers_count:]
    c_refs, refs = refs[:buffers_count], refs[buffers_count:]
    small_ref, tables, refs = refs[0], refs[1:7], refs[7:]
    p_refs, refs = refs[:buffers_count], refs[buffers_count:]
    g_refs, refs = refs[:buffers_count], refs[buffers_count:]
    saved, (picks, cots, results, back) = (refs[:5], refs[5:10]), refs[10:]
    slots = 4 * CAP
    small = small_ref[...]
    expert_row = lax.broadcasted_iota(jnp.int32, (EXPERT_COUNT, ROWS), 0)
    slot_row = lax.broadcasted_iota(jnp.int32, (slots, 4 * ROWS), 0).astype(F32)
    slot_weights = [[None, None], [None, None]]
    for h in range(2):
        blocks = layout_of[4 * h : 4 * (h + 1)]
        xs, cs, places, weights = [], [], [[], []], [[], []]
        for b, (i, j) in enumerate(blocks):
            rows = x_refs[i][ROWS * j : ROWS * (j + 1), :]
            xs.append(rows)
            cs.append(c_refs[i][WIDE * j : WIDE * j + ROWS, :])
            table = route_table(c_refs[i][WIDE * j + ROWS : WIDE * (j + 1), 0:256])
            weight = route_weights_of(table, small, rows)
            for l in range(2):
                here = expert_row == names[l]
                place = jnp.sum(jnp.where(here, table, 0.0), axis=0, keepdims=True)
                places[l].append(jnp.where(place < NOT_CHOSEN, place + b * CAP, 4096.0))
                weights[l].append(jnp.sum(jnp.where(here, weight, 0.0), axis=0, keepdims=True))
        for l in range(2):
            chosen = slot_row == jnp.concatenate(places[l], axis=1)
            weight = jnp.concatenate(weights[l], axis=1)
            slot_weights[l][h] = jnp.sum(jnp.where(chosen, weight, 0.0), axis=1, keepdims=True)
            picks[h, slots * l : slots * (l + 1), :] = chosen.astype(F32).astype(BF)
        pick = picks[h]
        inputs = row_by_col(pick, jnp.concatenate(xs, axis=0)).astype(BF)
        cot = row_by_col(pick, jnp.concatenate(cs, axis=0)).astype(BF)
        for l in range(2):
            saved[l][0][slots * h : slots * (h + 1), :] = inputs[slots * l : slots * (l + 1)]
            cots[l, slots * h : slots * (h + 1), :] = cot[slots * l : slots * (l + 1)]
    slot_routes = []
    for l in range(2):
        gate, up, down = tables[3 * l : 3 * l + 3]
        weight = jnp.concatenate(slot_weights[l], axis=0)
        xs_ref, pc_ref, ac_ref, gg_ref, gu_ref = saved[l]
        inputs = xs_ref[...]
        gate_pre = row_by_row(inputs, gate[...])
        up_pre = row_by_row(inputs, up[...])
        sigma = jax.nn.sigmoid(gate_pre)
        acts = (gate_pre * sigma * up_pre).astype(BF)
        ac_ref[...] = acts
        cot = cots[l].astype(F32)
        result = row_by_col(acts, down[...])
        slot_routes.append(jnp.sum(cot * result, axis=1, keepdims=True))
        results[l] = (weight * result).astype(BF)
        pair_cot = (weight * cot).astype(BF)
        pc_ref[...] = pair_cot
        act_grad = row_by_row(pair_cot, down[...])
        gate_grad = (act_grad * up_pre * sigma * (1.0 + gate_pre * (1.0 - sigma))).astype(BF)
        up_grad = (act_grad * gate_pre * sigma).astype(BF)
        gg_ref[...] = gate_grad
        gu_ref[...] = up_grad
        back[l] = (row_by_col(gate_grad, gate[...]) + row_by_col(up_grad, up[...])).astype(BF)
    for h in range(2):
        pick = picks[h]
        at = slice(slots * h, slots * (h + 1))
        out = col_by_col(pick, jnp.concatenate([results[0, at], results[1, at]], axis=0)).astype(BF)
        grad = col_by_col(pick, jnp.concatenate([back[0, at], back[1, at]], axis=0)).astype(BF)
        routes = []
        for l in range(2):
            chosen = pick[slots * l : slots * (l + 1)].astype(F32)
            routes.append(jnp.sum(chosen * slot_routes[l][at], axis=0, keepdims=True))
        for b, (i, j) in enumerate(layout_of[4 * h : 4 * (h + 1)]):
            rows = slice(ROWS * b, ROWS * (b + 1))
            p_refs[i][ROWS * j : ROWS * (j + 1), :] = out[rows]
            g_refs[i][WIDE * j : WIDE * j + ROWS, :] = grad[rows]
            route = jnp.zeros((EXPERT_COUNT, ROWS), F32)
            for l in range(2):
                route = route + jnp.where(expert_row == names[l], routes[l][:, rows], 0.0)
            high = route.astype(BF)
            low = (route - high.astype(F32)).astype(BF)
            extra = slice(WIDE * j + ROWS, WIDE * (j + 1))
            g_refs[i][extra, 0:128] = high[:16]
            g_refs[i][extra, 128:256] = high[16:]
            g_refs[i][extra, 256:384] = low[:16]
            g_refs[i][extra, 384:512] = low[16:]
            g_refs[i][extra, 512:] = jnp.zeros((EXTRA, MODEL - 512), BF)


def weight_grad_kernel(calls, added, *refs):
    saved, refs = refs[: 5 * calls], refs[5 * calls :]
    extra, outs = refs[: 3 * added], refs[3 * added :]
    for o, (left, right) in enumerate(((3, 0), (4, 0), (2, 1))):
        total = extra[o][...] if added else None
        for c in range(calls):
            term = col_by_col(saved[5 * c + left][...], saved[5 * c + right][...])
            total = term if total is None else total + term
        outs[o][...] = total


def backward_kernel(buffers_count, pieces_count, *refs):
    place, buffers, refs = refs[0], refs[1 : 1 + buffers_count], refs[1 + buffers_count :]
    pieces, refs = refs[:pieces_count], refs[pieces_count:]
    moe_ref, resid_ref, cot_ref, small_ref, heads_ref, query_ref, kv_ref, probs_ref = refs[:8]
    x_ref, cos_ref, sin_ref, live_ref = refs[8:12]
    in_ref, mine_ref, theirs_ref = refs[12:15]
    weights, terms, grads, sems, out_sems = refs[15:]
    copies = start_weights(place, buffers, weights, sems)
    small = small_ref[...]
    small_f = small.astype(F32)
    total = pieces[0][...].astype(F32)
    for piece in pieces[1:]:
        total = total + piece[...].astype(F32)
    extra = total[ROWS:]
    route_grad = jnp.concatenate(
        [extra[:, 0:128] + extra[:, 256:384], extra[:, 128:256] + extra[:, 384:512]], axis=0
    )
    moe_in = moe_ref[...]
    table = route_table(cot_ref[ROWS:, 0:256])
    weight = route_weights_of(table, small, moe_in)
    logit_grad = weight * (route_grad - jnp.sum(weight * route_grad, axis=0, keepdims=True))
    logit_grad = jnp.concatenate(
        [logit_grad, jnp.zeros((ROWS - EXPERT_COUNT, ROWS), F32)], axis=0
    ).astype(BF)
    moe_in_grad = total[:ROWS] + col_by_col(logit_grad, small)
    router_grad = row_by_col(logit_grad, moe_in)
    residual = resid_ref[...]
    inverse = lax.rsqrt(jnp.mean(residual * residual, axis=-1, keepdims=True) + EPS)
    unit = residual * inverse
    moe_gain_grad = jnp.sum(moe_in_grad * unit, axis=0, keepdims=True)
    grad_unit = moe_in_grad * small_f[EXPERT_COUNT + 1 : EXPERT_COUNT + 2, :]
    mean = jnp.mean(grad_unit * unit, axis=-1, keepdims=True)
    residual_grad = cot_ref[:ROWS, :].astype(F32) + inverse * (grad_unit - unit * mean)
    in_ref[...] = residual_grad
    residual_bf = residual_grad.astype(BF)
    for copy in copies:
        copy.wait()

    def weight_rows(which, chunk):
        return weights[8 * chunk : 8 * (chunk + 1), PART * which : PART * (which + 1), :].reshape(
            256, MODEL
        )

    heads = heads_ref[...]
    for chunk in range(4):
        at = slice(256 * chunk, 256 * (chunk + 1))
        grad = col_by_col(heads[:, at], residual_bf).astype(BF)
        terms[8 * chunk : 8 * (chunk + 1), 2 * PART : 3 * PART, :] = grad.reshape(8, PART, MODEL)
        grads[:, at] = row_by_row(residual_bf, weight_rows(2, chunk)).astype(BF)
    cosine, sine = cos_ref[...], sin_ref[...]
    scale = HEAD_WIDTH ** (-0.5)
    query_grads, key_grads, value_grads = [], [], []
    for head in range(KEY_VALUE_HEADS):
        pair, second = head // 2, head % 2 == 1
        key = doubled(kv_ref[:, 128 * pair : 128 * (pair + 1)].astype(F32), second).astype(BF)
        value = doubled(
            kv_ref[:, 512 + 128 * pair : 512 + 128 * (pair + 1)].astype(F32), second
        ).astype(BF)
        at = slice(128 * head, 128 * (head + 1))
        query = split_pair(query_ref[:, at])
        head_grad = split_pair(grads[:, at])
        mixed = split_pair(heads_ref[:, at])
        inner = jnp.sum(head_grad.astype(F32) * mixed.astype(F32), axis=-1, keepdims=True)
        probs = probs_ref[head]
        score_grad = (probs * (row_by_row(head_grad, value) - inner)).astype(BF)
        part = join_pair(row_by_col(score_grad, key)) * scale
        query_grads.append((part * cosine - half_swap(part) * sine).astype(BF))
        part = col_by_col(score_grad, query) * scale
        key_grads.append(part + pltpu.roll(part, HEAD_WIDTH, 1))
        part = col_by_col(probs.astype(BF), head_grad)
        value_grads.append(part + pltpu.roll(part, HEAD_WIDTH, 1))
    lane = lax.broadcasted_iota(jnp.int32, (ROWS, 128), 1)
    kv_grads = []
    for parts in (key_grads, value_grads):
        for pair in range(KEY_VALUE_HEADS // 2):
            part = jnp.where(lane < HEAD_WIDTH, parts[2 * pair], parts[2 * pair + 1])
            if parts is key_grads:
                part = part * cosine - half_swap(part) * sine
            kv_grads.append(part.astype(BF))
    query_grad = jnp.concatenate(query_grads, axis=1)
    kv_grad = jnp.concatenate(kv_grads, axis=1)
    x = x_ref[...].astype(F32)
    inverse = lax.rsqrt(jnp.mean(x * x, axis=-1, keepdims=True) + EPS)
    unit = x * inverse
    gain = small_f[EXPERT_COUNT : EXPERT_COUNT + 1, :]
    attn_in = (unit * gain).astype(BF)
    back = []
    for chunk in range(4):
        at = slice(256 * chunk, 256 * (chunk + 1))
        for which, grad in ((0, query_grad), (1, kv_grad)):
            term = col_by_col(attn_in[:, at], grad).astype(BF)
            terms[8 * chunk : 8 * (chunk + 1), PART * which : PART * (which + 1), :] = term.reshape(
                8, PART, MODEL
            )
        back.append(
            row_by_row(query_grad, weight_rows(0, chunk)) + row_by_row(kv_grad, weight_rows(1, chunk))
        )
    attn_in_grad = jnp.concatenate(back, axis=1)
    attn_gain_grad = jnp.sum(attn_in_grad * unit, axis=0, keepdims=True)
    row = lax.broadcasted_iota(jnp.int32, (ROWS, MODEL), 0)
    columns = jnp.where(row == EXPERT_COUNT, attn_gain_grad, router_grad)
    columns = jnp.where(row == EXPERT_COUNT + 1, moe_gain_grad, columns).T.astype(BF)
    for p in range(BLOCKS):
        for j in range(2):
            terms[p, 3 * PART :, 128 * j : 128 * (j + 1)] = columns[
                p * PART + j * EXTRA : p * PART + (j + 1) * EXTRA
            ]
        terms[p, 3 * PART :, 256:] = jnp.zeros((EXTRA, MODEL - 256), BF)
    copies = []
    for i in range(BLOCKS):
        target = (mine_ref, theirs_ref)[i // (BLOCKS // 2)]
        rows = pl.ds(PACK * (i % (BLOCKS // 2)), PACK)
        copies.append(
            pltpu.make_async_copy(terms.at[place[i]], target.at[rows], out_sems.at[i])
        )
        copies[-1].start()
    grad_unit = attn_in_grad * gain
    mean = jnp.mean(grad_unit * unit, axis=-1, keepdims=True)
    input_grad = in_ref[...] + inverse * (grad_unit - unit * mean)
    in_ref[...] = jnp.where(live_ref[...] > 0.0, input_grad, 0.0)
    for copy in copies:
        copy.wait()


def params():
    return pltpu.CompilerParams(vmem_limit_bytes=VMEM_LIMIT)


def shape(dims, dtype):
    return jax.ShapeDtypeStruct(dims, dtype)


def spec(space):
    return pl.BlockSpec(memory_space=space)


def body(
    block_input,
    seq_lengths,
    seq_devices,
    expert_ids,
    attn_gain,
    query_weight,
    keyvalue_weight,
    output_weight,
    moe_gain,
    router_weight,
    gate_weight,
    up_weight,
    down_weight,
    output_grad,
):
    device = lax.axis_index("fsdp").astype(jnp.int32)
    count = lax.axis_size("fsdp")
    hidden = gate_weight.shape[0]
    vmem, smem, anywhere = spec(pltpu.VMEM), spec(pltpu.SMEM), spec(pl.ANY)

    small = jnp.concatenate([router_weight, attn_gain[:, None], moe_gain[:, None]], axis=1)
    small = jnp.pad(small, ((0, 0), (0, 128 - small.shape[1])))
    if count == 32:
        packed = pl.pallas_call(
            pack_kernel, out_shape=shape((PACK, MODEL), BF), compiler_params=params()
        )(query_weight, keyvalue_weight, output_weight, small)
        mine = gather_peers(packed, count)
        near = permute(jnp.concatenate(mine[:8], axis=0), swap_perm(1))
        dense = mine + [near] + [permute(part, swap_perm(1)) for part in mine[8:]]
        place = jnp.stack(peer_plan(device, count) + peer_plan(device ^ 1, count))
    else:
        whole = [
            lax.all_gather(w, "fsdp", axis=0, tiled=True)
            for w in (query_weight, keyvalue_weight, output_weight, small)
        ]
        extra = whole[3].reshape(BLOCKS, 2, EXTRA, 128).transpose(0, 2, 1, 3).reshape(BLOCKS, EXTRA, 256)
        extra = jnp.pad(extra, ((0, 0), (0, 0), (0, MODEL - 256)))
        packed = jnp.concatenate([w.reshape(BLOCKS, PART, MODEL) for w in whole[:3]] + [extra], axis=1)
        dense = [packed.reshape(BLOCKS * PACK, MODEL)]
        place = jnp.arange(BLOCKS, dtype=jnp.int32)

    own_tables = [gate_weight, up_weight, down_weight]
    tables = own_tables + [permute(t, swap_perm(1, count)) for t in own_tables]
    names = jnp.stack([device, device ^ 1]) * hidden // EXPERT_HIDDEN

    live_rows, segment, position = layout(seq_lengths, seq_devices, device, ROWS)
    row_slots = jnp.arange(ROWS, dtype=jnp.int32)
    allowed = (segment[:, None] == segment[None, :]) & (row_slots[:, None] >= row_slots[None, :])
    allowed = allowed.astype(F32)
    cosine, sine = rope_tables(position)
    live_col = live_rows[:, None]
    live = live_col.astype(F32)
    masked_grad = jnp.where(live_col, output_grad, jnp.zeros((), BF))
    hit = jnp.any(
        expert_ids[None, :, :] == jnp.arange(EXPERT_COUNT, dtype=jnp.int32)[:, None, None], axis=2
    )
    before = (row_slots[:, None] < row_slots[None, :]).astype(BF)
    rank = jnp.dot(hit.astype(BF), before, preferred_element_type=F32)
    table = jnp.where(hit, rank, float(NOT_CHOSEN)).astype(BF)
    table = jnp.concatenate([table[:EXTRA], table[EXTRA:]], axis=1)
    table = jnp.pad(table, ((0, 0), (0, MODEL - 256)))
    own_cots = jnp.concatenate([masked_grad, table], axis=0)
    cots = gather_peers(own_cots, count)

    moe_in, residual, heads, query, keyvalue, probs, small = pl.pallas_call(
        partial(attention_kernel, len(dense)),
        out_shape=(
            shape((ROWS, MODEL), BF),
            shape((ROWS, MODEL), F32),
            shape((ROWS, MODEL), BF),
            shape((ROWS, MODEL), BF),
            shape((ROWS, MODEL), BF),
            shape((KEY_VALUE_HEADS, 2 * ROWS, ROWS), F32),
            shape((128, MODEL), BF),
        ),
        in_specs=[smem] + [anywhere] * len(dense) + [vmem] * 4,
        out_specs=(vmem,) * 7,
        scratch_shapes=[
            pltpu.VMEM((BLOCKS, PACK, MODEL), BF),
            pltpu.VMEM((MODEL, 128), F32),
            pltpu.SemaphoreType.DMA((BLOCKS,)),
        ],
        compiler_params=params(),
    )(place, *dense, block_input, cosine, sine, allowed)

    peers = gather_peers(moe_in, count)
    calls = [(range(8), 1), (range(8, 12), 2)] if count == 32 else [
        (range(first, first + 8), 1) for first in range(0, count // 2, 8)
    ]
    slots = 8 * CAP
    outs, backs, saved = [], [], ([], [])
    for which, size in calls:
        number = len(which)
        layout_of = [(i, j) for i in range(number) for j in range(size)]
        got = pl.pallas_call(
            partial(expert_kernel, layout_of, number, hidden),
            out_shape=(shape((size * ROWS, MODEL), BF),) * number
            + (shape((size * WIDE, MODEL), BF),) * number
            + ((shape((slots, MODEL), BF),) * 2 + (shape((slots, hidden), BF),) * 3) * 2,
            in_specs=[smem] + [vmem] * (2 * number + 7),
            out_specs=(vmem,) * (2 * number + 10),
            scratch_shapes=[
                pltpu.VMEM((2, slots, 4 * ROWS), BF),
                pltpu.VMEM((2, slots, MODEL), BF),
                pltpu.VMEM((2, slots, MODEL), BF),
                pltpu.VMEM((2, slots, MODEL), BF),
            ],
            compiler_params=params(),
        )(names, *[peers[i] for i in which], *[cots[i] for i in which], small, *tables)
        outs += got[:number]
        backs += got[number : 2 * number]
        saved[0].extend(got[2 * number : 2 * number + 5])
        saved[1].extend(got[2 * number + 5 :])

    def weight_grads(local, added):
        return pl.pallas_call(
            partial(weight_grad_kernel, len(calls), len(added) // 3),
            out_shape=(shape((hidden, MODEL), F32),) * 3,
            in_specs=[vmem] * (len(saved[local]) + len(added)),
            out_specs=(vmem,) * 3,
            compiler_params=params(),
        )(*saved[local], *added)

    back_pieces = sum_to_peers(backs, count)
    from_sibling = [permute(g, swap_perm(1, count)) for g in weight_grads(1, [])]
    gate_grad, up_grad, down_grad = weight_grads(0, from_sibling)
    out_pieces = sum_to_peers(outs, count)
    block_output = jnp.where(live_col, add_wide(residual, *out_pieces), 0.0).astype(BF)

    input_grad, mine, theirs = pl.pallas_call(
        partial(backward_kernel, len(dense), len(back_pieces)),
        out_shape=(
            shape((ROWS, MODEL), F32),
            shape((BLOCKS // 2 * PACK, MODEL), BF),
            shape((BLOCKS // 2 * PACK, MODEL), BF),
        ),
        in_specs=[smem] + [anywhere] * len(dense) + [vmem] * (len(back_pieces) + 12),
        out_specs=(vmem, anywhere, anywhere),
        scratch_shapes=[
            pltpu.VMEM((BLOCKS, PACK, MODEL), BF),
            pltpu.VMEM((BLOCKS, PACK, MODEL), BF),
            pltpu.VMEM((ROWS, MODEL), BF),
            pltpu.SemaphoreType.DMA((BLOCKS,)),
            pltpu.SemaphoreType.DMA((BLOCKS,)),
        ],
        compiler_params=params(),
    )(
        place, *dense, *back_pieces, moe_in, residual, own_cots, small, heads, query, keyvalue,
        probs, block_input, cosine, sine, live,
    )

    if count == 32:
        received = permute(theirs, swap_perm(1))
        edges = [i * PACK for i in list(range(9)) + [10, 12, 14, 16]]
        pieces = sum_to_peers(
            [add_round(mine[a:b], received[a:b]) for a, b in zip(edges[:-1], edges[1:])], count
        )
        total = add_wide(*pieces)
        query_grad, keyvalue_grad, output_weight_grad = [
            total[PART * i : PART * (i + 1)] for i in range(3)
        ]
        small_grad = jnp.concatenate([total[3 * PART :, 0:128], total[3 * PART :, 128:256]], axis=0)
    else:
        terms = jnp.concatenate([mine, theirs], axis=0).reshape(BLOCKS, PACK, MODEL).astype(F32)
        extra = terms[:, 3 * PART :, :256].reshape(BLOCKS, EXTRA, 2, 128).transpose(0, 2, 1, 3)
        wholes = [terms[:, PART * i : PART * (i + 1)].reshape(MODEL, MODEL) for i in range(3)]
        wholes.append(extra.reshape(MODEL, 128))
        query_grad, keyvalue_grad, output_weight_grad, small_grad = [
            lax.psum_scatter(w, "fsdp", scatter_dimension=0, tiled=True) for w in wholes
        ]
    return (
        block_output,
        input_grad,
        small_grad[:, EXPERT_COUNT],
        query_grad,
        keyvalue_grad,
        output_weight_grad,
        small_grad[:, EXPERT_COUNT + 1],
        small_grad[:, :EXPERT_COUNT],
        gate_grad,
        up_grad,
        down_grad,
    )


def solution(mesh):
    placed = (
        P("fsdp", None),
        P(),
        P(),
        P("fsdp", None),
        P("fsdp"),
        P("fsdp", None),
        P("fsdp", None),
        P("fsdp", None),
        P("fsdp"),
        P("fsdp", None),
        P("fsdp", None),
        P("fsdp", None),
        P("fsdp", None),
        P("fsdp", None),
    )
    return jax.shard_map(
        body,
        mesh=mesh,
        in_specs=placed,
        out_specs=(
            P("fsdp", None),
            P("fsdp", None),
            P("fsdp"),
            P("fsdp", None),
            P("fsdp", None),
            P("fsdp", None),
            P("fsdp"),
            P("fsdp", None),
            P("fsdp", None),
            P("fsdp", None),
            P("fsdp", None),
        ),
        check_vma=False,
    )
```

```python
from functools import partial

import jax
import jax.numpy as jnp
from jax import lax
from jax.experimental import pallas as pl
from jax.experimental.pallas import tpu as pltpu
from jax.sharding import PartitionSpec as P

QUERY_HEADS = 16
KEY_VALUE_HEADS = 8
HEAD_WIDTH = 64
EXPERT_COUNT = 32
EXPERT_HIDDEN = 512
TOPK = 8
CAP = 40

EPS = 1e-06
ROPE_BASE = 10000.0

MODEL = 1024
ROWS = 128
PART = 32
EXTRA = 16
PACK = 3 * PART + EXTRA
BLOCKS = MODEL // PART
WIDE = ROWS + EXTRA
WHOLE = PACK + ROWS
NOT_CHOSEN = 64
VMEM_LIMIT = 62 * 1024 * 1024
SMALL = 48

BF = jnp.bfloat16
F32 = jnp.float32


def dot(a, b, a_dim, b_dim):
    return lax.dot_general(a, b, (((a_dim,), (b_dim,)), ((), ())), preferred_element_type=F32)


def row_by_col(a, b):
    return dot(a, b, 1, 0)


def row_by_row(a, b):
    return dot(a, b, 1, 1)


def col_by_col(a, b):
    return dot(a, b, 0, 0)


GATES = {
    "heads back": ("sibling grad 0", "sibling grad 1", "sibling grad 2",),
    "sibling grad 0": ("g.a2",),
    "sibling grad 1": ("g.a3",),
    "sibling grad 2": ("g.c2",),
    "s.z2": ("input grad", "table grad 0",),
    "input grad": ("s.c2",),
    "table grad 0": ("s.b3",),
    "m.across3": ("experts near",),
    "experts near": ("m.z3",),
    "s.c2": ("s.a0",),
    "g.b0": ("g.a0",),
    "p.z2": ("s.c3",),
}


def layout(seq_lengths, seq_devices, device, count_of_rows):
    on_device = seq_devices == device
    lengths = jnp.where(on_device, seq_lengths, 0)
    starts = jnp.cumsum(lengths) - lengths
    filled_rows = jnp.sum(lengths)
    row_slots = jnp.arange(count_of_rows, dtype=jnp.int32)
    inside = (row_slots[:, None] >= starts[None, :]) & (
        row_slots[:, None] < (starts + lengths)[None, :]
    )
    live_rows = jnp.any(inside, axis=1)
    seq_count = seq_lengths.shape[0]
    numbers = jnp.arange(seq_count, dtype=jnp.int32)
    segment = jnp.where(
        live_rows, jnp.sum(jnp.where(inside, numbers[None, :], 0), axis=1), seq_count
    )
    begins = jnp.where(
        live_rows, jnp.sum(jnp.where(inside, starts[None, :], 0), axis=1), filled_rows
    )
    return (live_rows, segment, row_slots - begins)


def rope_tables(position):
    half = HEAD_WIDTH // 2
    lanes = jnp.arange(2 * HEAD_WIDTH, dtype=jnp.int32)
    exponent = (lanes % half).astype(F32) * 2.0 / HEAD_WIDTH
    angles = position.astype(F32)[:, None] * (ROPE_BASE ** (-exponent))[None, :]
    sign = jnp.where(lanes % HEAD_WIDTH < half, -1.0, 1.0)
    return jnp.cos(angles), jnp.sin(angles) * sign[None, :]


def permute(value, perm):
    return lax.ppermute(value, "fsdp", perm)


def swap_perm(mask, count=32):
    return [(i, i ^ mask) for i in range(count)]


def first_perm():
    return [(i, i ^ (4 if i % 2 == 0 else 2)) for i in range(32)]


def second_perm():
    return [(i, i ^ (2 if i % 2 == 0 else 4)) for i in range(32)]


def parity_groups(count):
    return [list(range(0, count, 2)), list(range(1, count, 2))]


def peer_plan(device, count):
    if count != 32:
        return [device % 2 + 2 * i for i in range(count // 2)]
    core = device % 2
    first = jnp.where(core == 0, 4, 2)
    second = 6 - first
    return [device ^ (8 * z) ^ step for z in range(4) for step in (0, first, second, 6)]


def behind(value, *others):
    return lax.optimization_barrier((value,) + others)[0] if others else value


STEPS = {
    "z1": ("", swap_perm(8)),
    "z2": ("", swap_perm(16)),
    "z3": ("z2", swap_perm(8)),
    "first0": ("", first_perm()),
    "second0": ("", second_perm()),
    "across0": ("first0", second_perm()),
    "first1": ("first0", swap_perm(8)),
    "second1": ("z1", second_perm()),
    "across1": ("across0", swap_perm(8)),
    "first2": ("z2", first_perm()),
    "second2": ("z2", second_perm()),
    "across2": ("first2", second_perm()),
    "first3": ("z3", first_perm()),
    "second3": ("z3", second_perm()),
    "across3": ("first3", second_perm()),
}
class Graph:
    def __init__(self, gates):
        self.gates, self.steps, self.have = gates, {}, {}

    def put(self, name, function, *needs):
        self.steps[name] = (function, needs)

    def get(self, name):
        if name not in self.have:
            self.have[name] = None
            function, needs = self.steps[name]
            values = [self.get(n) for n in needs]
            gates = [jax.tree.leaves(self.get(g))[0] for g in self.gates.get(name, ())]
            if gates and values:
                values[0] = jax.tree.map(lambda v: behind(v, *gates), values[0])
            with jax.named_scope(name.replace(" ", "_")):
                self.have[name] = function(*values)
        return self.have[name]


def put_permute(graph, name, perm, source, make=None):
    graph.put(name, lambda *v: permute(make(*v) if make else v[0], perm), *([source] if isinstance(source, str) else source))


def put_gather(graph, tag, source):
    for step, (base, perm) in STEPS.items():
        put_permute(graph, tag + step, perm, tag + base if base else source)


def gathered(tag, source):
    names = [[base, f"{tag}first{p}", f"{tag}second{p}", f"{tag}across{p}"] for p, base in enumerate((source, tag + "z1", tag + "z2", tag + "z3"))]
    return [n for plane in names for n in plane]


def put_sum(graph, tag, terms):
    own, one, two, three = [terms[4 * p : 4 * (p + 1)] for p in range(4)]
    for p, plane in ((2, two), (3, three)):
        put_permute(graph, f"{tag}a{p}", second_perm(), plane[3])
        put_permute(graph, f"{tag}b{p}", second_perm(), plane[2])
        put_permute(graph, f"{tag}c{p}", first_perm(), (plane[1], f"{tag}a{p}"), add_round)
    put_permute(graph, f"{tag}z3", swap_perm(8), (three[0], f"{tag}b3", f"{tag}c3"), add_round)
    put_permute(graph, f"{tag}z2", swap_perm(16), (two[0], f"{tag}b2", f"{tag}c2", f"{tag}z3"), add_round)
    put_permute(graph, f"{tag}b1", second_perm(), one[2])
    put_permute(graph, f"{tag}f1", swap_perm(8), one[1])
    put_permute(graph, f"{tag}d1", swap_perm(8), one[3])
    put_permute(graph, f"{tag}z1", swap_perm(8), (one[0], f"{tag}b1"), add_round)
    put_permute(graph, f"{tag}a0", second_perm(), (own[3], f"{tag}d1"), add_round)
    put_permute(graph, f"{tag}b0", second_perm(), own[2])
    put_permute(graph, f"{tag}c0", first_perm(), (own[1], f"{tag}f1", f"{tag}a0"), add_round)
    return [own[0]] + [f"{tag}{n}" for n in ("c0", "b0", "z1", "z2")]


def put_column_sum(graph, tag, parts):
    put_permute(graph, tag + "across", second_perm(), parts[3])
    put_permute(graph, tag + "second", second_perm(), parts[2])
    put_permute(graph, tag + "first", first_perm(), (parts[1], tag + "across"), add_round)
    graph.put(tag + "column", add_wide, parts[0], tag + "first", tag + "second")


def gather_whole(shard, count):
    whole = lax.all_gather(shard, "fsdp", axis=0, axis_index_groups=parity_groups(count))
    return [whole[i] for i in range(count // 2)]


def add_wide(*terms):
    return sum(t.astype(F32) for t in terms)


def add_round(*terms):
    return add_wide(*terms).astype(BF)


def sum_whole(terms, count):
    stacked = jnp.concatenate([t.astype(F32) for t in terms], axis=0)
    return [
        lax.psum_scatter(
            stacked, "fsdp", scatter_dimension=0, tiled=True, axis_index_groups=parity_groups(count)
        )
    ]


def filled_rows(device, lengths, devices):
    return lax.fori_loop(
        0,
        lengths.shape[0],
        lambda i, rows: rows + jnp.where(devices[i] == device[0], lengths[i], 0),
        jnp.int32(0),
    )


def pack_kernel(with_weights, device, lengths, devices, ids, out_grad, *refs):
    packed = refs[-1]
    if with_weights:
        query, keyvalue, output, router, attn_gain, moe_gain = refs[:-1]
        square = jnp.zeros((128, 128), F32)
        row = lax.broadcasted_iota(jnp.int32, (128, 128), 0)
        for i, gain in enumerate((attn_gain, moe_gain)):
            wide = jnp.concatenate(
                [gain[...].astype(F32).reshape(1, PART), jnp.zeros((1, 128 - PART), F32)], axis=1
            )
            square = jnp.where(row == EXPERT_COUNT + i, wide, square)
        small = square.T[:PART]
        small = small + jnp.concatenate(
            [router[...].astype(F32), jnp.zeros((PART, 128 - EXPERT_COUNT), F32)], axis=1
        )
        small = small.astype(BF)
        packed[0:PART, :] = query[...]
        packed[PART : 2 * PART, :] = keyvalue[...]
        packed[2 * PART : 3 * PART, :] = output[...]
        packed[3 * PART : PACK, :] = jnp.zeros((EXTRA, MODEL), BF)
        packed[3 * PART : PACK, 0:128] = small[0:EXTRA, :]
        packed[3 * PART : PACK, 128:256] = small[EXTRA:, :]
    else:
        packed[0:EXTRA, :] = jnp.zeros((EXTRA, MODEL), BF)
    filled = filled_rows(device, lengths, devices)
    first = PACK if with_weights else EXTRA
    rows = lax.broadcasted_iota(jnp.int32, (ROWS, MODEL), 0)
    packed[first : first + ROWS, :] = jnp.where(
        rows < filled, out_grad[...].astype(F32), 0.0
    ).astype(BF)
    wide = ids[...].astype(F32)
    expert = lax.broadcasted_iota(jnp.int32, (EXPERT_COUNT, ROWS), 0).astype(F32)
    hit = jnp.zeros((EXPERT_COUNT, ROWS), F32)
    for k in range(TOPK):
        hit = hit + jnp.where(expert == wide[k : k + 1, :], 1.0, 0.0)
    row = lax.broadcasted_iota(jnp.int32, (ROWS, ROWS), 0)
    column = lax.broadcasted_iota(jnp.int32, (ROWS, ROWS), 1)
    before = jnp.where(row < column, 1.0, 0.0).astype(BF)
    rank = row_by_col(hit.astype(BF), before)
    table = jnp.where(hit > 0.0, rank, float(NOT_CHOSEN)).astype(BF)
    packed[first - EXTRA : first, 256:384] = table[:EXTRA]
    packed[first - EXTRA : first, 384:512] = table[EXTRA:]


def join_kernel(rows, *refs):
    parts, out, sems = refs[:-2], refs[-2], refs[-1]
    copies = [
        pltpu.make_async_copy(part.at[pl.ds(0, rows)], out.at[pl.ds(rows * i, rows)], sems.at[i])
        for i, part in enumerate(parts)
    ]
    for copy in copies:
        copy.start()
    for copy in copies:
        copy.wait()


def start_weights(place, buffers, weights, sems, first, last):
    copies = []
    for buffer in buffers:
        for j in range(buffer.shape[0] // PACK if buffer.shape[0] != WHOLE else 1):
            i = len(copies)
            copies.append(
                pltpu.make_async_copy(
                    buffer.at[pl.ds(j * PACK + first, last - first)], weights.at[place[i]], sems.at[i]
                )
            )
            copies[-1].start()
    return copies


def half_swap(chunk):
    lane = lax.broadcasted_iota(jnp.int32, chunk.shape, 1)
    half = HEAD_WIDTH // 2
    return jnp.where(
        lane % HEAD_WIDTH < half, pltpu.roll(chunk, 128 - half, 1), pltpu.roll(chunk, half, 1)
    )


def doubled(chunk, second):
    lane = lax.broadcasted_iota(jnp.int32, chunk.shape, 1)
    turned = pltpu.roll(chunk, HEAD_WIDTH, 1)
    keep = lane >= HEAD_WIDTH if second else lane < HEAD_WIDTH
    return jnp.where(keep, chunk, turned)


def split_pair(chunk):
    lane = lax.broadcasted_iota(jnp.int32, chunk.shape, 1)
    zero = jnp.zeros_like(chunk)
    return jnp.concatenate(
        [jnp.where(lane < HEAD_WIDTH, chunk, zero), jnp.where(lane < HEAD_WIDTH, zero, chunk)], axis=0
    )


def join_pair(stacked):
    lane = lax.broadcasted_iota(jnp.int32, (ROWS, 128), 1)
    return jnp.where(lane < HEAD_WIDTH, stacked[:ROWS], stacked[ROWS:])


def attention_kernel(buffers_count, *refs):
    place, buffers, refs = refs[0], refs[1 : 1 + buffers_count], refs[1 + buffers_count :]
    x_ref, cos_ref, sin_ref, allowed_ref = refs[:4]
    moe_ref, resid_ref, share_ref, query_ref, kv_ref, probs_ref, small_ref = refs[4:11]
    weights, columns, sems = refs[11:]
    copies = start_weights(place, buffers, weights, sems, 0, PACK)
    x = x_ref[...].astype(F32)
    unit = x * lax.rsqrt(jnp.mean(x * x, axis=-1, keepdims=True) + EPS)
    for copy in copies:
        copy.wait()
    for p in range(BLOCKS):
        for j in range(2):
            columns[pl.ds(p * PART + j * EXTRA, EXTRA), :] = weights[
                p, 3 * PART :, 128 * j : 128 * (j + 1)
            ].astype(F32)
    small = columns[...].T
    small_ref[...] = small.astype(BF)
    attn_in = (unit * small[EXPERT_COUNT : EXPERT_COUNT + 1, :]).astype(BF)
    share_ref[:ROWS, :] = attn_in
    cosine, sine = cos_ref[...], sin_ref[...]

    def weight_columns(which, chunk):
        lanes = slice(256 * chunk, 256 * (chunk + 1))
        return weights[:, PART * which : PART * (which + 1), lanes].reshape(MODEL, 256)

    for chunk in range(4):
        query_pre = row_by_col(attn_in, weight_columns(0, chunk))
        kv_pre = row_by_col(attn_in, weight_columns(1, chunk))
        for j in range(2):
            at = slice(256 * chunk + 128 * j, 256 * chunk + 128 * (j + 1))
            part = query_pre[:, 128 * j : 128 * (j + 1)]
            query_ref[:, at] = (part * cosine + half_swap(part) * sine).astype(BF)
            part = kv_pre[:, 128 * j : 128 * (j + 1)]
            if chunk < 2:
                part = part * cosine + half_swap(part) * sine
            kv_ref[:, at] = part.astype(BF)
    allowed = jnp.concatenate([allowed_ref[...], allowed_ref[...]], axis=0) > 0.0
    scale = HEAD_WIDTH ** (-0.5)
    for head in range(KEY_VALUE_HEADS):
        pair, second = head // 2, head % 2 == 1
        key = doubled(kv_ref[:, 128 * pair : 128 * (pair + 1)].astype(F32), second).astype(BF)
        value = doubled(
            kv_ref[:, 512 + 128 * pair : 512 + 128 * (pair + 1)].astype(F32), second
        ).astype(BF)
        at = slice(128 * head, 128 * (head + 1))
        scores = row_by_row(split_pair(query_ref[:, at]), key) * scale
        scores = jnp.where(allowed, scores, -jnp.inf)
        raised = jnp.exp(scores - jnp.max(scores, axis=-1, keepdims=True))
        probs = raised / jnp.sum(raised, axis=-1, keepdims=True)
        probs_ref[head] = probs
        share_ref[ROWS:, at] = join_pair(row_by_col(probs.astype(BF), value)).astype(BF)
    heads = share_ref[ROWS:, :]
    for chunk in range(4):
        at = slice(256 * chunk, 256 * (chunk + 1))
        resid_ref[:, at] = x_ref[:, at].astype(F32) + row_by_col(heads, weight_columns(2, chunk))
    residual = resid_ref[...]
    unit = residual * lax.rsqrt(jnp.mean(residual * residual, axis=-1, keepdims=True) + EPS)
    moe_ref[...] = (unit * small[EXPERT_COUNT + 1 : EXPERT_COUNT + 2, :]).astype(BF)


def route_table(extra):
    return jnp.concatenate([extra[:, 0:128], extra[:, 128:256]], axis=0).astype(F32)


def route_weights_of(table, small, rows):
    logits = row_by_row(small, rows)[:EXPERT_COUNT]
    raised = jnp.where(table < NOT_CHOSEN, jnp.exp(logits), 0.0)
    return raised / jnp.sum(raised, axis=0, keepdims=True)


def expert_kernel(sizes, *refs):
    x_sizes, c_first = sizes
    names, refs = refs[0], refs[1:]
    x_hbm, refs = refs[: len(x_sizes)], refs[len(x_sizes) :]
    c_hbm, refs = refs[:8], refs[8:]
    small_ref, tables_hbm, refs = refs[0], refs[1:7], refs[7:]
    p_hbm, g_hbm, saved_hbm, refs = refs[:4], refs[4:12], refs[12:22], refs[22:]
    xs_all, cs_all, tables, ps, gs, saved_wide, saved_thin, picks, cots, results, back, in_sems, out_sems = refs
    copies = []

    def fetch(source, target):
        copies.append(pltpu.make_async_copy(source, target, in_sems.at[len(copies)]))
        copies[-1].start()

    def send(source, target, number):
        copy = pltpu.make_async_copy(source, target, out_sems.at[number])
        copy.start()
        return copy

    at = 0
    for ref, size in zip(x_hbm, x_sizes):
        for j in range(size):
            fetch(ref.at[pl.ds(ROWS * j, ROWS)], xs_all.at[at])
            at += 1
    for i, ref in enumerate(c_hbm):
        fetch(ref.at[pl.ds(c_first, WIDE)], cs_all.at[i])
    for i, ref in enumerate(tables_hbm):
        fetch(ref, tables.at[i])
    slots = 4 * CAP
    small = small_ref[...]
    expert_row = lax.broadcasted_iota(jnp.int32, (EXPERT_COUNT, ROWS), 0)
    slot_row = lax.broadcasted_iota(jnp.int32, (slots, 4 * ROWS), 0).astype(F32)
    slot_weights = [[None, None], [None, None]]
    for copy in copies[:16]:
        copy.wait()
    for h in range(2):
        places, weights = [[], []], [[], []]
        for b in range(4):
            table = route_table(cs_all[4 * h + b, :EXTRA, 256:512])
            weight = route_weights_of(table, small, xs_all[4 * h + b])
            for l in range(2):
                here = expert_row == names[l]
                place = jnp.sum(jnp.where(here, table, 0.0), axis=0, keepdims=True)
                places[l].append(jnp.where(place < NOT_CHOSEN, place + b * CAP, 4096.0))
                weights[l].append(jnp.sum(jnp.where(here, weight, 0.0), axis=0, keepdims=True))
        for l in range(2):
            chosen = slot_row == jnp.concatenate(places[l], axis=1)
            weight = jnp.concatenate(weights[l], axis=1)
            slot_weights[l][h] = jnp.sum(jnp.where(chosen, weight, 0.0), axis=1, keepdims=True)
            picks[h, slots * l : slots * (l + 1), :] = chosen.astype(F32).astype(BF)
        pick = picks[h]
        rows = xs_all[4 * h : 4 * (h + 1)].reshape(4 * ROWS, MODEL)
        cot_rows = cs_all[4 * h : 4 * (h + 1), EXTRA:, :].reshape(4 * ROWS, MODEL)
        inputs = row_by_col(pick, rows).astype(BF)
        cot = row_by_col(pick, cot_rows).astype(BF)
        for l in range(2):
            saved_wide[2 * l, slots * h : slots * (h + 1), :] = inputs[slots * l : slots * (l + 1)]
            cots[l, slots * h : slots * (h + 1), :] = cot[slots * l : slots * (l + 1)]
    slot_routes, sends = [], []
    for l in range(2):
        gate, up, down = tables.at[3 * l], tables.at[3 * l + 1], tables.at[3 * l + 2]
        for copy in copies[16 + 3 * l : 19 + 3 * l]:
            copy.wait()
        weight = jnp.concatenate(slot_weights[l], axis=0)
        inputs = saved_wide[2 * l]
        gate_pre = row_by_row(inputs, gate[...])
        up_pre = row_by_row(inputs, up[...])
        sigma = jax.nn.sigmoid(gate_pre)
        acts = (gate_pre * sigma * up_pre).astype(BF)
        saved_thin[3 * l] = acts
        cot = cots[l].astype(F32)
        result = row_by_col(acts, down[...])
        slot_routes.append(jnp.sum(cot * result, axis=1, keepdims=True))
        results[l] = (weight * result).astype(BF)
        pair_cot = (weight * cot).astype(BF)
        saved_wide[2 * l + 1] = pair_cot
        act_grad = row_by_row(pair_cot, down[...])
        gate_grad = (act_grad * up_pre * sigma * (1.0 + gate_pre * (1.0 - sigma))).astype(BF)
        up_grad = (act_grad * gate_pre * sigma).astype(BF)
        saved_thin[3 * l + 1] = gate_grad
        saved_thin[3 * l + 2] = up_grad
        back[l] = (row_by_col(gate_grad, gate[...]) + row_by_col(up_grad, up[...])).astype(BF)
        for i in range(5):
            source = saved_wide.at[2 * l + i] if i < 2 else saved_thin.at[3 * l + i - 2]
            sends.append(send(source, saved_hbm[5 * l + i], 16 + 5 * l + i))
    for h in range(2):
        pick = picks[h]
        at = slice(slots * h, slots * (h + 1))
        grad = col_by_col(pick, jnp.concatenate([back[0, at], back[1, at]], axis=0)).astype(BF)
        routes = []
        for l in range(2):
            chosen = pick[slots * l : slots * (l + 1)].astype(F32)
            routes.append(jnp.sum(chosen * slot_routes[l][at], axis=0, keepdims=True))
        for b in range(4):
            i = 4 * h + b
            rows = slice(ROWS * b, ROWS * (b + 1))
            gs[i, :ROWS, :] = grad[rows]
            route = jnp.zeros((EXPERT_COUNT, ROWS), F32)
            for l in range(2):
                route = route + jnp.where(expert_row == names[l], routes[l][:, rows], 0.0)
            high = route.astype(BF)
            low = (route - high.astype(F32)).astype(BF)
            gs[i, ROWS:, 0:128] = high[:16]
            gs[i, ROWS:, 128:256] = high[16:]
            gs[i, ROWS:, 256:384] = low[:16]
            gs[i, ROWS:, 384:512] = low[16:]
            gs[i, ROWS:, 512:] = jnp.zeros((EXTRA, MODEL - 512), BF)
            sends.append(send(gs.at[i], g_hbm[i], 8 + i))
        out = col_by_col(pick, jnp.concatenate([results[0, at], results[1, at]], axis=0)).astype(BF)
        for b in range(4):
            i = 4 * h + b
            ps[i] = out[ROWS * b : ROWS * (b + 1)]
            sends.append(send(ps.at[i], p_hbm[i % 4].at[pl.ds(ROWS * (i // 4), ROWS)], i))
    for copy in sends:
        copy.wait()


def weight_grad_kernel(calls, *refs):
    saved, added, out = refs[: 2 * calls], refs[2 * calls : -1], refs[-1]
    total = added[0][...] if added else None
    for c in range(calls):
        term = col_by_col(saved[2 * c][...], saved[2 * c + 1][...])
        total = term if total is None else total + term
    out[...] = total


def head_backward_kernel(buffers_count, pieces_count, *refs):
    place, buffers, refs = refs[0], refs[1 : 1 + buffers_count], refs[1 + buffers_count :]
    pieces, refs = refs[:pieces_count], refs[pieces_count:]
    moe_ref, resid_ref, cot_ref, small_ref, share_ref, query_ref, kv_ref, probs_ref = refs[:8]
    cos_ref, sin_ref = refs[8:10]
    resid_grad_ref, grads_ref = refs[10:12]
    weights, grads, sems = refs[12:]
    copies = start_weights(place, buffers, weights, sems, 2 * PART, 3 * PART)
    small = small_ref[...]
    total = pieces[0][...].astype(F32)
    for piece in pieces[1:]:
        total = total + piece[...].astype(F32)
    extra = total[ROWS:]
    route_grad = jnp.concatenate(
        [extra[:, 0:128] + extra[:, 256:384], extra[:, 128:256] + extra[:, 384:512]], axis=0
    )
    moe_in = moe_ref[...]
    first = cot_ref.shape[0] - WIDE
    table = route_table(cot_ref[first : first + EXTRA, 256:512])
    weight = route_weights_of(table, small, moe_in)
    logit_grad = weight * (route_grad - jnp.sum(weight * route_grad, axis=0, keepdims=True))
    logit_grad = jnp.concatenate(
        [logit_grad, jnp.zeros((ROWS - EXPERT_COUNT, ROWS), F32)], axis=0
    ).astype(BF)
    moe_in_grad = total[:ROWS] + col_by_col(logit_grad, small)
    router_grad = row_by_col(logit_grad, moe_in)[:SMALL]
    residual = resid_ref[...]
    inverse = lax.rsqrt(jnp.mean(residual * residual, axis=-1, keepdims=True) + EPS)
    unit = residual * inverse
    moe_gain_grad = jnp.sum(moe_in_grad * unit, axis=0, keepdims=True)
    row = lax.broadcasted_iota(jnp.int32, (SMALL, MODEL), 0)
    grads_ref[3 * ROWS :, :] = jnp.where(row == EXPERT_COUNT + 1, moe_gain_grad, router_grad).astype(BF)
    grad_unit = moe_in_grad * small[EXPERT_COUNT : EXPERT_COUNT + 8].astype(F32)[1:2]
    mean = jnp.mean(grad_unit * unit, axis=-1, keepdims=True)
    cot = cot_ref[first + EXTRA :, :]
    residual_grad = cot.astype(F32) + inverse * (grad_unit - unit * mean)
    resid_grad_ref[...] = residual_grad
    residual_bf = residual_grad.astype(BF)
    grads_ref[:ROWS, :] = residual_bf
    for copy in copies:
        copy.wait()
    for chunk in range(4):
        at = slice(256 * chunk, 256 * (chunk + 1))
        rows = weights[8 * chunk : 8 * (chunk + 1)].reshape(256, MODEL)
        grads[:, at] = row_by_row(residual_bf, rows).astype(BF)
    cosine, sine = cos_ref[...], sin_ref[...]
    scale = HEAD_WIDTH ** (-0.5)
    key_grads, value_grads = [], []
    for head in range(KEY_VALUE_HEADS):
        pair, second = head // 2, head % 2 == 1
        key = doubled(kv_ref[:, 128 * pair : 128 * (pair + 1)].astype(F32), second).astype(BF)
        value = doubled(
            kv_ref[:, 512 + 128 * pair : 512 + 128 * (pair + 1)].astype(F32), second
        ).astype(BF)
        at = slice(128 * head, 128 * (head + 1))
        query = split_pair(query_ref[:, at])
        head_grad = split_pair(grads[:, at])
        mixed = split_pair(share_ref[ROWS:, at])
        inner = jnp.sum(head_grad.astype(F32) * mixed.astype(F32), axis=-1, keepdims=True)
        probs = probs_ref[head]
        score_grad = (probs * (row_by_row(head_grad, value) - inner)).astype(BF)
        part = join_pair(row_by_col(score_grad, key)) * scale
        grads_ref[ROWS : 2 * ROWS, at] = (part * cosine - half_swap(part) * sine).astype(BF)
        part = col_by_col(score_grad, query) * scale
        key_grads.append(part + pltpu.roll(part, HEAD_WIDTH, 1))
        part = col_by_col(probs.astype(BF), head_grad)
        value_grads.append(part + pltpu.roll(part, HEAD_WIDTH, 1))
    lane = lax.broadcasted_iota(jnp.int32, (ROWS, 128), 1)
    for which, parts in enumerate((key_grads, value_grads)):
        for pair in range(KEY_VALUE_HEADS // 2):
            part = jnp.where(lane < HEAD_WIDTH, parts[2 * pair], parts[2 * pair + 1])
            if which == 0:
                part = part * cosine - half_swap(part) * sine
            at = slice(512 * which + 128 * pair, 512 * which + 128 * (pair + 1))
            grads_ref[2 * ROWS : 3 * ROWS, at] = part.astype(BF)


def input_grad_kernel(buffers_count, place, device, lengths, devices, *refs):
    buffers, refs = refs[:buffers_count], refs[buffers_count:]
    grads_ref, resid_grad_ref, small_ref, x_ref, in_ref = refs[:5]
    weights, sems = refs[5:]
    copies = start_weights(place, buffers, weights, sems, 0, 2 * PART)
    x = x_ref[...].astype(F32)
    inverse = lax.rsqrt(jnp.mean(x * x, axis=-1, keepdims=True) + EPS)
    unit = x * inverse
    query_grad, kv_grad = grads_ref[ROWS : 2 * ROWS, :], grads_ref[2 * ROWS : 3 * ROWS, :]
    for copy in copies:
        copy.wait()
    back = []
    for chunk in range(4):
        rows = weights[8 * chunk : 8 * (chunk + 1)]
        back.append(
            row_by_row(query_grad, rows[:, :PART].reshape(256, MODEL))
            + row_by_row(kv_grad, rows[:, PART:].reshape(256, MODEL))
        )
    attn_in_grad = jnp.concatenate(back, axis=1)
    grad_unit = attn_in_grad * small_ref[EXPERT_COUNT : EXPERT_COUNT + 8].astype(F32)[0:1]
    mean = jnp.mean(grad_unit * unit, axis=-1, keepdims=True)
    input_grad = resid_grad_ref[...] + inverse * (grad_unit - unit * mean)
    rows = lax.broadcasted_iota(jnp.int32, (ROWS, MODEL), 0)
    in_ref[...] = jnp.where(rows < filled_rows(device, lengths, devices), input_grad, 0.0)


def dense_grad_kernel(parties, blocks, *refs):
    place, refs = refs[0], refs[1:]
    shares, grads, refs = refs[:parties], refs[parties : 2 * parties], refs[2 * parties :]
    outs, terms = refs[:blocks], refs[blocks]
    attn_in = jnp.concatenate([r[:ROWS, :] for r in shares], axis=0)
    heads = jnp.concatenate([r[ROWS:, :] for r in shares], axis=0)
    residual, query, keyvalue = [
        jnp.concatenate([r[ROWS * i : ROWS * (i + 1), :] for r in grads], axis=0) for i in range(3)
    ]
    for chunk in range(4):
        at = slice(256 * chunk, 256 * (chunk + 1))
        for which, left, right in ((0, attn_in, query), (1, attn_in, keyvalue), (2, heads, residual)):
            term = col_by_col(left[:, at], right).astype(BF).reshape(8, PART, MODEL)
            terms[8 * chunk : 8 * (chunk + 1), PART * which : PART * (which + 1), :] = term
    columns = sum(r[3 * ROWS :, :].astype(F32) for r in grads)
    columns = jnp.concatenate([columns, jnp.zeros((128 - SMALL, MODEL), F32)], axis=0).T.astype(BF)
    for p in range(BLOCKS):
        for j in range(2):
            terms[p, 3 * PART :, 128 * j : 128 * (j + 1)] = columns[
                p * PART + j * EXTRA : p * PART + (j + 1) * EXTRA
            ]
        terms[p, 3 * PART :, 256:] = jnp.zeros((EXTRA, MODEL - 256), BF)
    for i in range(blocks):
        outs[i][...] = terms[place[i]]


def params():
    return pltpu.CompilerParams(vmem_limit_bytes=VMEM_LIMIT)


def shape(dims, dtype):
    return jax.ShapeDtypeStruct(dims, dtype)


def spec(space):
    return pl.BlockSpec(memory_space=space)


def pack_call(sequences, expert_ids, output_grad, *weights):
    smem, vmem = spec(pltpu.SMEM), spec(pltpu.VMEM)
    return pl.pallas_call(
        partial(pack_kernel, bool(weights)),
        out_shape=shape((WHOLE if weights else WIDE, MODEL), BF),
        in_specs=[smem] * 3 + [vmem] * (2 + len(weights)),
        out_specs=vmem,
        compiler_params=params(),
    )(*sequences, expert_ids.T, output_grad, *weights)


def join_call(rows, *parts):
    anywhere = spec(pl.ANY)
    return pl.pallas_call(
        partial(join_kernel, rows),
        out_shape=shape((rows * len(parts), MODEL), BF),
        in_specs=[anywhere] * len(parts),
        out_specs=spec(pltpu.VMEM),
        scratch_shapes=[pltpu.SemaphoreType.DMA((len(parts),))],
        compiler_params=params(),
    )(*parts)


def attention_call(place, block_input, cosine, sine, allowed, *dense):
    vmem = spec(pltpu.VMEM)
    return pl.pallas_call(
        partial(attention_kernel, len(dense)),
        out_shape=(
            shape((ROWS, MODEL), BF),
            shape((ROWS, MODEL), F32),
            shape((2 * ROWS, MODEL), BF),
            shape((ROWS, MODEL), BF),
            shape((ROWS, MODEL), BF),
            shape((KEY_VALUE_HEADS, 2 * ROWS, ROWS), F32),
            shape((128, MODEL), BF),
        ),
        in_specs=[spec(pltpu.SMEM)] + [spec(pl.ANY)] * len(dense) + [vmem] * 4,
        out_specs=(vmem,) * 7,
        scratch_shapes=[
            pltpu.VMEM((BLOCKS, PACK, MODEL), BF),
            pltpu.VMEM((MODEL, 128), F32),
            pltpu.SemaphoreType.DMA((BLOCKS,)),
        ],
        compiler_params=params(),
    )(place, *dense, block_input, cosine, sine, allowed)


def expert_call(first, small, tables, names, *rows_and_cots):
    hidden, slots = tables[0].shape[0], 8 * CAP
    anywhere = spec(pl.ANY)
    got = pl.pallas_call(
        partial(expert_kernel, ((1,) * 8, first)),
        out_shape=(shape((2 * ROWS, MODEL), BF),) * 4
        + (shape((WIDE, MODEL), BF),) * 8
        + ((shape((slots, MODEL), BF),) * 2 + (shape((slots, hidden), BF),) * 3) * 2,
        in_specs=[spec(pltpu.SMEM)] + [anywhere] * 16 + [spec(pltpu.VMEM)] + [anywhere] * 6,
        out_specs=(anywhere,) * 22,
        scratch_shapes=[
            pltpu.VMEM((8, ROWS, MODEL), BF),
            pltpu.VMEM((8, WIDE, MODEL), BF),
            pltpu.VMEM((6, hidden, MODEL), BF),
            pltpu.VMEM((8, ROWS, MODEL), BF),
            pltpu.VMEM((8, WIDE, MODEL), BF),
            pltpu.VMEM((4, slots, MODEL), BF),
            pltpu.VMEM((6, slots, hidden), BF),
            pltpu.VMEM((2, slots, 4 * ROWS), BF),
            pltpu.VMEM((2, slots, MODEL), BF),
            pltpu.VMEM((2, slots, MODEL), BF),
            pltpu.VMEM((2, slots, MODEL), BF),
            pltpu.SemaphoreType.DMA((22,)),
            pltpu.SemaphoreType.DMA((26,)),
        ],
        compiler_params=params(),
    )(names, *rows_and_cots, small, *tables)
    return got[:4], got[4:12], got[12:17], got[17:]


def weight_grad_call(which, calls, *added):
    left, right = ((3, 0), (4, 0), (2, 1))[which]
    saves = [saved[i] for saved in calls for i in (left, right)]
    vmem = spec(pltpu.VMEM)
    return pl.pallas_call(
        partial(weight_grad_kernel, len(calls)),
        out_shape=shape((saves[0].shape[1], MODEL), F32),
        in_specs=[vmem] * (len(saves) + len(added)),
        out_specs=vmem,
        compiler_params=params(),
    )(*saves, *added)


def head_backward_call(place, dense, pieces, others):
    vmem = spec(pltpu.VMEM)
    return pl.pallas_call(
        partial(head_backward_kernel, len(dense), len(pieces)),
        out_shape=(shape((ROWS, MODEL), F32), shape((3 * ROWS + SMALL, MODEL), BF)),
        in_specs=[spec(pltpu.SMEM)] + [spec(pl.ANY)] * len(dense) + [vmem] * (len(pieces) + 10),
        out_specs=(vmem,) * 2,
        scratch_shapes=[
            pltpu.VMEM((BLOCKS, PART, MODEL), BF),
            pltpu.VMEM((ROWS, MODEL), BF),
            pltpu.SemaphoreType.DMA((BLOCKS,)),
        ],
        compiler_params=params(),
    )(place, *dense, *pieces, *others)


def dense_grad_call(blocks, place, *parties):
    vmem = spec(pltpu.VMEM)
    return pl.pallas_call(
        partial(dense_grad_kernel, len(parties) // 2, blocks),
        out_shape=(shape((PACK, MODEL), BF),) * blocks,
        in_specs=[spec(pltpu.SMEM)] + [vmem] * len(parties),
        out_specs=(vmem,) * blocks,
        scratch_shapes=[pltpu.VMEM((BLOCKS, PACK, MODEL), BF)],
        compiler_params=params(),
    )(place, *parties)


def input_grad_call(place, sequences, dense, *others):
    smem, vmem = spec(pltpu.SMEM), spec(pltpu.VMEM)
    return pl.pallas_call(
        partial(input_grad_kernel, len(dense)),
        out_shape=shape((ROWS, MODEL), F32),
        in_specs=[smem] * 4 + [spec(pl.ANY)] * len(dense) + [vmem] * 4,
        out_specs=vmem,
        scratch_shapes=[
            pltpu.VMEM((BLOCKS, 2 * PART, MODEL), BF),
            pltpu.SemaphoreType.DMA((BLOCKS,)),
        ],
        compiler_params=params(),
    )(place, *sequences, *dense, *others)


def attention_inputs(seq_lengths, seq_devices, device):
    live_rows, segment, position = layout(seq_lengths, seq_devices, device, ROWS)
    row_slots = jnp.arange(ROWS, dtype=jnp.int32)
    allowed = (segment[:, None] == segment[None, :]) & (row_slots[:, None] >= row_slots[None, :])
    return live_rows, (*rope_tables(position), allowed.astype(F32))


def finish(live_rows, residual, out_pieces, gain, weights, grads):
    block_output = jnp.where(live_rows[:, None], add_wide(residual, *out_pieces), 0.0).astype(BF)
    weighted = sum(w.astype(F32) * g for w, g in zip(weights, grads))
    return block_output, jnp.sum(weighted, axis=1) / gain.astype(F32)


def small_columns(rows):
    return jnp.concatenate([rows[..., 0:128], rows[..., 128:256]], axis=-2)


def graph_on_slice(device, inputs):
    (block_input, seq_lengths, seq_devices, expert_ids, attn_gain, query_weight, keyvalue_weight,
     output_weight, moe_gain, router_weight, gate_weight, up_weight, down_weight, output_grad) = inputs
    own_tables = (gate_weight, up_weight, down_weight)
    sequences = (device.reshape(1), seq_lengths, seq_devices)
    names = jnp.stack([device, device ^ 1])
    graph = Graph(GATES)
    put = graph.put

    weights = (query_weight, keyvalue_weight, output_weight, router_weight, attn_gain, moe_gain)
    put("packed", lambda: pack_call(sequences, expert_ids, output_grad, *weights))
    put_gather(graph, "d.", "packed")
    cots = gathered("d.", "packed")
    for i, table in enumerate(own_tables):
        put(f"tables {i}", lambda table=table: permute(table, swap_perm(1)))
    early = [n for n in cots if n not in ("d.across1", "d.across2", "d.first3", "d.second3", "d.across3")]
    late = ["d.across1", "d.across2", "d.first3", "d.second3"]
    for name, parts in (("early", early), ("late", late)):
        put("joined " + name, partial(join_call, PACK), *parts)
        put_permute(graph, "sibling " + name, swap_perm(1), "joined " + name)
    put_permute(graph, "sibling last", swap_perm(1), "d.across3")
    dense = cots + ["sibling early", "sibling late", "sibling last"]
    order = cots + early + late + ["d.across3"]
    at = {n: i for i, n in enumerate(cots)}
    plan = peer_plan(device, 32), peer_plan(device ^ 1, 32)
    place = jnp.stack([plan[i // 16][at[n]] for i, n in enumerate(order)])

    put("layout", lambda v: attention_inputs(behind(seq_lengths, v), seq_devices, device), "packed")
    put("attention", lambda l, *v: attention_call(place, block_input, *l[1], *v), "layout", *dense)
    for i, name in enumerate(("moe in", "residual", "share", "query", "keyvalue", "probs", "small")):
        put(name, lambda v, i=i: v[i], "attention")
    put_permute(graph, "share sibling", swap_perm(1), "share")

    put_gather(graph, "m.", "moe in")
    rows = gathered("m.", "moe in")
    for name, at in (("near", slice(0, 8)), ("far", slice(8, 16))):
        put(
            "experts " + name,
            lambda small, *v: expert_call(3 * PART, small, (*own_tables, *v[:3]), names, *v[3:]),
            "small", "tables 0", "tables 1", "tables 2", *rows[at], *cots[at],
        )
        for i in range(4):
            put(f"out {name} {i}", lambda v, i=i: v[0][i], "experts " + name)
        for i in range(8):
            put(f"back {name} {i}", lambda v, i=i: v[1][i], "experts " + name)
    for i in range(3):
        put(f"sibling grad {i}", lambda a, b, i=i: weight_grad_call(i, (a[3], b[3])), "experts near", "experts far")
        put_permute(graph, f"received grad {i}", swap_perm(1), f"sibling grad {i}")
        put(
            f"table grad {i}", lambda r, a, b, i=i: weight_grad_call(i, (a[2], b[2]), r),
            f"received grad {i}", "experts near", "experts far",
        )

    back_pieces = put_sum(graph, "g.", [f"back {n} {i}" for n in ("near", "far") for i in range(8)])
    put_column_sum(graph, "p.far ", [f"out far {i}" for i in range(4)])
    put_column_sum(graph, "p.near ", [f"out near {i}" for i in range(4)])
    put_permute(
        graph, "p.z1", swap_perm(8), ("p.near column", "p.far column"),
        lambda n, f: jnp.concatenate([n[ROWS:], f[ROWS:]], axis=0).astype(BF),
    )
    put_permute(graph, "p.z2", swap_perm(16), ("p.far column", "p.z1"), lambda f, z: add_round(f[:ROWS], z[ROWS:]))

    others = ["moe in", "residual", "packed", "small", "share", "query", "keyvalue", "probs"]
    put(
        "heads back",
        lambda *v: head_backward_call(place, v[:19], v[19:24], (*v[24:32], *v[32][1][:2])),
        *dense, *back_pieces, *others, "layout",
    )
    put("grads", lambda v: v[1], "heads back")
    put_permute(graph, "grads sibling", swap_perm(1), "grads")
    put(
        "dense grads",
        lambda *v: dense_grad_call(BLOCKS // 2, place, *v),
        "share", "share sibling", "grads", "grads sibling",
    )
    for i in range(16):
        put(f"term {i}", lambda v, i=i: v[i], "dense grads")
    pieces = put_sum(graph, "s.", [f"term {i}" for i in range(16)])
    put("total", add_wide, *pieces)
    put(
        "input grad",
        lambda h, g, small, *v: input_grad_call(place, sequences, v, g, h[0], small, block_input),
        "heads back", "grads", "small", *dense,
    )

    return graph


def body_on_slice(device, inputs):
    attn_gain, query_weight, keyvalue_weight = inputs[4:7]
    graph = graph_on_slice(device, inputs)
    total = graph.get("total")
    query_grad, keyvalue_grad, output_weight_grad = [total[PART * i : PART * (i + 1)] for i in range(3)]
    small_grad = small_columns(total[3 * PART :])
    block_output, attn_gain_grad = finish(
        graph.get("layout")[0],
        graph.get("residual"),
        (graph.get("p.near column")[:ROWS], graph.get("p.z1")[:ROWS], graph.get("p.z2")),
        attn_gain,
        (query_weight, keyvalue_weight),
        (query_grad, keyvalue_grad),
    )
    return (
        block_output,
        graph.get("input grad"),
        attn_gain_grad,
        query_grad,
        keyvalue_grad,
        output_weight_grad,
        small_grad[:, EXPERT_COUNT + 1],
        small_grad[:, :EXPERT_COUNT],
        *[graph.get(f"table grad {i}") for i in range(3)],
    )


def body_elsewhere(device, count, inputs):
    (block_input, seq_lengths, seq_devices, expert_ids, attn_gain, query_weight, keyvalue_weight,
     output_weight, moe_gain, router_weight, gate_weight, up_weight, down_weight, output_grad) = inputs
    own_tables = (gate_weight, up_weight, down_weight)
    sequences = (device.reshape(1), seq_lengths, seq_devices)
    hidden = gate_weight.shape[0]
    packed = pack_call(sequences, expert_ids, output_grad)
    small = jnp.concatenate([router_weight, attn_gain[:, None], moe_gain[:, None]], axis=1)
    small = jnp.pad(small, ((0, 0), (0, 128 - small.shape[1])))
    whole = [
        lax.all_gather(w, "fsdp", axis=0, tiled=True)
        for w in (query_weight, keyvalue_weight, output_weight, small)
    ]
    extra = whole[3].reshape(BLOCKS, 2, EXTRA, 128).transpose(0, 2, 1, 3).reshape(BLOCKS, EXTRA, 256)
    extra = jnp.pad(extra, ((0, 0), (0, 0), (0, MODEL - 256)))
    dense = jnp.concatenate([w.reshape(BLOCKS, PART, MODEL) for w in whole[:3]] + [extra], axis=1)
    dense = dense.reshape(BLOCKS * PACK, MODEL)
    place = jnp.arange(BLOCKS, dtype=jnp.int32)
    names = jnp.stack([device, device ^ 1]) * hidden // EXPERT_HIDDEN
    tables = (*own_tables, *(permute(t, swap_perm(1, count)) for t in own_tables))
    live_rows, others = attention_inputs(seq_lengths, seq_devices, device)
    moe_in, residual, share, query, keyvalue, probs, small = attention_call(
        place, block_input, *others, dense
    )
    rows, cots = gather_whole(moe_in, count), gather_whole(packed, count)
    calls = [
        expert_call(0, small, tables, names, *rows[i : i + 8], *cots[i : i + 8])
        for i in range(0, len(rows), 8)
    ]
    back_pieces = sum_whole([b for call in calls for b in call[1]], count)
    outs = [call[0][j][ROWS * h : ROWS * (h + 1)] for call in calls for h in range(2) for j in range(4)]
    out_pieces = sum_whole(outs, count)
    received = [weight_grad_call(i, [call[3] for call in calls]) for i in range(3)]
    received = [permute(r, swap_perm(1, count)) for r in received]
    expert_grads = [weight_grad_call(i, [call[2] for call in calls], received[i]) for i in range(3)]
    residual_grad, grads = head_backward_call(
        place, (dense,), back_pieces,
        (moe_in, residual, packed, small, share, query, keyvalue, probs, *others[:2]),
    )
    terms = jnp.stack(dense_grad_call(BLOCKS, place, share, grads)).astype(F32)
    wholes = [terms[:, PART * i : PART * (i + 1)].reshape(MODEL, MODEL) for i in range(3)]
    wholes.append(small_columns(terms[:, 3 * PART :]).reshape(MODEL, 128))
    query_grad, keyvalue_grad, output_weight_grad, small_grad = [
        lax.psum_scatter(w, "fsdp", scatter_dimension=0, tiled=True) for w in wholes
    ]
    input_grad = input_grad_call(place, sequences, (dense,), grads, residual_grad, small, block_input)
    block_output, attn_gain_grad = finish(
        live_rows, residual, out_pieces, attn_gain, (query_weight, keyvalue_weight),
        (query_grad, keyvalue_grad),
    )
    return (
        block_output,
        input_grad,
        attn_gain_grad,
        query_grad,
        keyvalue_grad,
        output_weight_grad,
        small_grad[:, EXPERT_COUNT + 1],
        small_grad[:, :EXPERT_COUNT],
        *expert_grads,
    )


def body(*inputs):
    device = lax.axis_index("fsdp").astype(jnp.int32)
    count = lax.axis_size("fsdp")
    return body_on_slice(device, inputs) if count == 32 else body_elsewhere(device, count, inputs)


def solution(mesh):
    placed = (
        P("fsdp", None),
        P(),
        P(),
        P("fsdp", None),
        P("fsdp"),
        P("fsdp", None),
        P("fsdp", None),
        P("fsdp", None),
        P("fsdp"),
        P("fsdp", None),
        P("fsdp", None),
        P("fsdp", None),
        P("fsdp", None),
        P("fsdp", None),
    )
    return jax.shard_map(
        body,
        mesh=mesh,
        in_specs=placed,
        out_specs=(
            P("fsdp", None),
            P("fsdp", None),
            P("fsdp"),
            P("fsdp", None),
            P("fsdp", None),
            P("fsdp", None),
            P("fsdp"),
            P("fsdp", None),
            P("fsdp", None),
            P("fsdp", None),
            P("fsdp", None),
        ),
        check_vma=False,
    )
```

```python
from functools import partial

import jax
import jax.numpy as jnp
from jax import lax
from jax.experimental import pallas as pl
from jax.experimental.pallas import tpu as pltpu
from jax.sharding import PartitionSpec as P

QUERY_HEADS = 16
KEY_VALUE_HEADS = 8
HEAD_WIDTH = 64
EXPERT_COUNT = 32
EXPERT_HIDDEN = 512
TOPK = 8
CAP = 40

EPS = 1e-06
ROPE_BASE = 10000.0

MODEL = 1024
ROWS = 128
PART = 32
EXTRA = 16
PACK = 3 * PART + EXTRA
BLOCKS = MODEL // PART
WIDE = ROWS + EXTRA
NOT_CHOSEN = 64
VMEM_LIMIT = 62 * 1024 * 1024
SMALL = 48

BF = jnp.bfloat16
F32 = jnp.float32


def dot(a, b, a_dim, b_dim):
    return lax.dot_general(a, b, (((a_dim,), (b_dim,)), ((), ())), preferred_element_type=F32)


def row_by_col(a, b):
    return dot(a, b, 1, 0)


def row_by_row(a, b):
    return dot(a, b, 1, 1)


def col_by_col(a, b):
    return dot(a, b, 0, 0)


GATES = {
    "experts far": ("m.across1", "m.first1", "m.second1", "m.second0", "m.across0",),
    "experts near": ("experts far",),
    "g.c2": ("experts near",),
    "g.c3": ("experts near",),
    "g.f1": ("g.a2",),
    "g.d1": ("g.a2",),
    "g.b1": ("g.a2",),
    "g.b0": ("g.c2", "g.c3",),
    "g.z3": ("g.f1", "g.d1", "g.b1",),
    "g.z2": ("g.a0",),
    "sibling grads": ("g.z3",),
    "received grads": ("g.z2", "g.c0", "g.z1", "g.b0",),
    "s.b1": ("s.a2",),
    "s.b0": ("s.c2",),
    "s.z3": ("s.f1", "s.d1", "s.b1",),
    "s.z2": ("s.a0", "received grads",),
    "s.c2": ("s.d1", "s.f1",),
    "input grad": ("s.z3",),
    "table grads": ("s.z3",),
    "s.z1": ("s.z3",),
}


def layout(seq_lengths, seq_devices, device, count_of_rows):
    on_device = seq_devices == device
    lengths = jnp.where(on_device, seq_lengths, 0)
    starts = jnp.cumsum(lengths) - lengths
    filled_rows = jnp.sum(lengths)
    row_slots = jnp.arange(count_of_rows, dtype=jnp.int32)
    inside = (row_slots[:, None] >= starts[None, :]) & (
        row_slots[:, None] < (starts + lengths)[None, :]
    )
    live_rows = jnp.any(inside, axis=1)
    seq_count = seq_lengths.shape[0]
    numbers = jnp.arange(seq_count, dtype=jnp.int32)
    segment = jnp.where(
        live_rows, jnp.sum(jnp.where(inside, numbers[None, :], 0), axis=1), seq_count
    )
    begins = jnp.where(
        live_rows, jnp.sum(jnp.where(inside, starts[None, :], 0), axis=1), filled_rows
    )
    return (live_rows, segment, row_slots - begins)


def rope_tables(position):
    half = HEAD_WIDTH // 2
    lanes = jnp.arange(2 * HEAD_WIDTH, dtype=jnp.int32)
    exponent = (lanes % half).astype(F32) * 2.0 / HEAD_WIDTH
    angles = position.astype(F32)[:, None] * (ROPE_BASE ** (-exponent))[None, :]
    sign = jnp.where(lanes % HEAD_WIDTH < half, -1.0, 1.0)
    return jnp.cos(angles), jnp.sin(angles) * sign[None, :]


def permute(value, perm):
    return lax.ppermute(value, "fsdp", perm)


def swap_perm(mask, count=32):
    return [(i, i ^ mask) for i in range(count)]


def first_perm():
    return [(i, i ^ (4 if i % 2 == 0 else 2)) for i in range(32)]


def second_perm():
    return [(i, i ^ (2 if i % 2 == 0 else 4)) for i in range(32)]


def parity_groups(count):
    return [list(range(0, count, 2)), list(range(1, count, 2))]


def peer_plan(device, count):
    if count != 32:
        return [device % 2 + 2 * i for i in range(count // 2)]
    core = device % 2
    first = jnp.where(core == 0, 4, 2)
    second = 6 - first
    return [device ^ (8 * z) ^ step for z in range(4) for step in (0, first, second, 6)]


def behind(value, *others):
    return lax.optimization_barrier((value,) + others)[0] if others else value


STEPS = {
    "z1": ("", swap_perm(8)),
    "z2": ("", swap_perm(16)),
    "z3": ("z2", swap_perm(8)),
    "first0": ("", first_perm()),
    "second0": ("", second_perm()),
    "across0": ("first0", second_perm()),
    "first1": ("first0", swap_perm(8)),
    "second1": ("z1", second_perm()),
    "across1": ("across0", swap_perm(8)),
    "first2": ("z2", first_perm()),
    "second2": ("z2", second_perm()),
    "across2": ("first2", second_perm()),
    "first3": ("z3", first_perm()),
    "second3": ("z3", second_perm()),
    "across3": ("first3", second_perm()),
}
class Graph:
    def __init__(self, gates):
        self.gates, self.steps, self.have = gates, {}, {}

    def put(self, name, function, *needs):
        self.steps[name] = (function, needs)

    def get(self, name):
        if name not in self.have:
            self.have[name] = None
            function, needs = self.steps[name]
            values = [self.get(n) for n in needs]
            gates = [jax.tree.leaves(self.get(g))[0] for g in self.gates.get(name, ())]
            if gates and values:
                values[0] = jax.tree.map(lambda v: behind(v, *gates), values[0])
            with jax.named_scope(name.replace(" ", "_")):
                self.have[name] = function(*values)
        return self.have[name]


def put_permute(graph, name, perm, source, make=None):
    graph.put(name, lambda *v: permute(make(*v) if make else v[0], perm), *([source] if isinstance(source, str) else source))


def put_gather(graph, tag, source):
    for step, (base, perm) in STEPS.items():
        put_permute(graph, tag + step, perm, tag + base if base else source)


def gathered(tag, source):
    names = [[base, f"{tag}first{p}", f"{tag}second{p}", f"{tag}across{p}"] for p, base in enumerate((source, tag + "z1", tag + "z2", tag + "z3"))]
    return [n for plane in names for n in plane]


def put_sum(graph, tag, terms):
    own, one, two, three = [terms[4 * p : 4 * (p + 1)] for p in range(4)]
    for p, plane in ((2, two), (3, three)):
        put_permute(graph, f"{tag}a{p}", second_perm(), plane[3])
        put_permute(graph, f"{tag}b{p}", second_perm(), plane[2])
        put_permute(graph, f"{tag}c{p}", first_perm(), (plane[1], f"{tag}a{p}"), add_round)
    put_permute(graph, f"{tag}z3", swap_perm(8), (three[0], f"{tag}b3", f"{tag}c3"), add_round)
    put_permute(graph, f"{tag}z2", swap_perm(16), (two[0], f"{tag}b2", f"{tag}c2", f"{tag}z3"), add_round)
    put_permute(graph, f"{tag}b1", second_perm(), one[2])
    put_permute(graph, f"{tag}f1", swap_perm(8), one[1])
    put_permute(graph, f"{tag}d1", swap_perm(8), one[3])
    put_permute(graph, f"{tag}z1", swap_perm(8), (one[0], f"{tag}b1"), add_round)
    put_permute(graph, f"{tag}a0", second_perm(), (own[3], f"{tag}d1"), add_round)
    put_permute(graph, f"{tag}b0", second_perm(), own[2])
    put_permute(graph, f"{tag}c0", first_perm(), (own[1], f"{tag}f1", f"{tag}a0"), add_round)
    return [own[0]] + [f"{tag}{n}" for n in ("c0", "b0", "z1", "z2")]


def gather_whole(shard, count):
    whole = lax.all_gather(shard, "fsdp", axis=0, axis_index_groups=parity_groups(count))
    return [whole[i] for i in range(count // 2)]


def add_wide(*terms):
    return sum(t.astype(F32) for t in terms)


def add_round(*terms):
    return add_wide(*terms).astype(BF)


def sum_whole(terms, count):
    stacked = jnp.concatenate([t.astype(F32) for t in terms], axis=0)
    return [
        lax.psum_scatter(
            stacked, "fsdp", scatter_dimension=0, tiled=True, axis_index_groups=parity_groups(count)
        )
    ]


def filled_rows(device, lengths, devices):
    return lax.fori_loop(
        0,
        lengths.shape[0],
        lambda i, rows: rows + jnp.where(devices[i] == device[0], lengths[i], 0),
        jnp.int32(0),
    )


def pack_kernel(with_weights, device, lengths, devices, ids, out_grad, *refs):
    cot = refs[-1]
    if with_weights:
        query, keyvalue, output, router, attn_gain, moe_gain, packed = refs[:-1]
        square = jnp.zeros((128, 128), F32)
        row = lax.broadcasted_iota(jnp.int32, (128, 128), 0)
        for i, gain in enumerate((attn_gain, moe_gain)):
            wide = jnp.concatenate(
                [gain[...].astype(F32).reshape(1, PART), jnp.zeros((1, 128 - PART), F32)], axis=1
            )
            square = jnp.where(row == EXPERT_COUNT + i, wide, square)
        small = square.T[:PART]
        small = small + jnp.concatenate(
            [router[...].astype(F32), jnp.zeros((PART, 128 - EXPERT_COUNT), F32)], axis=1
        )
        small = small.astype(BF)
        packed[0:PART, :] = query[...]
        packed[PART : 2 * PART, :] = keyvalue[...]
        packed[2 * PART : 3 * PART, :] = output[...]
        packed[3 * PART : PACK, :] = jnp.zeros((EXTRA, MODEL), BF)
        packed[3 * PART : PACK, 0:128] = small[0:EXTRA, :]
        packed[3 * PART : PACK, 128:256] = small[EXTRA:, :]
    filled = filled_rows(device, lengths, devices)
    rows = lax.broadcasted_iota(jnp.int32, (ROWS, MODEL), 0)
    cot[EXTRA:, :] = jnp.where(
        rows < filled, out_grad[...].astype(F32), 0.0
    ).astype(BF)
    wide = ids[...].astype(F32)
    expert = lax.broadcasted_iota(jnp.int32, (EXPERT_COUNT, ROWS), 0).astype(F32)
    hit = jnp.zeros((EXPERT_COUNT, ROWS), F32)
    for k in range(TOPK):
        hit = hit + jnp.where(expert == wide[k : k + 1, :], 1.0, 0.0)
    row = lax.broadcasted_iota(jnp.int32, (ROWS, ROWS), 0)
    column = lax.broadcasted_iota(jnp.int32, (ROWS, ROWS), 1)
    before = jnp.where(row < column, 1.0, 0.0).astype(BF)
    rank = row_by_col(hit.astype(BF), before)
    table = jnp.where(hit > 0.0, rank, float(NOT_CHOSEN)).astype(BF)
    cot[:EXTRA, :] = jnp.zeros((EXTRA, MODEL), BF)
    cot[:EXTRA, 256:384] = table[:EXTRA]
    cot[:EXTRA, 384:512] = table[EXTRA:]


def join_kernel(rows, *refs):
    parts, out, sems = refs[:-2], refs[-2], refs[-1]
    copies = [
        pltpu.make_async_copy(part.at[pl.ds(0, rows)], out.at[pl.ds(rows * i, rows)], sems.at[i])
        for i, part in enumerate(parts)
    ]
    for copy in copies:
        copy.start()
    for copy in copies:
        copy.wait()


def start_weights(place, buffers, weights, sems, first, last):
    copies = []
    for buffer in buffers:
        for j in range(buffer.shape[0] // PACK):
            i = len(copies)
            copies.append(
                pltpu.make_async_copy(
                    buffer.at[pl.ds(j * PACK + first, last - first)], weights.at[place[i]], sems.at[i]
                )
            )
            copies[-1].start()
    return copies


def half_swap(chunk):
    lane = lax.broadcasted_iota(jnp.int32, chunk.shape, 1)
    half = HEAD_WIDTH // 2
    return jnp.where(
        lane % HEAD_WIDTH < half, pltpu.roll(chunk, 128 - half, 1), pltpu.roll(chunk, half, 1)
    )


def doubled(chunk, second):
    lane = lax.broadcasted_iota(jnp.int32, chunk.shape, 1)
    turned = pltpu.roll(chunk, HEAD_WIDTH, 1)
    keep = lane >= HEAD_WIDTH if second else lane < HEAD_WIDTH
    return jnp.where(keep, chunk, turned)


def split_pair(chunk):
    lane = lax.broadcasted_iota(jnp.int32, chunk.shape, 1)
    zero = jnp.zeros_like(chunk)
    return jnp.concatenate(
        [jnp.where(lane < HEAD_WIDTH, chunk, zero), jnp.where(lane < HEAD_WIDTH, zero, chunk)], axis=0
    )


def join_pair(stacked):
    lane = lax.broadcasted_iota(jnp.int32, (ROWS, 128), 1)
    return jnp.where(lane < HEAD_WIDTH, stacked[:ROWS], stacked[ROWS:])


def attention_kernel(buffers_count, *refs):
    place, buffers, refs = refs[0], refs[1 : 1 + buffers_count], refs[1 + buffers_count :]
    x_ref, cos_ref, sin_ref, allowed_ref = refs[:4]
    moe_ref, resid_ref, share_ref, query_ref, kv_ref, probs_ref, small_ref = refs[4:11]
    weights, columns, sems = refs[11:]
    copies = start_weights(place, buffers, weights, sems, 0, PACK)
    x = x_ref[...].astype(F32)
    unit = x * lax.rsqrt(jnp.mean(x * x, axis=-1, keepdims=True) + EPS)
    for copy in copies:
        copy.wait()
    for p in range(BLOCKS):
        for j in range(2):
            columns[pl.ds(p * PART + j * EXTRA, EXTRA), :] = weights[
                p, 3 * PART :, 128 * j : 128 * (j + 1)
            ].astype(F32)
    small = columns[...].T
    small_ref[...] = small.astype(BF)
    attn_in = (unit * small[EXPERT_COUNT : EXPERT_COUNT + 1, :]).astype(BF)
    share_ref[:ROWS, :] = attn_in
    cosine, sine = cos_ref[...], sin_ref[...]

    def weight_columns(which, chunk):
        lanes = slice(256 * chunk, 256 * (chunk + 1))
        return weights[:, PART * which : PART * (which + 1), lanes].reshape(MODEL, 256)

    for chunk in range(4):
        query_pre = row_by_col(attn_in, weight_columns(0, chunk))
        kv_pre = row_by_col(attn_in, weight_columns(1, chunk))
        for j in range(2):
            at = slice(256 * chunk + 128 * j, 256 * chunk + 128 * (j + 1))
            part = query_pre[:, 128 * j : 128 * (j + 1)]
            query_ref[:, at] = (part * cosine + half_swap(part) * sine).astype(BF)
            part = kv_pre[:, 128 * j : 128 * (j + 1)]
            if chunk < 2:
                part = part * cosine + half_swap(part) * sine
            kv_ref[:, at] = part.astype(BF)
    allowed = jnp.concatenate([allowed_ref[...], allowed_ref[...]], axis=0) > 0.0
    scale = HEAD_WIDTH ** (-0.5)
    for head in range(KEY_VALUE_HEADS):
        pair, second = head // 2, head % 2 == 1
        key = doubled(kv_ref[:, 128 * pair : 128 * (pair + 1)].astype(F32), second).astype(BF)
        value = doubled(
            kv_ref[:, 512 + 128 * pair : 512 + 128 * (pair + 1)].astype(F32), second
        ).astype(BF)
        at = slice(128 * head, 128 * (head + 1))
        scores = row_by_row(split_pair(query_ref[:, at]), key) * scale
        scores = jnp.where(allowed, scores, -jnp.inf)
        raised = jnp.exp(scores - jnp.max(scores, axis=-1, keepdims=True))
        probs = raised / jnp.sum(raised, axis=-1, keepdims=True)
        probs_ref[head] = probs
        share_ref[ROWS:, at] = join_pair(row_by_col(probs.astype(BF), value)).astype(BF)
    heads = share_ref[ROWS:, :]
    for chunk in range(4):
        at = slice(256 * chunk, 256 * (chunk + 1))
        resid_ref[:, at] = x_ref[:, at].astype(F32) + row_by_col(heads, weight_columns(2, chunk))
    residual = resid_ref[...]
    unit = residual * lax.rsqrt(jnp.mean(residual * residual, axis=-1, keepdims=True) + EPS)
    moe_ref[...] = (unit * small[EXPERT_COUNT + 1 : EXPERT_COUNT + 2, :]).astype(BF)


def route_table(extra):
    return jnp.concatenate([extra[:, 0:128], extra[:, 128:256]], axis=0).astype(F32)


def route_weights_of(table, small, rows):
    logits = row_by_row(small, rows)[:EXPERT_COUNT]
    raised = jnp.where(table < NOT_CHOSEN, jnp.exp(logits), 0.0)
    return raised / jnp.sum(raised, axis=0, keepdims=True)


def expert_kernel(sizes, *refs):
    x_sizes, c_first = sizes
    names, refs = refs[0], refs[1:]
    x_hbm, refs = refs[: len(x_sizes)], refs[len(x_sizes) :]
    peers, gathered, refs = refs[0], refs[1], refs[2:]
    small_ref, tables_hbm, refs = refs[0], refs[1:7], refs[7:]
    p_hbm, g_hbm, saved_hbm, refs = refs[:4], refs[4:12], refs[12:22], refs[22:]
    xs_all, cs_all, tables, ps, gs, saved_wide, saved_thin, picks, cots, results, back, in_sems, out_sems = refs
    copies = []

    def fetch(source, target):
        copies.append(pltpu.make_async_copy(source, target, in_sems.at[len(copies)]))
        copies[-1].start()

    def send(source, target, number):
        copy = pltpu.make_async_copy(source, target, out_sems.at[number])
        copy.start()
        return copy

    at = 0
    for ref, size in zip(x_hbm, x_sizes):
        for j in range(size):
            fetch(ref.at[pl.ds(ROWS * j, ROWS)], xs_all.at[at])
            at += 1
    for i in range(8):
        fetch(gathered.at[peers[c_first + i]], cs_all.at[i])
    for i, ref in enumerate(tables_hbm):
        fetch(ref, tables.at[i])
    slots = 4 * CAP
    small = small_ref[...]
    expert_row = lax.broadcasted_iota(jnp.int32, (EXPERT_COUNT, ROWS), 0)
    slot_row = lax.broadcasted_iota(jnp.int32, (slots, 4 * ROWS), 0).astype(F32)
    slot_weights = [[None, None], [None, None]]
    for copy in copies[:16]:
        copy.wait()
    for h in range(2):
        places, weights = [[], []], [[], []]
        for b in range(4):
            table = route_table(cs_all[4 * h + b, :EXTRA, 256:512])
            weight = route_weights_of(table, small, xs_all[4 * h + b])
            for l in range(2):
                here = expert_row == names[l]
                place = jnp.sum(jnp.where(here, table, 0.0), axis=0, keepdims=True)
                places[l].append(jnp.where(place < NOT_CHOSEN, place + b * CAP, 4096.0))
                weights[l].append(jnp.sum(jnp.where(here, weight, 0.0), axis=0, keepdims=True))
        for l in range(2):
            chosen = slot_row == jnp.concatenate(places[l], axis=1)
            weight = jnp.concatenate(weights[l], axis=1)
            slot_weights[l][h] = jnp.sum(jnp.where(chosen, weight, 0.0), axis=1, keepdims=True)
            picks[h, slots * l : slots * (l + 1), :] = chosen.astype(F32).astype(BF)
        pick = picks[h]
        rows = xs_all[4 * h : 4 * (h + 1)].reshape(4 * ROWS, MODEL)
        cot_rows = cs_all[4 * h : 4 * (h + 1), EXTRA:, :].reshape(4 * ROWS, MODEL)
        inputs = row_by_col(pick, rows).astype(BF)
        cot = row_by_col(pick, cot_rows).astype(BF)
        for l in range(2):
            saved_wide[2 * l, slots * h : slots * (h + 1), :] = inputs[slots * l : slots * (l + 1)]
            cots[l, slots * h : slots * (h + 1), :] = cot[slots * l : slots * (l + 1)]
    slot_routes, sends = [], []
    for l in range(2):
        gate, up, down = tables.at[3 * l], tables.at[3 * l + 1], tables.at[3 * l + 2]
        for copy in copies[16 + 3 * l : 19 + 3 * l]:
            copy.wait()
        weight = jnp.concatenate(slot_weights[l], axis=0)
        inputs = saved_wide[2 * l]
        gate_pre = row_by_row(inputs, gate[...])
        up_pre = row_by_row(inputs, up[...])
        sigma = jax.nn.sigmoid(gate_pre)
        acts = (gate_pre * sigma * up_pre).astype(BF)
        saved_thin[3 * l] = acts
        cot = cots[l].astype(F32)
        result = row_by_col(acts, down[...])
        slot_routes.append(jnp.sum(cot * result, axis=1, keepdims=True))
        results[l] = (weight * result).astype(BF)
        pair_cot = (weight * cot).astype(BF)
        saved_wide[2 * l + 1] = pair_cot
        act_grad = row_by_row(pair_cot, down[...])
        gate_grad = (act_grad * up_pre * sigma * (1.0 + gate_pre * (1.0 - sigma))).astype(BF)
        up_grad = (act_grad * gate_pre * sigma).astype(BF)
        saved_thin[3 * l + 1] = gate_grad
        saved_thin[3 * l + 2] = up_grad
        back[l] = (row_by_col(gate_grad, gate[...]) + row_by_col(up_grad, up[...])).astype(BF)
        for i in range(5):
            source = saved_wide.at[2 * l + i] if i < 2 else saved_thin.at[3 * l + i - 2]
            sends.append(send(source, saved_hbm[5 * l + i], 16 + 5 * l + i))
    for h in range(2):
        pick = picks[h]
        at = slice(slots * h, slots * (h + 1))
        grad = col_by_col(pick, jnp.concatenate([back[0, at], back[1, at]], axis=0)).astype(BF)
        routes = []
        for l in range(2):
            chosen = pick[slots * l : slots * (l + 1)].astype(F32)
            routes.append(jnp.sum(chosen * slot_routes[l][at], axis=0, keepdims=True))
        for b in range(4):
            i = 4 * h + b
            rows = slice(ROWS * b, ROWS * (b + 1))
            gs[i, :ROWS, :] = grad[rows]
            route = jnp.zeros((EXPERT_COUNT, ROWS), F32)
            for l in range(2):
                route = route + jnp.where(expert_row == names[l], routes[l][:, rows], 0.0)
            high = route.astype(BF)
            low = (route - high.astype(F32)).astype(BF)
            gs[i, ROWS:, 0:128] = high[:16]
            gs[i, ROWS:, 128:256] = high[16:]
            gs[i, ROWS:, 256:384] = low[:16]
            gs[i, ROWS:, 384:512] = low[16:]
            gs[i, ROWS:, 512:] = jnp.zeros((EXTRA, MODEL - 512), BF)
            sends.append(send(gs.at[i], g_hbm[i], 8 + i))
        out = col_by_col(pick, jnp.concatenate([results[0, at], results[1, at]], axis=0)).astype(BF)
        for b in range(4):
            i = 4 * h + b
            ps[i] = out[ROWS * b : ROWS * (b + 1)]
            sends.append(send(ps.at[i], p_hbm[i % 4].at[pl.ds(ROWS * (i // 4), ROWS)], i))
    for copy in sends:
        copy.wait()


def weight_grad_kernel(calls, added, *refs):
    saved, refs = refs[: 5 * calls], refs[5 * calls :]
    received, refs = refs[:added], refs[added:]
    outs, refs = refs[: 3 if added else 1], refs[3 if added else 1 :]
    wide, thin, extra, sums, in_sems, out_sems = refs
    hidden = thin.shape[2]
    copies = {}

    def fetch(name, source, target):
        copies[name] = pltpu.make_async_copy(source, target, in_sems.at[len(copies)])
        copies[name].start()

    order = ((3, 0), (4, 0), (2, 1))
    for o, pair in enumerate(order):
        for c in range(calls):
            for i in pair:
                if (c, i) not in copies:
                    target = wide.at[2 * c + i] if i < 2 else thin.at[3 * c + i - 2]
                    fetch((c, i), saved[5 * c + i], target)
        if added:
            fetch(o, received[0].at[pl.ds(hidden * o, hidden)], extra.at[o])
    waited, sends = set(), []
    for o, (left, right) in enumerate(order):
        total = None
        for c in range(calls):
            for i in (left, right):
                if (c, i) not in waited:
                    waited.add((c, i))
                    copies[c, i].wait()
            term = col_by_col(thin[3 * c + left - 2], wide[2 * c + right])
            total = term if total is None else total + term
        if added:
            copies[o].wait()
            total = total + extra[o]
        sums[o] = total
        target = outs[o] if added else outs[0].at[pl.ds(hidden * o, hidden)]
        sends.append(pltpu.make_async_copy(sums.at[o], target, out_sems.at[o]))
        sends[-1].start()
    for copy in sends:
        copy.wait()


def head_backward_kernel(buffers_count, pieces_count, *refs):
    place, buffers, refs = refs[0], refs[1 : 1 + buffers_count], refs[1 + buffers_count :]
    pieces, refs = refs[:pieces_count], refs[pieces_count:]
    moe_ref, resid_ref, cot_ref, small_ref, share_ref, query_ref, kv_ref, probs_ref = refs[:8]
    cos_ref, sin_ref = refs[8:10]
    resid_grad_ref, grads_ref = refs[10:12]
    weights, grads, sems = refs[12:]
    copies = start_weights(place, buffers, weights, sems, 2 * PART, 3 * PART)
    small = small_ref[...]
    total = pieces[0][...].astype(F32)
    for piece in pieces[1:]:
        total = total + piece[...].astype(F32)
    extra = total[ROWS:]
    route_grad = jnp.concatenate(
        [extra[:, 0:128] + extra[:, 256:384], extra[:, 128:256] + extra[:, 384:512]], axis=0
    )
    moe_in = moe_ref[...]
    first = cot_ref.shape[0] - WIDE
    table = route_table(cot_ref[first : first + EXTRA, 256:512])
    weight = route_weights_of(table, small, moe_in)
    logit_grad = weight * (route_grad - jnp.sum(weight * route_grad, axis=0, keepdims=True))
    logit_grad = jnp.concatenate(
        [logit_grad, jnp.zeros((ROWS - EXPERT_COUNT, ROWS), F32)], axis=0
    ).astype(BF)
    moe_in_grad = total[:ROWS] + col_by_col(logit_grad, small)
    router_grad = row_by_col(logit_grad, moe_in)[:SMALL]
    residual = resid_ref[...]
    inverse = lax.rsqrt(jnp.mean(residual * residual, axis=-1, keepdims=True) + EPS)
    unit = residual * inverse
    moe_gain_grad = jnp.sum(moe_in_grad * unit, axis=0, keepdims=True)
    row = lax.broadcasted_iota(jnp.int32, (SMALL, MODEL), 0)
    grads_ref[3 * ROWS :, :] = jnp.where(row == EXPERT_COUNT + 1, moe_gain_grad, router_grad).astype(BF)
    grad_unit = moe_in_grad * small[EXPERT_COUNT : EXPERT_COUNT + 8].astype(F32)[1:2]
    mean = jnp.mean(grad_unit * unit, axis=-1, keepdims=True)
    cot = cot_ref[first + EXTRA :, :]
    residual_grad = cot.astype(F32) + inverse * (grad_unit - unit * mean)
    resid_grad_ref[...] = residual_grad
    residual_bf = residual_grad.astype(BF)
    grads_ref[:ROWS, :] = residual_bf
    for copy in copies:
        copy.wait()
    for chunk in range(4):
        at = slice(256 * chunk, 256 * (chunk + 1))
        rows = weights[8 * chunk : 8 * (chunk + 1)].reshape(256, MODEL)
        grads[:, at] = row_by_row(residual_bf, rows).astype(BF)
    cosine, sine = cos_ref[...], sin_ref[...]
    scale = HEAD_WIDTH ** (-0.5)
    key_grads, value_grads = [], []
    for head in range(KEY_VALUE_HEADS):
        pair, second = head // 2, head % 2 == 1
        key = doubled(kv_ref[:, 128 * pair : 128 * (pair + 1)].astype(F32), second).astype(BF)
        value = doubled(
            kv_ref[:, 512 + 128 * pair : 512 + 128 * (pair + 1)].astype(F32), second
        ).astype(BF)
        at = slice(128 * head, 128 * (head + 1))
        query = split_pair(query_ref[:, at])
        head_grad = split_pair(grads[:, at])
        mixed = split_pair(share_ref[ROWS:, at])
        inner = jnp.sum(head_grad.astype(F32) * mixed.astype(F32), axis=-1, keepdims=True)
        probs = probs_ref[head]
        score_grad = (probs * (row_by_row(head_grad, value) - inner)).astype(BF)
        part = join_pair(row_by_col(score_grad, key)) * scale
        grads_ref[ROWS : 2 * ROWS, at] = (part * cosine - half_swap(part) * sine).astype(BF)
        part = col_by_col(score_grad, query) * scale
        key_grads.append(part + pltpu.roll(part, HEAD_WIDTH, 1))
        part = col_by_col(probs.astype(BF), head_grad)
        value_grads.append(part + pltpu.roll(part, HEAD_WIDTH, 1))
    lane = lax.broadcasted_iota(jnp.int32, (ROWS, 128), 1)
    for which, parts in enumerate((key_grads, value_grads)):
        for pair in range(KEY_VALUE_HEADS // 2):
            part = jnp.where(lane < HEAD_WIDTH, parts[2 * pair], parts[2 * pair + 1])
            if which == 0:
                part = part * cosine - half_swap(part) * sine
            at = slice(512 * which + 128 * pair, 512 * which + 128 * (pair + 1))
            grads_ref[2 * ROWS : 3 * ROWS, at] = part.astype(BF)


def input_grad_kernel(buffers_count, place, device, lengths, devices, *refs):
    buffers, refs = refs[:buffers_count], refs[buffers_count:]
    grads_ref, resid_grad_ref, small_ref, x_ref, in_ref = refs[:5]
    weights, sems = refs[5:]
    copies = start_weights(place, buffers, weights, sems, 0, 2 * PART)
    x = x_ref[...].astype(F32)
    inverse = lax.rsqrt(jnp.mean(x * x, axis=-1, keepdims=True) + EPS)
    unit = x * inverse
    query_grad, kv_grad = grads_ref[ROWS : 2 * ROWS, :], grads_ref[2 * ROWS : 3 * ROWS, :]
    for copy in copies:
        copy.wait()
    back = []
    for chunk in range(4):
        rows = weights[8 * chunk : 8 * (chunk + 1)]
        back.append(
            row_by_row(query_grad, rows[:, :PART].reshape(256, MODEL))
            + row_by_row(kv_grad, rows[:, PART:].reshape(256, MODEL))
        )
    attn_in_grad = jnp.concatenate(back, axis=1)
    grad_unit = attn_in_grad * small_ref[EXPERT_COUNT : EXPERT_COUNT + 8].astype(F32)[0:1]
    mean = jnp.mean(grad_unit * unit, axis=-1, keepdims=True)
    input_grad = resid_grad_ref[...] + inverse * (grad_unit - unit * mean)
    rows = lax.broadcasted_iota(jnp.int32, (ROWS, MODEL), 0)
    in_ref[...] = jnp.where(rows < filled_rows(device, lengths, devices), input_grad, 0.0)


def dense_grad_kernel(parties, blocks, *refs):
    place, refs = refs[0], refs[1:]
    results = refs[2 * parties : -blocks - 2]
    refs = refs[: 2 * parties] + refs[-blocks - 2 :]
    sems = refs[-1]
    shares, grads, refs = refs[:parties], refs[parties : 2 * parties], refs[2 * parties :]
    outs, terms = refs[:blocks], refs[blocks]
    copies = []
    for i in range(4 * len(results) // 2 if results else 0):
        source = results[4 * (i // 8) + i % 4].at[pl.ds(ROWS * (i // 4 % 2), ROWS)]
        copies.append(pltpu.make_async_copy(source, outs[i].at[pl.ds(PACK, ROWS)], sems.at[i]))
        copies[-1].start()
    attn_in = jnp.concatenate([r[:ROWS, :] for r in shares], axis=0)
    heads = jnp.concatenate([r[ROWS:, :] for r in shares], axis=0)
    residual, query, keyvalue = [
        jnp.concatenate([r[ROWS * i : ROWS * (i + 1), :] for r in grads], axis=0) for i in range(3)
    ]
    for chunk in range(4):
        at = slice(256 * chunk, 256 * (chunk + 1))
        for which, left, right in ((0, attn_in, query), (1, attn_in, keyvalue), (2, heads, residual)):
            term = col_by_col(left[:, at], right).astype(BF).reshape(8, PART, MODEL)
            terms[8 * chunk : 8 * (chunk + 1), PART * which : PART * (which + 1), :] = term
    columns = sum(r[3 * ROWS :, :].astype(F32) for r in grads)
    columns = jnp.concatenate([columns, jnp.zeros((128 - SMALL, MODEL), F32)], axis=0).T.astype(BF)
    for p in range(BLOCKS):
        for j in range(2):
            terms[p, 3 * PART :, 128 * j : 128 * (j + 1)] = columns[
                p * PART + j * EXTRA : p * PART + (j + 1) * EXTRA
            ]
        terms[p, 3 * PART :, 256:] = jnp.zeros((EXTRA, MODEL - 256), BF)
    for i in range(blocks):
        outs[i][:PACK, :] = terms[place[i]]
    for copy in copies:
        copy.wait()


def params():
    return pltpu.CompilerParams(vmem_limit_bytes=VMEM_LIMIT)


def shape(dims, dtype):
    return jax.ShapeDtypeStruct(dims, dtype)


def spec(space):
    return pl.BlockSpec(memory_space=space)


def pack_call(sequences, expert_ids, output_grad, *weights):
    smem, vmem = spec(pltpu.SMEM), spec(pltpu.VMEM)
    return pl.pallas_call(
        partial(pack_kernel, bool(weights)),
        out_shape=((shape((PACK, MODEL), BF),) if weights else ()) + (shape((WIDE, MODEL), BF),),
        in_specs=[smem] * 3 + [vmem] * (2 + len(weights)),
        out_specs=(vmem,) * (2 if weights else 1),
        compiler_params=params(),
    )(*sequences, expert_ids.T, output_grad, *weights)


def join_call(rows, *parts):
    anywhere = spec(pl.ANY)
    return pl.pallas_call(
        partial(join_kernel, rows),
        out_shape=shape((rows * len(parts), MODEL), BF),
        in_specs=[anywhere] * len(parts),
        out_specs=spec(pltpu.VMEM),
        scratch_shapes=[pltpu.SemaphoreType.DMA((len(parts),))],
        compiler_params=params(),
    )(*parts)


def attention_call(place, block_input, cosine, sine, allowed, *dense):
    vmem = spec(pltpu.VMEM)
    return pl.pallas_call(
        partial(attention_kernel, len(dense)),
        out_shape=(
            shape((ROWS, MODEL), BF),
            shape((ROWS, MODEL), F32),
            shape((2 * ROWS, MODEL), BF),
            shape((ROWS, MODEL), BF),
            shape((ROWS, MODEL), BF),
            shape((KEY_VALUE_HEADS, 2 * ROWS, ROWS), F32),
            shape((128, MODEL), BF),
        ),
        in_specs=[spec(pltpu.SMEM)] + [spec(pl.ANY)] * len(dense) + [vmem] * 4,
        out_specs=(vmem,) * 7,
        scratch_shapes=[
            pltpu.VMEM((BLOCKS, PACK, MODEL), BF),
            pltpu.VMEM((MODEL, 128), F32),
            pltpu.SemaphoreType.DMA((BLOCKS,)),
        ],
        compiler_params=params(),
    )(place, *dense, block_input, cosine, sine, allowed)


def expert_call(first, small, tables, names, peers, gathered, *rows):
    hidden, slots = tables[0].shape[0], 8 * CAP
    anywhere = spec(pl.ANY)
    got = pl.pallas_call(
        partial(expert_kernel, ((1,) * 8, first)),
        out_shape=(shape((2 * ROWS, MODEL), BF),) * 4
        + (shape((WIDE, MODEL), BF),) * 8
        + ((shape((slots, MODEL), BF),) * 2 + (shape((slots, hidden), BF),) * 3) * 2,
        in_specs=[spec(pltpu.SMEM)] + [anywhere] * 8 + [spec(pltpu.SMEM)] + [anywhere] + [spec(pltpu.VMEM)] + [anywhere] * 6,
        out_specs=(anywhere,) * 22,
        scratch_shapes=[
            pltpu.VMEM((8, ROWS, MODEL), BF),
            pltpu.VMEM((8, WIDE, MODEL), BF),
            pltpu.VMEM((6, hidden, MODEL), BF),
            pltpu.VMEM((8, ROWS, MODEL), BF),
            pltpu.VMEM((8, WIDE, MODEL), BF),
            pltpu.VMEM((4, slots, MODEL), BF),
            pltpu.VMEM((6, slots, hidden), BF),
            pltpu.VMEM((2, slots, 4 * ROWS), BF),
            pltpu.VMEM((2, slots, MODEL), BF),
            pltpu.VMEM((2, slots, MODEL), BF),
            pltpu.VMEM((2, slots, MODEL), BF),
            pltpu.SemaphoreType.DMA((22,)),
            pltpu.SemaphoreType.DMA((26,)),
        ],
        compiler_params=params(),
    )(names, *rows, peers, gathered, small, *tables)
    return got[:4], got[4:12], got[12:17], got[17:]


def weight_grad_call(calls, *added):
    saves = [v for saved in calls for v in saved]
    hidden, slots = saves[2].shape[1], saves[2].shape[0]
    table = shape((hidden, MODEL), F32)
    anywhere = spec(pl.ANY)
    number = len(calls)
    return pl.pallas_call(
        partial(weight_grad_kernel, number, len(added)),
        out_shape=(table,) * 3 if added else shape((3 * hidden, MODEL), F32),
        in_specs=[anywhere] * (len(saves) + len(added)),
        out_specs=(anywhere,) * 3 if added else anywhere,
        scratch_shapes=[
            pltpu.VMEM((2 * number, slots, MODEL), BF),
            pltpu.VMEM((3 * number, slots, hidden), BF),
            pltpu.VMEM((3, hidden, MODEL), F32),
            pltpu.VMEM((3, hidden, MODEL), F32),
            pltpu.SemaphoreType.DMA((5 * number + 3,)),
            pltpu.SemaphoreType.DMA((3,)),
        ],
        compiler_params=params(),
    )(*saves, *added)


def head_backward_call(place, dense, pieces, others):
    vmem = spec(pltpu.VMEM)
    return pl.pallas_call(
        partial(head_backward_kernel, len(dense), len(pieces)),
        out_shape=(shape((ROWS, MODEL), F32), shape((3 * ROWS + SMALL, MODEL), BF)),
        in_specs=[spec(pltpu.SMEM)] + [spec(pl.ANY)] * len(dense) + [vmem] * (len(pieces) + 10),
        out_specs=(vmem,) * 2,
        scratch_shapes=[
            pltpu.VMEM((BLOCKS, PART, MODEL), BF),
            pltpu.VMEM((ROWS, MODEL), BF),
            pltpu.SemaphoreType.DMA((BLOCKS,)),
        ],
        compiler_params=params(),
    )(place, *dense, *pieces, *others)


def dense_grad_call(blocks, place, parties, results=()):
    vmem = spec(pltpu.VMEM)
    rows = PACK + ROWS if results else PACK
    return pl.pallas_call(
        partial(dense_grad_kernel, len(parties) // 2, blocks),
        out_shape=(shape((rows, MODEL), BF),) * blocks,
        in_specs=[spec(pltpu.SMEM)] + [vmem] * len(parties) + [spec(pl.ANY)] * len(results),
        out_specs=(vmem,) * blocks,
        scratch_shapes=[
            pltpu.VMEM((BLOCKS, PACK, MODEL), BF),
            pltpu.SemaphoreType.DMA((BLOCKS // 2,)),
        ],
        compiler_params=params(),
    )(place, *parties, *results)


def input_grad_call(place, sequences, dense, *others):
    smem, vmem = spec(pltpu.SMEM), spec(pltpu.VMEM)
    return pl.pallas_call(
        partial(input_grad_kernel, len(dense)),
        out_shape=shape((ROWS, MODEL), F32),
        in_specs=[smem] * 4 + [spec(pl.ANY)] * len(dense) + [vmem] * 4,
        out_specs=vmem,
        scratch_shapes=[
            pltpu.VMEM((BLOCKS, 2 * PART, MODEL), BF),
            pltpu.SemaphoreType.DMA((BLOCKS,)),
        ],
        compiler_params=params(),
    )(place, *sequences, *dense, *others)


def attention_inputs(seq_lengths, seq_devices, device):
    live_rows, segment, position = layout(seq_lengths, seq_devices, device, ROWS)
    row_slots = jnp.arange(ROWS, dtype=jnp.int32)
    allowed = (segment[:, None] == segment[None, :]) & (row_slots[:, None] >= row_slots[None, :])
    return live_rows, (*rope_tables(position), allowed.astype(F32))


def finish(live_rows, residual, out_pieces, gain, weights, grads):
    block_output = jnp.where(live_rows[:, None], add_wide(residual, *out_pieces), 0.0).astype(BF)
    weighted = sum(w.astype(F32) * g for w, g in zip(weights, grads))
    return block_output, jnp.sum(weighted, axis=1) / gain.astype(F32)


def small_columns(rows):
    return jnp.concatenate([rows[..., 0:128], rows[..., 128:256]], axis=-2)


def graph_on_slice(device, inputs):
    (block_input, seq_lengths, seq_devices, expert_ids, attn_gain, query_weight, keyvalue_weight,
     output_weight, moe_gain, router_weight, gate_weight, up_weight, down_weight, output_grad) = inputs
    own_tables = (gate_weight, up_weight, down_weight)
    sequences = (device.reshape(1), seq_lengths, seq_devices)
    names = jnp.stack([device, device ^ 1])
    graph = Graph(GATES)
    put = graph.put

    weights = (query_weight, keyvalue_weight, output_weight, router_weight, attn_gain, moe_gain)
    put("shards", lambda: pack_call(sequences, expert_ids, output_grad, *weights))
    put("packed", lambda v: v[0], "shards")
    put("cot", lambda v: v[1], "shards")
    put("cots", lambda v: lax.all_gather(v, "fsdp", axis=0, axis_index_groups=parity_groups(32)), "cot")
    peers = jnp.stack(peer_plan(device, 32)) // 2
    put_gather(graph, "d.", "packed")
    cots = gathered("d.", "packed")
    for i, table in enumerate(own_tables):
        put(f"tables {i}", lambda table=table: permute(table, swap_perm(1)))
    early = [n for n in cots if n not in ("d.across1", "d.across2", "d.first3", "d.second3", "d.across3")]
    late = ["d.across1", "d.across2", "d.first3", "d.second3"]
    for name, parts in (("early", early), ("late", late)):
        put("joined " + name, partial(join_call, PACK), *parts)
        put_permute(graph, "sibling " + name, swap_perm(1), "joined " + name)
    put_permute(graph, "sibling last", swap_perm(1), "d.across3")
    dense = cots + ["sibling early", "sibling late", "sibling last"]
    order = cots + early + late + ["d.across3"]
    at = {n: i for i, n in enumerate(cots)}
    plan = peer_plan(device, 32), peer_plan(device ^ 1, 32)
    place = jnp.stack([plan[i // 16][at[n]] for i, n in enumerate(order)])

    put("layout", lambda v: attention_inputs(behind(seq_lengths, v), seq_devices, device), "packed")
    put("attention", lambda l, *v: attention_call(place, block_input, *l[1], *v), "layout", *dense)
    for i, name in enumerate(("moe in", "residual", "share", "query", "keyvalue", "probs", "small")):
        put(name, lambda v, i=i: v[i], "attention")
    put_permute(graph, "share sibling", swap_perm(1), "share")

    put_gather(graph, "m.", "moe in")
    rows = gathered("m.", "moe in")
    for name, at in (("near", slice(0, 8)), ("far", slice(8, 16))):
        put(
            "experts " + name,
            lambda small, *v, at=at: expert_call(at.start, small, (*own_tables, *v[:3]), names, peers, *v[3:]),
            "small", "tables 0", "tables 1", "tables 2", "cots", *rows[at],
        )
        for i in range(4):
            put(f"out {name} {i}", lambda v, i=i: v[0][i], "experts " + name)
        for i in range(8):
            put(f"back {name} {i}", lambda v, i=i: v[1][i], "experts " + name)
    put("sibling grads", lambda a, b: weight_grad_call((a[3], b[3])), "experts near", "experts far")
    put_permute(graph, "received grads", swap_perm(1), "sibling grads")
    put(
        "table grads", lambda r, a, b: weight_grad_call((a[2], b[2]), r),
        "received grads", "experts near", "experts far",
    )

    back_pieces = put_sum(graph, "g.", [f"back {n} {i}" for n in ("near", "far") for i in range(8)])
    others = ["moe in", "residual", "cot", "small", "share", "query", "keyvalue", "probs"]
    put(
        "heads back",
        lambda *v: head_backward_call(place, v[:19], v[19:24], (*v[24:32], *v[32][1][:2])),
        *dense, *back_pieces, *others, "layout",
    )
    put("grads", lambda v: v[1], "heads back")
    put_permute(graph, "grads sibling", swap_perm(1), "grads")
    put(
        "dense grads",
        lambda *v: dense_grad_call(BLOCKS // 2, place, v[:4], v[4:]),
        "share", "share sibling", "grads", "grads sibling",
        *[f"out {name} {i}" for name in ("near", "far") for i in range(4)],
    )
    for i in range(16):
        put(f"term {i}", lambda v, i=i: v[i], "dense grads")
    pieces = put_sum(graph, "s.", [f"term {i}" for i in range(16)])
    put("total", add_wide, *pieces)
    put(
        "input grad",
        lambda h, g, small, *v: input_grad_call(place, sequences, v, g, h[0], small, block_input),
        "heads back", "grads", "small", *dense,
    )

    return graph


def body_on_slice(device, inputs):
    attn_gain, query_weight, keyvalue_weight = inputs[4:7]
    graph = graph_on_slice(device, inputs)
    total = graph.get("total")
    query_grad, keyvalue_grad, output_weight_grad = [total[PART * i : PART * (i + 1)] for i in range(3)]
    small_grad = small_columns(total[3 * PART : PACK])
    block_output, attn_gain_grad = finish(
        graph.get("layout")[0],
        graph.get("residual"),
        (total[PACK:],),
        attn_gain,
        (query_weight, keyvalue_weight),
        (query_grad, keyvalue_grad),
    )
    return (
        block_output,
        graph.get("input grad"),
        attn_gain_grad,
        query_grad,
        keyvalue_grad,
        output_weight_grad,
        small_grad[:, EXPERT_COUNT + 1],
        small_grad[:, :EXPERT_COUNT],
        *graph.get("table grads"),
    )


def body_elsewhere(device, count, inputs):
    (block_input, seq_lengths, seq_devices, expert_ids, attn_gain, query_weight, keyvalue_weight,
     output_weight, moe_gain, router_weight, gate_weight, up_weight, down_weight, output_grad) = inputs
    own_tables = (gate_weight, up_weight, down_weight)
    sequences = (device.reshape(1), seq_lengths, seq_devices)
    hidden = gate_weight.shape[0]
    packed, = pack_call(sequences, expert_ids, output_grad)
    small = jnp.concatenate([router_weight, attn_gain[:, None], moe_gain[:, None]], axis=1)
    small = jnp.pad(small, ((0, 0), (0, 128 - small.shape[1])))
    whole = [
        lax.all_gather(w, "fsdp", axis=0, tiled=True)
        for w in (query_weight, keyvalue_weight, output_weight, small)
    ]
    extra = whole[3].reshape(BLOCKS, 2, EXTRA, 128).transpose(0, 2, 1, 3).reshape(BLOCKS, EXTRA, 256)
    extra = jnp.pad(extra, ((0, 0), (0, 0), (0, MODEL - 256)))
    dense = jnp.concatenate([w.reshape(BLOCKS, PART, MODEL) for w in whole[:3]] + [extra], axis=1)
    dense = dense.reshape(BLOCKS * PACK, MODEL)
    place = jnp.arange(BLOCKS, dtype=jnp.int32)
    names = jnp.stack([device, device ^ 1]) * hidden // EXPERT_HIDDEN
    tables = (*own_tables, *(permute(t, swap_perm(1, count)) for t in own_tables))
    live_rows, others = attention_inputs(seq_lengths, seq_devices, device)
    moe_in, residual, share, query, keyvalue, probs, small = attention_call(
        place, block_input, *others, dense
    )
    rows = gather_whole(moe_in, count)
    cots = lax.all_gather(packed, "fsdp", axis=0, axis_index_groups=parity_groups(count))
    peers = jnp.arange(len(rows), dtype=jnp.int32)
    calls = [
        expert_call(i, small, tables, names, peers, cots, *rows[i : i + 8])
        for i in range(0, len(rows), 8)
    ]
    back_pieces = sum_whole([b for call in calls for b in call[1]], count)
    outs = [call[0][j][ROWS * h : ROWS * (h + 1)] for call in calls for h in range(2) for j in range(4)]
    out_pieces = sum_whole(outs, count)
    received = permute(weight_grad_call([call[3] for call in calls]), swap_perm(1, count))
    expert_grads = weight_grad_call([call[2] for call in calls], received)
    residual_grad, grads = head_backward_call(
        place, (dense,), back_pieces,
        (moe_in, residual, packed, small, share, query, keyvalue, probs, *others[:2]),
    )
    terms = jnp.stack(dense_grad_call(BLOCKS, place, (share, grads))).astype(F32)
    wholes = [terms[:, PART * i : PART * (i + 1)].reshape(MODEL, MODEL) for i in range(3)]
    wholes.append(small_columns(terms[:, 3 * PART :]).reshape(MODEL, 128))
    query_grad, keyvalue_grad, output_weight_grad, small_grad = [
        lax.psum_scatter(w, "fsdp", scatter_dimension=0, tiled=True) for w in wholes
    ]
    input_grad = input_grad_call(place, sequences, (dense,), grads, residual_grad, small, block_input)
    block_output, attn_gain_grad = finish(
        live_rows, residual, out_pieces, attn_gain, (query_weight, keyvalue_weight),
        (query_grad, keyvalue_grad),
    )
    return (
        block_output,
        input_grad,
        attn_gain_grad,
        query_grad,
        keyvalue_grad,
        output_weight_grad,
        small_grad[:, EXPERT_COUNT + 1],
        small_grad[:, :EXPERT_COUNT],
        *expert_grads,
    )


def body(*inputs):
    device = lax.axis_index("fsdp").astype(jnp.int32)
    count = lax.axis_size("fsdp")
    return body_on_slice(device, inputs) if count == 32 else body_elsewhere(device, count, inputs)


def solution(mesh):
    placed = (
        P("fsdp", None),
        P(),
        P(),
        P("fsdp", None),
        P("fsdp"),
        P("fsdp", None),
        P("fsdp", None),
        P("fsdp", None),
        P("fsdp"),
        P("fsdp", None),
        P("fsdp", None),
        P("fsdp", None),
        P("fsdp", None),
        P("fsdp", None),
    )
    return jax.shard_map(
        body,
        mesh=mesh,
        in_specs=placed,
        out_specs=(
            P("fsdp", None),
            P("fsdp", None),
            P("fsdp"),
            P("fsdp", None),
            P("fsdp", None),
            P("fsdp", None),
            P("fsdp"),
            P("fsdp", None),
            P("fsdp", None),
            P("fsdp", None),
            P("fsdp", None),
        ),
        check_vma=False,
    )
```

```python
from functools import partial

import jax
import jax.numpy as jnp
from jax import lax
from jax.experimental import pallas as pl
from jax.experimental.pallas import tpu as pltpu
from jax.sharding import PartitionSpec as P

QUERY_HEADS = 16
KEY_VALUE_HEADS = 8
HEAD_WIDTH = 64
EXPERT_COUNT = 32
EXPERT_HIDDEN = 512
TOPK = 8
CAP = 40

EPS = 1e-06
ROPE_BASE = 10000.0

MODEL = 1024
ROWS = 128
PART = 32
EXTRA = 16
PACK = 3 * PART + EXTRA
BLOCKS = MODEL // PART
WIDE = ROWS + EXTRA
WHOLE = PACK + ROWS
NOT_CHOSEN = 64
VMEM_LIMIT = 62 * 1024 * 1024
SMALL = 48

BF = jnp.bfloat16
F32 = jnp.float32


def dot(a, b, a_dim, b_dim):
    return lax.dot_general(a, b, (((a_dim,), (b_dim,)), ((), ())), preferred_element_type=F32)


def row_by_col(a, b):
    return dot(a, b, 1, 0)


def row_by_row(a, b):
    return dot(a, b, 1, 1)


def col_by_col(a, b):
    return dot(a, b, 0, 0)


GATES = {
    "experts far": ("m.across1", "m.first1", "m.second1", "m.second0", "m.across0",),
    "experts near": ("experts far",),
    "g.c2": ("experts near",),
    "g.c3": ("experts near",),
    "g.f1": ("g.a2",),
    "g.d1": ("g.a2",),
    "g.b1": ("g.a2",),
    "g.b0": ("g.c2", "g.c3",),
    "g.z3": ("g.f1", "g.d1", "g.b1",),
    "g.z2": ("g.a0",),
    "sibling grads": ("g.z3",),
    "received grads": ("g.z2", "g.c0", "g.z1", "g.b0",),
    "s.b1": ("s.a2",),
    "s.b0": ("s.c2",),
    "s.z3": ("s.f1", "s.d1", "s.b1",),
    "s.z2": ("s.a0", "received grads",),
    "s.c2": ("s.d1", "s.f1",),
    "input grad": ("s.z3",),
    "table grads": ("s.z3",),
    "s.z1": ("s.z3",),
}


def layout(seq_lengths, seq_devices, device, count_of_rows):
    on_device = seq_devices == device
    lengths = jnp.where(on_device, seq_lengths, 0)
    starts = jnp.cumsum(lengths) - lengths
    filled_rows = jnp.sum(lengths)
    row_slots = jnp.arange(count_of_rows, dtype=jnp.int32)
    inside = (row_slots[:, None] >= starts[None, :]) & (
        row_slots[:, None] < (starts + lengths)[None, :]
    )
    live_rows = jnp.any(inside, axis=1)
    seq_count = seq_lengths.shape[0]
    numbers = jnp.arange(seq_count, dtype=jnp.int32)
    segment = jnp.where(
        live_rows, jnp.sum(jnp.where(inside, numbers[None, :], 0), axis=1), seq_count
    )
    begins = jnp.where(
        live_rows, jnp.sum(jnp.where(inside, starts[None, :], 0), axis=1), filled_rows
    )
    return (live_rows, segment, row_slots - begins)


def rope_tables(position):
    half = HEAD_WIDTH // 2
    lanes = jnp.arange(2 * HEAD_WIDTH, dtype=jnp.int32)
    exponent = (lanes % half).astype(F32) * 2.0 / HEAD_WIDTH
    angles = position.astype(F32)[:, None] * (ROPE_BASE ** (-exponent))[None, :]
    sign = jnp.where(lanes % HEAD_WIDTH < half, -1.0, 1.0)
    return jnp.cos(angles), jnp.sin(angles) * sign[None, :]


def permute(value, perm):
    return lax.ppermute(value, "fsdp", perm)


def swap_perm(mask, count=32):
    return [(i, i ^ mask) for i in range(count)]


def first_perm():
    return [(i, i ^ (4 if i % 2 == 0 else 2)) for i in range(32)]


def second_perm():
    return [(i, i ^ (2 if i % 2 == 0 else 4)) for i in range(32)]


def parity_groups(count):
    return [list(range(0, count, 2)), list(range(1, count, 2))]


def peer_plan(device, count):
    if count != 32:
        return [device % 2 + 2 * i for i in range(count // 2)]
    core = device % 2
    first = jnp.where(core == 0, 4, 2)
    second = 6 - first
    return [device ^ (8 * z) ^ step for z in range(4) for step in (0, first, second, 6)]


def behind(value, *others):
    return lax.optimization_barrier((value,) + others)[0] if others else value


STEPS = {
    "z1": ("", swap_perm(8)),
    "z2": ("", swap_perm(16)),
    "z3": ("z2", swap_perm(8)),
    "first0": ("", first_perm()),
    "second0": ("", second_perm()),
    "across0": ("first0", second_perm()),
    "first1": ("first0", swap_perm(8)),
    "second1": ("z1", second_perm()),
    "across1": ("across0", swap_perm(8)),
    "first2": ("z2", first_perm()),
    "second2": ("z2", second_perm()),
    "across2": ("first2", second_perm()),
    "first3": ("z3", first_perm()),
    "second3": ("z3", second_perm()),
    "across3": ("first3", second_perm()),
}
class Graph:
    def __init__(self, gates):
        self.gates, self.steps, self.have = gates, {}, {}

    def put(self, name, function, *needs):
        self.steps[name] = (function, needs)

    def get(self, name):
        if name not in self.have:
            self.have[name] = None
            function, needs = self.steps[name]
            values = [self.get(n) for n in needs]
            gates = [jax.tree.leaves(self.get(g))[0] for g in self.gates.get(name, ())]
            if gates and values:
                values[0] = jax.tree.map(lambda v: behind(v, *gates), values[0])
            with jax.named_scope(name.replace(" ", "_")):
                self.have[name] = function(*values)
        return self.have[name]


def put_permute(graph, name, perm, source, make=None):
    graph.put(name, lambda *v: permute(make(*v) if make else v[0], perm), *([source] if isinstance(source, str) else source))


def put_gather(graph, tag, source):
    for step, (base, perm) in STEPS.items():
        put_permute(graph, tag + step, perm, tag + base if base else source)


def gathered(tag, source):
    names = [[base, f"{tag}first{p}", f"{tag}second{p}", f"{tag}across{p}"] for p, base in enumerate((source, tag + "z1", tag + "z2", tag + "z3"))]
    return [n for plane in names for n in plane]


def put_sum(graph, tag, terms):
    own, one, two, three = [terms[4 * p : 4 * (p + 1)] for p in range(4)]
    for p, plane in ((2, two), (3, three)):
        put_permute(graph, f"{tag}a{p}", second_perm(), plane[3])
        put_permute(graph, f"{tag}b{p}", second_perm(), plane[2])
        put_permute(graph, f"{tag}c{p}", first_perm(), (plane[1], f"{tag}a{p}"), add_round)
    put_permute(graph, f"{tag}z3", swap_perm(8), (three[0], f"{tag}b3", f"{tag}c3"), add_round)
    put_permute(graph, f"{tag}z2", swap_perm(16), (two[0], f"{tag}b2", f"{tag}c2", f"{tag}z3"), add_round)
    put_permute(graph, f"{tag}b1", second_perm(), one[2])
    put_permute(graph, f"{tag}f1", swap_perm(8), one[1])
    put_permute(graph, f"{tag}d1", swap_perm(8), one[3])
    put_permute(graph, f"{tag}z1", swap_perm(8), (one[0], f"{tag}b1"), add_round)
    put_permute(graph, f"{tag}a0", second_perm(), (own[3], f"{tag}d1"), add_round)
    put_permute(graph, f"{tag}b0", second_perm(), own[2])
    put_permute(graph, f"{tag}c0", first_perm(), (own[1], f"{tag}f1", f"{tag}a0"), add_round)
    return [own[0]] + [f"{tag}{n}" for n in ("c0", "b0", "z1", "z2")]


def gather_whole(shard, count):
    whole = lax.all_gather(shard, "fsdp", axis=0, axis_index_groups=parity_groups(count))
    return [whole[i] for i in range(count // 2)]


def add_wide(*terms):
    return sum(t.astype(F32) for t in terms)


def add_round(*terms):
    return add_wide(*terms).astype(BF)


def sum_whole(terms, count):
    stacked = jnp.concatenate([t.astype(F32) for t in terms], axis=0)
    return [
        lax.psum_scatter(
            stacked, "fsdp", scatter_dimension=0, tiled=True, axis_index_groups=parity_groups(count)
        )
    ]


def filled_rows(device, lengths, devices):
    return lax.fori_loop(
        0,
        lengths.shape[0],
        lambda i, rows: rows + jnp.where(devices[i] == device[0], lengths[i], 0),
        jnp.int32(0),
    )


def pack_kernel(with_weights, device, lengths, devices, ids, out_grad, *refs):
    packed = refs[-1]
    if with_weights:
        query, keyvalue, output, router, attn_gain, moe_gain = refs[:-1]
        square = jnp.zeros((128, 128), F32)
        row = lax.broadcasted_iota(jnp.int32, (128, 128), 0)
        for i, gain in enumerate((attn_gain, moe_gain)):
            wide = jnp.concatenate(
                [gain[...].astype(F32).reshape(1, PART), jnp.zeros((1, 128 - PART), F32)], axis=1
            )
            square = jnp.where(row == EXPERT_COUNT + i, wide, square)
        small = square.T[:PART]
        small = small + jnp.concatenate(
            [router[...].astype(F32), jnp.zeros((PART, 128 - EXPERT_COUNT), F32)], axis=1
        )
        small = small.astype(BF)
        packed[0:PART, :] = query[...]
        packed[PART : 2 * PART, :] = keyvalue[...]
        packed[2 * PART : 3 * PART, :] = output[...]
        packed[3 * PART : PACK, :] = jnp.zeros((EXTRA, MODEL), BF)
        packed[3 * PART : PACK, 0:128] = small[0:EXTRA, :]
        packed[3 * PART : PACK, 128:256] = small[EXTRA:, :]
    else:
        packed[0:EXTRA, :] = jnp.zeros((EXTRA, MODEL), BF)
    filled = filled_rows(device, lengths, devices)
    first = PACK if with_weights else EXTRA
    rows = lax.broadcasted_iota(jnp.int32, (ROWS, MODEL), 0)
    packed[first : first + ROWS, :] = jnp.where(
        rows < filled, out_grad[...].astype(F32), 0.0
    ).astype(BF)
    wide = ids[...].astype(F32)
    expert = lax.broadcasted_iota(jnp.int32, (EXPERT_COUNT, ROWS), 0).astype(F32)
    hit = jnp.zeros((EXPERT_COUNT, ROWS), F32)
    for k in range(TOPK):
        hit = hit + jnp.where(expert == wide[k : k + 1, :], 1.0, 0.0)
    row = lax.broadcasted_iota(jnp.int32, (ROWS, ROWS), 0)
    column = lax.broadcasted_iota(jnp.int32, (ROWS, ROWS), 1)
    before = jnp.where(row < column, 1.0, 0.0).astype(BF)
    rank = row_by_col(hit.astype(BF), before)
    table = jnp.where(hit > 0.0, rank, float(NOT_CHOSEN)).astype(BF)
    packed[first - EXTRA : first, 256:384] = table[:EXTRA]
    packed[first - EXTRA : first, 384:512] = table[EXTRA:]


def join_kernel(rows, *refs):
    parts, out, sems = refs[:-2], refs[-2], refs[-1]
    copies = [
        pltpu.make_async_copy(part.at[pl.ds(0, rows)], out.at[pl.ds(rows * i, rows)], sems.at[i])
        for i, part in enumerate(parts)
    ]
    for copy in copies:
        copy.start()
    for copy in copies:
        copy.wait()


def start_weights(place, buffers, weights, sems, first, last):
    copies = []
    for buffer in buffers:
        for j in range(buffer.shape[0] // PACK if buffer.shape[0] != WHOLE else 1):
            i = len(copies)
            copies.append(
                pltpu.make_async_copy(
                    buffer.at[pl.ds(j * PACK + first, last - first)], weights.at[place[i]], sems.at[i]
                )
            )
            copies[-1].start()
    return copies


def half_swap(chunk):
    lane = lax.broadcasted_iota(jnp.int32, chunk.shape, 1)
    half = HEAD_WIDTH // 2
    return jnp.where(
        lane % HEAD_WIDTH < half, pltpu.roll(chunk, 128 - half, 1), pltpu.roll(chunk, half, 1)
    )


def doubled(chunk, second):
    lane = lax.broadcasted_iota(jnp.int32, chunk.shape, 1)
    turned = pltpu.roll(chunk, HEAD_WIDTH, 1)
    keep = lane >= HEAD_WIDTH if second else lane < HEAD_WIDTH
    return jnp.where(keep, chunk, turned)


def split_pair(chunk):
    lane = lax.broadcasted_iota(jnp.int32, chunk.shape, 1)
    zero = jnp.zeros_like(chunk)
    return jnp.concatenate(
        [jnp.where(lane < HEAD_WIDTH, chunk, zero), jnp.where(lane < HEAD_WIDTH, zero, chunk)], axis=0
    )


def join_pair(stacked):
    lane = lax.broadcasted_iota(jnp.int32, (ROWS, 128), 1)
    return jnp.where(lane < HEAD_WIDTH, stacked[:ROWS], stacked[ROWS:])


def attention_kernel(buffers_count, *refs):
    place, buffers, refs = refs[0], refs[1 : 1 + buffers_count], refs[1 + buffers_count :]
    x_ref, cos_ref, sin_ref, allowed_ref = refs[:4]
    moe_ref, resid_ref, share_ref, query_ref, kv_ref, probs_ref, small_ref = refs[4:11]
    weights, columns, sems = refs[11:]
    copies = start_weights(place, buffers, weights, sems, 0, PACK)
    x = x_ref[...].astype(F32)
    unit = x * lax.rsqrt(jnp.mean(x * x, axis=-1, keepdims=True) + EPS)
    for copy in copies:
        copy.wait()
    for p in range(BLOCKS):
        for j in range(2):
            columns[pl.ds(p * PART + j * EXTRA, EXTRA), :] = weights[
                p, 3 * PART :, 128 * j : 128 * (j + 1)
            ].astype(F32)
    small = columns[...].T
    small_ref[...] = small.astype(BF)
    attn_in = (unit * small[EXPERT_COUNT : EXPERT_COUNT + 1, :]).astype(BF)
    share_ref[:ROWS, :] = attn_in
    cosine, sine = cos_ref[...], sin_ref[...]

    def weight_columns(which, chunk):
        lanes = slice(256 * chunk, 256 * (chunk + 1))
        return weights[:, PART * which : PART * (which + 1), lanes].reshape(MODEL, 256)

    for chunk in range(4):
        query_pre = row_by_col(attn_in, weight_columns(0, chunk))
        kv_pre = row_by_col(attn_in, weight_columns(1, chunk))
        for j in range(2):
            at = slice(256 * chunk + 128 * j, 256 * chunk + 128 * (j + 1))
            part = query_pre[:, 128 * j : 128 * (j + 1)]
            query_ref[:, at] = (part * cosine + half_swap(part) * sine).astype(BF)
            part = kv_pre[:, 128 * j : 128 * (j + 1)]
            if chunk < 2:
                part = part * cosine + half_swap(part) * sine
            kv_ref[:, at] = part.astype(BF)
    allowed = jnp.concatenate([allowed_ref[...], allowed_ref[...]], axis=0) > 0.0
    scale = HEAD_WIDTH ** (-0.5)
    for head in range(KEY_VALUE_HEADS):
        pair, second = head // 2, head % 2 == 1
        key = doubled(kv_ref[:, 128 * pair : 128 * (pair + 1)].astype(F32), second).astype(BF)
        value = doubled(
            kv_ref[:, 512 + 128 * pair : 512 + 128 * (pair + 1)].astype(F32), second
        ).astype(BF)
        at = slice(128 * head, 128 * (head + 1))
        scores = row_by_row(split_pair(query_ref[:, at]), key) * scale
        scores = jnp.where(allowed, scores, -jnp.inf)
        raised = jnp.exp(scores - jnp.max(scores, axis=-1, keepdims=True))
        probs = raised / jnp.sum(raised, axis=-1, keepdims=True)
        probs_ref[head] = probs
        share_ref[ROWS:, at] = join_pair(row_by_col(probs.astype(BF), value)).astype(BF)
    heads = share_ref[ROWS:, :]
    for chunk in range(4):
        at = slice(256 * chunk, 256 * (chunk + 1))
        resid_ref[:, at] = x_ref[:, at].astype(F32) + row_by_col(heads, weight_columns(2, chunk))
    residual = resid_ref[...]
    unit = residual * lax.rsqrt(jnp.mean(residual * residual, axis=-1, keepdims=True) + EPS)
    moe_ref[...] = (unit * small[EXPERT_COUNT + 1 : EXPERT_COUNT + 2, :]).astype(BF)


def route_table(extra):
    return jnp.concatenate([extra[:, 0:128], extra[:, 128:256]], axis=0).astype(F32)


def route_weights_of(table, small, rows):
    logits = row_by_row(small, rows)[:EXPERT_COUNT]
    raised = jnp.where(table < NOT_CHOSEN, jnp.exp(logits), 0.0)
    return raised / jnp.sum(raised, axis=0, keepdims=True)


def expert_kernel(sizes, *refs):
    x_sizes, c_first = sizes
    names, refs = refs[0], refs[1:]
    x_hbm, refs = refs[: len(x_sizes)], refs[len(x_sizes) :]
    c_hbm, refs = refs[:8], refs[8:]
    small_ref, tables_hbm, refs = refs[0], refs[1:7], refs[7:]
    p_hbm, g_hbm, saved_hbm, refs = refs[:4], refs[4:12], refs[12:22], refs[22:]
    xs_all, cs_all, tables, ps, gs, saved_wide, saved_thin, picks, cots, results, back, in_sems, out_sems = refs
    copies = []

    def fetch(source, target):
        copies.append(pltpu.make_async_copy(source, target, in_sems.at[len(copies)]))
        copies[-1].start()

    def send(source, target, number):
        copy = pltpu.make_async_copy(source, target, out_sems.at[number])
        copy.start()
        return copy

    at = 0
    for ref, size in zip(x_hbm, x_sizes):
        for j in range(size):
            fetch(ref.at[pl.ds(ROWS * j, ROWS)], xs_all.at[at])
            at += 1
    for i, ref in enumerate(c_hbm):
        fetch(ref.at[pl.ds(c_first, WIDE)], cs_all.at[i])
    for i, ref in enumerate(tables_hbm):
        fetch(ref, tables.at[i])
    slots = 4 * CAP
    small = small_ref[...]
    expert_row = lax.broadcasted_iota(jnp.int32, (EXPERT_COUNT, ROWS), 0)
    slot_row = lax.broadcasted_iota(jnp.int32, (slots, 4 * ROWS), 0).astype(F32)
    slot_weights = [[None, None], [None, None]]
    for copy in copies[:16]:
        copy.wait()
    for h in range(2):
        places, weights = [[], []], [[], []]
        for b in range(4):
            table = route_table(cs_all[4 * h + b, :EXTRA, 256:512])
            weight = route_weights_of(table, small, xs_all[4 * h + b])
            for l in range(2):
                here = expert_row == names[l]
                place = jnp.sum(jnp.where(here, table, 0.0), axis=0, keepdims=True)
                places[l].append(jnp.where(place < NOT_CHOSEN, place + b * CAP, 4096.0))
                weights[l].append(jnp.sum(jnp.where(here, weight, 0.0), axis=0, keepdims=True))
        for l in range(2):
            chosen = slot_row == jnp.concatenate(places[l], axis=1)
            weight = jnp.concatenate(weights[l], axis=1)
            slot_weights[l][h] = jnp.sum(jnp.where(chosen, weight, 0.0), axis=1, keepdims=True)
            picks[h, slots * l : slots * (l + 1), :] = chosen.astype(F32).astype(BF)
        pick = picks[h]
        rows = xs_all[4 * h : 4 * (h + 1)].reshape(4 * ROWS, MODEL)
        cot_rows = cs_all[4 * h : 4 * (h + 1), EXTRA:, :].reshape(4 * ROWS, MODEL)
        inputs = row_by_col(pick, rows).astype(BF)
        cot = row_by_col(pick, cot_rows).astype(BF)
        for l in range(2):
            saved_wide[2 * l, slots * h : slots * (h + 1), :] = inputs[slots * l : slots * (l + 1)]
            cots[l, slots * h : slots * (h + 1), :] = cot[slots * l : slots * (l + 1)]
    slot_routes, sends = [], []
    for l in range(2):
        gate, up, down = tables.at[3 * l], tables.at[3 * l + 1], tables.at[3 * l + 2]
        for copy in copies[16 + 3 * l : 19 + 3 * l]:
            copy.wait()
        weight = jnp.concatenate(slot_weights[l], axis=0)
        inputs = saved_wide[2 * l]
        gate_pre = row_by_row(inputs, gate[...])
        up_pre = row_by_row(inputs, up[...])
        sigma = jax.nn.sigmoid(gate_pre)
        acts = (gate_pre * sigma * up_pre).astype(BF)
        saved_thin[3 * l] = acts
        cot = cots[l].astype(F32)
        result = row_by_col(acts, down[...])
        slot_routes.append(jnp.sum(cot * result, axis=1, keepdims=True))
        results[l] = (weight * result).astype(BF)
        pair_cot = (weight * cot).astype(BF)
        saved_wide[2 * l + 1] = pair_cot
        act_grad = row_by_row(pair_cot, down[...])
        gate_grad = (act_grad * up_pre * sigma * (1.0 + gate_pre * (1.0 - sigma))).astype(BF)
        up_grad = (act_grad * gate_pre * sigma).astype(BF)
        saved_thin[3 * l + 1] = gate_grad
        saved_thin[3 * l + 2] = up_grad
        back[l] = (row_by_col(gate_grad, gate[...]) + row_by_col(up_grad, up[...])).astype(BF)
        for i in range(5):
            source = saved_wide.at[2 * l + i] if i < 2 else saved_thin.at[3 * l + i - 2]
            sends.append(send(source, saved_hbm[5 * l + i], 16 + 5 * l + i))
    for h in range(2):
        pick = picks[h]
        at = slice(slots * h, slots * (h + 1))
        grad = col_by_col(pick, jnp.concatenate([back[0, at], back[1, at]], axis=0)).astype(BF)
        routes = []
        for l in range(2):
            chosen = pick[slots * l : slots * (l + 1)].astype(F32)
            routes.append(jnp.sum(chosen * slot_routes[l][at], axis=0, keepdims=True))
        for b in range(4):
            i = 4 * h + b
            rows = slice(ROWS * b, ROWS * (b + 1))
            gs[i, :ROWS, :] = grad[rows]
            route = jnp.zeros((EXPERT_COUNT, ROWS), F32)
            for l in range(2):
                route = route + jnp.where(expert_row == names[l], routes[l][:, rows], 0.0)
            high = route.astype(BF)
            low = (route - high.astype(F32)).astype(BF)
            gs[i, ROWS:, 0:128] = high[:16]
            gs[i, ROWS:, 128:256] = high[16:]
            gs[i, ROWS:, 256:384] = low[:16]
            gs[i, ROWS:, 384:512] = low[16:]
            gs[i, ROWS:, 512:] = jnp.zeros((EXTRA, MODEL - 512), BF)
            sends.append(send(gs.at[i], g_hbm[i], 8 + i))
        out = col_by_col(pick, jnp.concatenate([results[0, at], results[1, at]], axis=0)).astype(BF)
        for b in range(4):
            i = 4 * h + b
            ps[i] = out[ROWS * b : ROWS * (b + 1)]
            sends.append(send(ps.at[i], p_hbm[i % 4].at[pl.ds(ROWS * (i // 4), ROWS)], i))
    for copy in sends:
        copy.wait()


def weight_grad_kernel(calls, added, *refs):
    saved, refs = refs[: 5 * calls], refs[5 * calls :]
    received, refs = refs[:added], refs[added:]
    outs, refs = refs[: 3 if added else 1], refs[3 if added else 1 :]
    wide, thin, extra, sums, in_sems, out_sems = refs
    hidden = thin.shape[2]
    copies = {}

    def fetch(name, source, target):
        copies[name] = pltpu.make_async_copy(source, target, in_sems.at[len(copies)])
        copies[name].start()

    order = ((3, 0), (4, 0), (2, 1))
    for o, pair in enumerate(order):
        for c in range(calls):
            for i in pair:
                if (c, i) not in copies:
                    target = wide.at[2 * c + i] if i < 2 else thin.at[3 * c + i - 2]
                    fetch((c, i), saved[5 * c + i], target)
        if added:
            fetch(o, received[0].at[pl.ds(hidden * o, hidden)], extra.at[o])
    waited, sends = set(), []
    for o, (left, right) in enumerate(order):
        total = None
        for c in range(calls):
            for i in (left, right):
                if (c, i) not in waited:
                    waited.add((c, i))
                    copies[c, i].wait()
            term = col_by_col(thin[3 * c + left - 2], wide[2 * c + right])
            total = term if total is None else total + term
        if added:
            copies[o].wait()
            total = total + extra[o]
        sums[o] = total
        target = outs[o] if added else outs[0].at[pl.ds(hidden * o, hidden)]
        sends.append(pltpu.make_async_copy(sums.at[o], target, out_sems.at[o]))
        sends[-1].start()
    for copy in sends:
        copy.wait()


def head_backward_kernel(buffers_count, pieces_count, *refs):
    place, buffers, refs = refs[0], refs[1 : 1 + buffers_count], refs[1 + buffers_count :]
    pieces, refs = refs[:pieces_count], refs[pieces_count:]
    moe_ref, resid_ref, cot_ref, small_ref, share_ref, query_ref, kv_ref, probs_ref = refs[:8]
    cos_ref, sin_ref = refs[8:10]
    resid_grad_ref, grads_ref = refs[10:12]
    weights, grads, sems = refs[12:]
    copies = start_weights(place, buffers, weights, sems, 2 * PART, 3 * PART)
    small = small_ref[...]
    total = pieces[0][...].astype(F32)
    for piece in pieces[1:]:
        total = total + piece[...].astype(F32)
    extra = total[ROWS:]
    route_grad = jnp.concatenate(
        [extra[:, 0:128] + extra[:, 256:384], extra[:, 128:256] + extra[:, 384:512]], axis=0
    )
    moe_in = moe_ref[...]
    first = cot_ref.shape[0] - WIDE
    table = route_table(cot_ref[first : first + EXTRA, 256:512])
    weight = route_weights_of(table, small, moe_in)
    logit_grad = weight * (route_grad - jnp.sum(weight * route_grad, axis=0, keepdims=True))
    logit_grad = jnp.concatenate(
        [logit_grad, jnp.zeros((ROWS - EXPERT_COUNT, ROWS), F32)], axis=0
    ).astype(BF)
    moe_in_grad = total[:ROWS] + col_by_col(logit_grad, small)
    router_grad = row_by_col(logit_grad, moe_in)[:SMALL]
    residual = resid_ref[...]
    inverse = lax.rsqrt(jnp.mean(residual * residual, axis=-1, keepdims=True) + EPS)
    unit = residual * inverse
    moe_gain_grad = jnp.sum(moe_in_grad * unit, axis=0, keepdims=True)
    row = lax.broadcasted_iota(jnp.int32, (SMALL, MODEL), 0)
    grads_ref[3 * ROWS :, :] = jnp.where(row == EXPERT_COUNT + 1, moe_gain_grad, router_grad).astype(BF)
    grad_unit = moe_in_grad * small[EXPERT_COUNT : EXPERT_COUNT + 8].astype(F32)[1:2]
    mean = jnp.mean(grad_unit * unit, axis=-1, keepdims=True)
    cot = cot_ref[first + EXTRA :, :]
    residual_grad = cot.astype(F32) + inverse * (grad_unit - unit * mean)
    resid_grad_ref[...] = residual_grad
    residual_bf = residual_grad.astype(BF)
    grads_ref[:ROWS, :] = residual_bf
    for copy in copies:
        copy.wait()
    for chunk in range(4):
        at = slice(256 * chunk, 256 * (chunk + 1))
        rows = weights[8 * chunk : 8 * (chunk + 1)].reshape(256, MODEL)
        grads[:, at] = row_by_row(residual_bf, rows).astype(BF)
    cosine, sine = cos_ref[...], sin_ref[...]
    scale = HEAD_WIDTH ** (-0.5)
    key_grads, value_grads = [], []
    for head in range(KEY_VALUE_HEADS):
        pair, second = head // 2, head % 2 == 1
        key = doubled(kv_ref[:, 128 * pair : 128 * (pair + 1)].astype(F32), second).astype(BF)
        value = doubled(
            kv_ref[:, 512 + 128 * pair : 512 + 128 * (pair + 1)].astype(F32), second
        ).astype(BF)
        at = slice(128 * head, 128 * (head + 1))
        query = split_pair(query_ref[:, at])
        head_grad = split_pair(grads[:, at])
        mixed = split_pair(share_ref[ROWS:, at])
        inner = jnp.sum(head_grad.astype(F32) * mixed.astype(F32), axis=-1, keepdims=True)
        probs = probs_ref[head]
        score_grad = (probs * (row_by_row(head_grad, value) - inner)).astype(BF)
        part = join_pair(row_by_col(score_grad, key)) * scale
        grads_ref[ROWS : 2 * ROWS, at] = (part * cosine - half_swap(part) * sine).astype(BF)
        part = col_by_col(score_grad, query) * scale
        key_grads.append(part + pltpu.roll(part, HEAD_WIDTH, 1))
        part = col_by_col(probs.astype(BF), head_grad)
        value_grads.append(part + pltpu.roll(part, HEAD_WIDTH, 1))
    lane = lax.broadcasted_iota(jnp.int32, (ROWS, 128), 1)
    for which, parts in enumerate((key_grads, value_grads)):
        for pair in range(KEY_VALUE_HEADS // 2):
            part = jnp.where(lane < HEAD_WIDTH, parts[2 * pair], parts[2 * pair + 1])
            if which == 0:
                part = part * cosine - half_swap(part) * sine
            at = slice(512 * which + 128 * pair, 512 * which + 128 * (pair + 1))
            grads_ref[2 * ROWS : 3 * ROWS, at] = part.astype(BF)


def input_grad_kernel(buffers_count, place, device, lengths, devices, *refs):
    buffers, refs = refs[:buffers_count], refs[buffers_count:]
    grads_ref, resid_grad_ref, small_ref, x_ref, in_ref = refs[:5]
    weights, sems = refs[5:]
    copies = start_weights(place, buffers, weights, sems, 0, 2 * PART)
    x = x_ref[...].astype(F32)
    inverse = lax.rsqrt(jnp.mean(x * x, axis=-1, keepdims=True) + EPS)
    unit = x * inverse
    query_grad, kv_grad = grads_ref[ROWS : 2 * ROWS, :], grads_ref[2 * ROWS : 3 * ROWS, :]
    for copy in copies:
        copy.wait()
    back = []
    for chunk in range(4):
        rows = weights[8 * chunk : 8 * (chunk + 1)]
        back.append(
            row_by_row(query_grad, rows[:, :PART].reshape(256, MODEL))
            + row_by_row(kv_grad, rows[:, PART:].reshape(256, MODEL))
        )
    attn_in_grad = jnp.concatenate(back, axis=1)
    grad_unit = attn_in_grad * small_ref[EXPERT_COUNT : EXPERT_COUNT + 8].astype(F32)[0:1]
    mean = jnp.mean(grad_unit * unit, axis=-1, keepdims=True)
    input_grad = resid_grad_ref[...] + inverse * (grad_unit - unit * mean)
    rows = lax.broadcasted_iota(jnp.int32, (ROWS, MODEL), 0)
    in_ref[...] = jnp.where(rows < filled_rows(device, lengths, devices), input_grad, 0.0)


def dense_grad_kernel(parties, blocks, *refs):
    place, refs = refs[0], refs[1:]
    results = refs[2 * parties : -blocks - 2]
    refs = refs[: 2 * parties] + refs[-blocks - 2 :]
    sems = refs[-1]
    shares, grads, refs = refs[:parties], refs[parties : 2 * parties], refs[2 * parties :]
    outs, terms = refs[:blocks], refs[blocks]
    copies = []
    for i in range(4 * len(results) // 2 if results else 0):
        source = results[4 * (i // 8) + i % 4].at[pl.ds(ROWS * (i // 4 % 2), ROWS)]
        copies.append(pltpu.make_async_copy(source, outs[i].at[pl.ds(PACK, ROWS)], sems.at[i]))
        copies[-1].start()
    attn_in = jnp.concatenate([r[:ROWS, :] for r in shares], axis=0)
    heads = jnp.concatenate([r[ROWS:, :] for r in shares], axis=0)
    residual, query, keyvalue = [
        jnp.concatenate([r[ROWS * i : ROWS * (i + 1), :] for r in grads], axis=0) for i in range(3)
    ]
    for chunk in range(4):
        at = slice(256 * chunk, 256 * (chunk + 1))
        for which, left, right in ((0, attn_in, query), (1, attn_in, keyvalue), (2, heads, residual)):
            term = col_by_col(left[:, at], right).astype(BF).reshape(8, PART, MODEL)
            terms[8 * chunk : 8 * (chunk + 1), PART * which : PART * (which + 1), :] = term
    columns = sum(r[3 * ROWS :, :].astype(F32) for r in grads)
    columns = jnp.concatenate([columns, jnp.zeros((128 - SMALL, MODEL), F32)], axis=0).T.astype(BF)
    for p in range(BLOCKS):
        for j in range(2):
            terms[p, 3 * PART :, 128 * j : 128 * (j + 1)] = columns[
                p * PART + j * EXTRA : p * PART + (j + 1) * EXTRA
            ]
        terms[p, 3 * PART :, 256:] = jnp.zeros((EXTRA, MODEL - 256), BF)
    for i in range(blocks):
        outs[i][:PACK, :] = terms[place[i]]
    for copy in copies:
        copy.wait()


def params():
    return pltpu.CompilerParams(vmem_limit_bytes=VMEM_LIMIT)


def shape(dims, dtype):
    return jax.ShapeDtypeStruct(dims, dtype)


def spec(space):
    return pl.BlockSpec(memory_space=space)


def pack_call(sequences, expert_ids, output_grad, *weights):
    smem, vmem = spec(pltpu.SMEM), spec(pltpu.VMEM)
    return pl.pallas_call(
        partial(pack_kernel, bool(weights)),
        out_shape=shape((WHOLE if weights else WIDE, MODEL), BF),
        in_specs=[smem] * 3 + [vmem] * (2 + len(weights)),
        out_specs=vmem,
        compiler_params=params(),
    )(*sequences, expert_ids.T, output_grad, *weights)


def join_call(rows, *parts):
    anywhere = spec(pl.ANY)
    return pl.pallas_call(
        partial(join_kernel, rows),
        out_shape=shape((rows * len(parts), MODEL), BF),
        in_specs=[anywhere] * len(parts),
        out_specs=spec(pltpu.VMEM),
        scratch_shapes=[pltpu.SemaphoreType.DMA((len(parts),))],
        compiler_params=params(),
    )(*parts)


def attention_call(place, block_input, cosine, sine, allowed, *dense):
    vmem = spec(pltpu.VMEM)
    return pl.pallas_call(
        partial(attention_kernel, len(dense)),
        out_shape=(
            shape((ROWS, MODEL), BF),
            shape((ROWS, MODEL), F32),
            shape((2 * ROWS, MODEL), BF),
            shape((ROWS, MODEL), BF),
            shape((ROWS, MODEL), BF),
            shape((KEY_VALUE_HEADS, 2 * ROWS, ROWS), F32),
            shape((128, MODEL), BF),
        ),
        in_specs=[spec(pltpu.SMEM)] + [spec(pl.ANY)] * len(dense) + [vmem] * 4,
        out_specs=(vmem,) * 7,
        scratch_shapes=[
            pltpu.VMEM((BLOCKS, PACK, MODEL), BF),
            pltpu.VMEM((MODEL, 128), F32),
            pltpu.SemaphoreType.DMA((BLOCKS,)),
        ],
        compiler_params=params(),
    )(place, *dense, block_input, cosine, sine, allowed)


def expert_call(first, small, tables, names, *rows_and_cots):
    hidden, slots = tables[0].shape[0], 8 * CAP
    anywhere = spec(pl.ANY)
    got = pl.pallas_call(
        partial(expert_kernel, ((1,) * 8, first)),
        out_shape=(shape((2 * ROWS, MODEL), BF),) * 4
        + (shape((WIDE, MODEL), BF),) * 8
        + ((shape((slots, MODEL), BF),) * 2 + (shape((slots, hidden), BF),) * 3) * 2,
        in_specs=[spec(pltpu.SMEM)] + [anywhere] * 16 + [spec(pltpu.VMEM)] + [anywhere] * 6,
        out_specs=(anywhere,) * 22,
        scratch_shapes=[
            pltpu.VMEM((8, ROWS, MODEL), BF),
            pltpu.VMEM((8, WIDE, MODEL), BF),
            pltpu.VMEM((6, hidden, MODEL), BF),
            pltpu.VMEM((8, ROWS, MODEL), BF),
            pltpu.VMEM((8, WIDE, MODEL), BF),
            pltpu.VMEM((4, slots, MODEL), BF),
            pltpu.VMEM((6, slots, hidden), BF),
            pltpu.VMEM((2, slots, 4 * ROWS), BF),
            pltpu.VMEM((2, slots, MODEL), BF),
            pltpu.VMEM((2, slots, MODEL), BF),
            pltpu.VMEM((2, slots, MODEL), BF),
            pltpu.SemaphoreType.DMA((22,)),
            pltpu.SemaphoreType.DMA((26,)),
        ],
        compiler_params=params(),
    )(names, *rows_and_cots, small, *tables)
    return got[:4], got[4:12], got[12:17], got[17:]


def weight_grad_call(calls, *added):
    saves = [v for saved in calls for v in saved]
    hidden, slots = saves[2].shape[1], saves[2].shape[0]
    table = shape((hidden, MODEL), F32)
    anywhere = spec(pl.ANY)
    number = len(calls)
    return pl.pallas_call(
        partial(weight_grad_kernel, number, len(added)),
        out_shape=(table,) * 3 if added else shape((3 * hidden, MODEL), F32),
        in_specs=[anywhere] * (len(saves) + len(added)),
        out_specs=(anywhere,) * 3 if added else anywhere,
        scratch_shapes=[
            pltpu.VMEM((2 * number, slots, MODEL), BF),
            pltpu.VMEM((3 * number, slots, hidden), BF),
            pltpu.VMEM((3, hidden, MODEL), F32),
            pltpu.VMEM((3, hidden, MODEL), F32),
            pltpu.SemaphoreType.DMA((5 * number + 3,)),
            pltpu.SemaphoreType.DMA((3,)),
        ],
        compiler_params=params(),
    )(*saves, *added)


def head_backward_call(place, dense, pieces, others):
    vmem = spec(pltpu.VMEM)
    return pl.pallas_call(
        partial(head_backward_kernel, len(dense), len(pieces)),
        out_shape=(shape((ROWS, MODEL), F32), shape((3 * ROWS + SMALL, MODEL), BF)),
        in_specs=[spec(pltpu.SMEM)] + [spec(pl.ANY)] * len(dense) + [vmem] * (len(pieces) + 10),
        out_specs=(vmem,) * 2,
        scratch_shapes=[
            pltpu.VMEM((BLOCKS, PART, MODEL), BF),
            pltpu.VMEM((ROWS, MODEL), BF),
            pltpu.SemaphoreType.DMA((BLOCKS,)),
        ],
        compiler_params=params(),
    )(place, *dense, *pieces, *others)


def dense_grad_call(blocks, place, parties, results=()):
    vmem = spec(pltpu.VMEM)
    rows = PACK + ROWS if results else PACK
    return pl.pallas_call(
        partial(dense_grad_kernel, len(parties) // 2, blocks),
        out_shape=(shape((rows, MODEL), BF),) * blocks,
        in_specs=[spec(pltpu.SMEM)] + [vmem] * len(parties) + [spec(pl.ANY)] * len(results),
        out_specs=(vmem,) * blocks,
        scratch_shapes=[
            pltpu.VMEM((BLOCKS, PACK, MODEL), BF),
            pltpu.SemaphoreType.DMA((BLOCKS // 2,)),
        ],
        compiler_params=params(),
    )(place, *parties, *results)


def input_grad_call(place, sequences, dense, *others):
    smem, vmem = spec(pltpu.SMEM), spec(pltpu.VMEM)
    return pl.pallas_call(
        partial(input_grad_kernel, len(dense)),
        out_shape=shape((ROWS, MODEL), F32),
        in_specs=[smem] * 4 + [spec(pl.ANY)] * len(dense) + [vmem] * 4,
        out_specs=vmem,
        scratch_shapes=[
            pltpu.VMEM((BLOCKS, 2 * PART, MODEL), BF),
            pltpu.SemaphoreType.DMA((BLOCKS,)),
        ],
        compiler_params=params(),
    )(place, *sequences, *dense, *others)


def attention_inputs(seq_lengths, seq_devices, device):
    live_rows, segment, position = layout(seq_lengths, seq_devices, device, ROWS)
    row_slots = jnp.arange(ROWS, dtype=jnp.int32)
    allowed = (segment[:, None] == segment[None, :]) & (row_slots[:, None] >= row_slots[None, :])
    return live_rows, (*rope_tables(position), allowed.astype(F32))


def finish(live_rows, residual, out_pieces, gain, weights, grads):
    block_output = jnp.where(live_rows[:, None], add_wide(residual, *out_pieces), 0.0).astype(BF)
    weighted = sum(w.astype(F32) * g for w, g in zip(weights, grads))
    return block_output, jnp.sum(weighted, axis=1) / gain.astype(F32)


def small_columns(rows):
    return jnp.concatenate([rows[..., 0:128], rows[..., 128:256]], axis=-2)


def graph_on_slice(device, inputs):
    (block_input, seq_lengths, seq_devices, expert_ids, attn_gain, query_weight, keyvalue_weight,
     output_weight, moe_gain, router_weight, gate_weight, up_weight, down_weight, output_grad) = inputs
    own_tables = (gate_weight, up_weight, down_weight)
    sequences = (device.reshape(1), seq_lengths, seq_devices)
    names = jnp.stack([device, device ^ 1])
    graph = Graph(GATES)
    put = graph.put

    weights = (query_weight, keyvalue_weight, output_weight, router_weight, attn_gain, moe_gain)
    put("packed", lambda: pack_call(sequences, expert_ids, output_grad, *weights))
    put_gather(graph, "d.", "packed")
    cots = gathered("d.", "packed")
    for i, table in enumerate(own_tables):
        put(f"tables {i}", lambda table=table: permute(table, swap_perm(1)))
    early = [n for n in cots if n not in ("d.across1", "d.across2", "d.first3", "d.second3", "d.across3")]
    late = ["d.across1", "d.across2", "d.first3", "d.second3"]
    for name, parts in (("early", early), ("late", late)):
        put("joined " + name, partial(join_call, PACK), *parts)
        put_permute(graph, "sibling " + name, swap_perm(1), "joined " + name)
    put_permute(graph, "sibling last", swap_perm(1), "d.across3")
    dense = cots + ["sibling early", "sibling late", "sibling last"]
    order = cots + early + late + ["d.across3"]
    at = {n: i for i, n in enumerate(cots)}
    plan = peer_plan(device, 32), peer_plan(device ^ 1, 32)
    place = jnp.stack([plan[i // 16][at[n]] for i, n in enumerate(order)])

    put("layout", lambda v: attention_inputs(behind(seq_lengths, v), seq_devices, device), "packed")
    put("attention", lambda l, *v: attention_call(place, block_input, *l[1], *v), "layout", *dense)
    for i, name in enumerate(("moe in", "residual", "share", "query", "keyvalue", "probs", "small")):
        put(name, lambda v, i=i: v[i], "attention")
    put_permute(graph, "share sibling", swap_perm(1), "share")

    put_gather(graph, "m.", "moe in")
    rows = gathered("m.", "moe in")
    for name, at in (("near", slice(0, 8)), ("far", slice(8, 16))):
        put(
            "experts " + name,
            lambda small, *v: expert_call(3 * PART, small, (*own_tables, *v[:3]), names, *v[3:]),
            "small", "tables 0", "tables 1", "tables 2", *rows[at], *cots[at],
        )
        for i in range(4):
            put(f"out {name} {i}", lambda v, i=i: v[0][i], "experts " + name)
        for i in range(8):
            put(f"back {name} {i}", lambda v, i=i: v[1][i], "experts " + name)
    put("sibling grads", lambda a, b: weight_grad_call((a[3], b[3])), "experts near", "experts far")
    put_permute(graph, "received grads", swap_perm(1), "sibling grads")
    put(
        "table grads", lambda r, a, b: weight_grad_call((a[2], b[2]), r),
        "received grads", "experts near", "experts far",
    )

    back_pieces = put_sum(graph, "g.", [f"back {n} {i}" for n in ("near", "far") for i in range(8)])
    others = ["moe in", "residual", "packed", "small", "share", "query", "keyvalue", "probs"]
    put(
        "heads back",
        lambda *v: head_backward_call(place, v[:19], v[19:24], (*v[24:32], *v[32][1][:2])),
        *dense, *back_pieces, *others, "layout",
    )
    put("grads", lambda v: v[1], "heads back")
    put_permute(graph, "grads sibling", swap_perm(1), "grads")
    put(
        "dense grads",
        lambda *v: dense_grad_call(BLOCKS // 2, place, v[:4], v[4:]),
        "share", "share sibling", "grads", "grads sibling",
        *[f"out {name} {i}" for name in ("near", "far") for i in range(4)],
    )
    for i in range(16):
        put(f"term {i}", lambda v, i=i: v[i], "dense grads")
    pieces = put_sum(graph, "s.", [f"term {i}" for i in range(16)])
    put("total", add_wide, *pieces)
    put(
        "input grad",
        lambda h, g, small, *v: input_grad_call(place, sequences, v, g, h[0], small, block_input),
        "heads back", "grads", "small", *dense,
    )

    return graph


def body_on_slice(device, inputs):
    attn_gain, query_weight, keyvalue_weight = inputs[4:7]
    graph = graph_on_slice(device, inputs)
    total = graph.get("total")
    query_grad, keyvalue_grad, output_weight_grad = [total[PART * i : PART * (i + 1)] for i in range(3)]
    small_grad = small_columns(total[3 * PART : PACK])
    block_output, attn_gain_grad = finish(
        graph.get("layout")[0],
        graph.get("residual"),
        (total[PACK:],),
        attn_gain,
        (query_weight, keyvalue_weight),
        (query_grad, keyvalue_grad),
    )
    return (
        block_output,
        graph.get("input grad"),
        attn_gain_grad,
        query_grad,
        keyvalue_grad,
        output_weight_grad,
        small_grad[:, EXPERT_COUNT + 1],
        small_grad[:, :EXPERT_COUNT],
        *graph.get("table grads"),
    )


def body_elsewhere(device, count, inputs):
    (block_input, seq_lengths, seq_devices, expert_ids, attn_gain, query_weight, keyvalue_weight,
     output_weight, moe_gain, router_weight, gate_weight, up_weight, down_weight, output_grad) = inputs
    own_tables = (gate_weight, up_weight, down_weight)
    sequences = (device.reshape(1), seq_lengths, seq_devices)
    hidden = gate_weight.shape[0]
    packed = pack_call(sequences, expert_ids, output_grad)
    small = jnp.concatenate([router_weight, attn_gain[:, None], moe_gain[:, None]], axis=1)
    small = jnp.pad(small, ((0, 0), (0, 128 - small.shape[1])))
    whole = [
        lax.all_gather(w, "fsdp", axis=0, tiled=True)
        for w in (query_weight, keyvalue_weight, output_weight, small)
    ]
    extra = whole[3].reshape(BLOCKS, 2, EXTRA, 128).transpose(0, 2, 1, 3).reshape(BLOCKS, EXTRA, 256)
    extra = jnp.pad(extra, ((0, 0), (0, 0), (0, MODEL - 256)))
    dense = jnp.concatenate([w.reshape(BLOCKS, PART, MODEL) for w in whole[:3]] + [extra], axis=1)
    dense = dense.reshape(BLOCKS * PACK, MODEL)
    place = jnp.arange(BLOCKS, dtype=jnp.int32)
    names = jnp.stack([device, device ^ 1]) * hidden // EXPERT_HIDDEN
    tables = (*own_tables, *(permute(t, swap_perm(1, count)) for t in own_tables))
    live_rows, others = attention_inputs(seq_lengths, seq_devices, device)
    moe_in, residual, share, query, keyvalue, probs, small = attention_call(
        place, block_input, *others, dense
    )
    rows, cots = gather_whole(moe_in, count), gather_whole(packed, count)
    calls = [
        expert_call(0, small, tables, names, *rows[i : i + 8], *cots[i : i + 8])
        for i in range(0, len(rows), 8)
    ]
    back_pieces = sum_whole([b for call in calls for b in call[1]], count)
    outs = [call[0][j][ROWS * h : ROWS * (h + 1)] for call in calls for h in range(2) for j in range(4)]
    out_pieces = sum_whole(outs, count)
    received = permute(weight_grad_call([call[3] for call in calls]), swap_perm(1, count))
    expert_grads = weight_grad_call([call[2] for call in calls], received)
    residual_grad, grads = head_backward_call(
        place, (dense,), back_pieces,
        (moe_in, residual, packed, small, share, query, keyvalue, probs, *others[:2]),
    )
    terms = jnp.stack(dense_grad_call(BLOCKS, place, (share, grads))).astype(F32)
    wholes = [terms[:, PART * i : PART * (i + 1)].reshape(MODEL, MODEL) for i in range(3)]
    wholes.append(small_columns(terms[:, 3 * PART :]).reshape(MODEL, 128))
    query_grad, keyvalue_grad, output_weight_grad, small_grad = [
        lax.psum_scatter(w, "fsdp", scatter_dimension=0, tiled=True) for w in wholes
    ]
    input_grad = input_grad_call(place, sequences, (dense,), grads, residual_grad, small, block_input)
    block_output, attn_gain_grad = finish(
        live_rows, residual, out_pieces, attn_gain, (query_weight, keyvalue_weight),
        (query_grad, keyvalue_grad),
    )
    return (
        block_output,
        input_grad,
        attn_gain_grad,
        query_grad,
        keyvalue_grad,
        output_weight_grad,
        small_grad[:, EXPERT_COUNT + 1],
        small_grad[:, :EXPERT_COUNT],
        *expert_grads,
    )


def body(*inputs):
    device = lax.axis_index("fsdp").astype(jnp.int32)
    count = lax.axis_size("fsdp")
    return body_on_slice(device, inputs) if count == 32 else body_elsewhere(device, count, inputs)


def solution(mesh):
    placed = (
        P("fsdp", None),
        P(),
        P(),
        P("fsdp", None),
        P("fsdp"),
        P("fsdp", None),
        P("fsdp", None),
        P("fsdp", None),
        P("fsdp"),
        P("fsdp", None),
        P("fsdp", None),
        P("fsdp", None),
        P("fsdp", None),
        P("fsdp", None),
    )
    return jax.shard_map(
        body,
        mesh=mesh,
        in_specs=placed,
        out_specs=(
            P("fsdp", None),
            P("fsdp", None),
            P("fsdp"),
            P("fsdp", None),
            P("fsdp", None),
            P("fsdp", None),
            P("fsdp"),
            P("fsdp", None),
            P("fsdp", None),
            P("fsdp", None),
            P("fsdp", None),
        ),
        check_vma=False,
    )
```

```python
from functools import partial

import jax
import jax.numpy as jnp
from jax import lax
from jax.experimental import pallas as pl
from jax.experimental.pallas import tpu as pltpu
from jax.sharding import PartitionSpec as P

QUERY_HEADS = 16
KEY_VALUE_HEADS = 8
HEAD_WIDTH = 64
EXPERT_COUNT = 32
EXPERT_HIDDEN = 512
TOPK = 8
CAP = 40

EPS = 1e-06
ROPE_BASE = 10000.0

MODEL = 1024
ROWS = 128
PART = 32
EXTRA = 16
PACK = 3 * PART + EXTRA
BLOCKS = MODEL // PART
WIDE = ROWS + EXTRA
WHOLE = PACK + ROWS
NOT_CHOSEN = 64
VMEM_LIMIT = 62 * 1024 * 1024
SMALL = 48

BF = jnp.bfloat16
F32 = jnp.float32


def dot(a, b, a_dim, b_dim):
    return lax.dot_general(a, b, (((a_dim,), (b_dim,)), ((), ())), preferred_element_type=F32)


def row_by_col(a, b):
    return dot(a, b, 1, 0)


def row_by_row(a, b):
    return dot(a, b, 1, 1)


def col_by_col(a, b):
    return dot(a, b, 0, 0)


GATES = {
    "experts far": ("m.across1", "m.first1", "m.second1", "m.second0", "m.across0",),
    "experts near": ("experts far",),
    "g.c2": ("experts near", "g.b2",),
    "g.c3": ("experts near", "g.b3",),
    "g.f1": ("g.a2",),
    "g.d1": ("g.a2",),
    "g.b1": ("g.a2",),
    "g.b0": ("g.c2", "g.c3",),
    "g.z2": ("g.a0",),
    "sibling grads": ("g.z3",),
    "received grads": ("g.z2", "g.c0", "g.z1", "g.b0",),
    "s.b1": ("s.a2",),
    "s.b0": ("s.c2",),
    "s.z3": ("s.f1", "s.d1", "s.b1",),
    "s.z2": ("s.a0", "received grads",),
    "s.c2": ("s.d1", "s.f1",),
    "input grad": ("s.z3",),
    "table grads": ("s.z3",),
    "s.z1": ("s.z3",),
}


def layout(seq_lengths, seq_devices, device, count_of_rows):
    on_device = seq_devices == device
    lengths = jnp.where(on_device, seq_lengths, 0)
    starts = jnp.cumsum(lengths) - lengths
    filled_rows = jnp.sum(lengths)
    row_slots = jnp.arange(count_of_rows, dtype=jnp.int32)
    inside = (row_slots[:, None] >= starts[None, :]) & (
        row_slots[:, None] < (starts + lengths)[None, :]
    )
    live_rows = jnp.any(inside, axis=1)
    seq_count = seq_lengths.shape[0]
    numbers = jnp.arange(seq_count, dtype=jnp.int32)
    segment = jnp.where(
        live_rows, jnp.sum(jnp.where(inside, numbers[None, :], 0), axis=1), seq_count
    )
    begins = jnp.where(
        live_rows, jnp.sum(jnp.where(inside, starts[None, :], 0), axis=1), filled_rows
    )
    return (live_rows, segment, row_slots - begins)


def rope_tables(position):
    half = HEAD_WIDTH // 2
    lanes = jnp.arange(2 * HEAD_WIDTH, dtype=jnp.int32)
    exponent = (lanes % half).astype(F32) * 2.0 / HEAD_WIDTH
    angles = position.astype(F32)[:, None] * (ROPE_BASE ** (-exponent))[None, :]
    sign = jnp.where(lanes % HEAD_WIDTH < half, -1.0, 1.0)
    return jnp.cos(angles), jnp.sin(angles) * sign[None, :]


def permute(value, perm):
    return lax.ppermute(value, "fsdp", perm)


def swap_perm(mask, count=32):
    return [(i, i ^ mask) for i in range(count)]


def first_perm():
    return [(i, i ^ (4 if i % 2 == 0 else 2)) for i in range(32)]


def second_perm():
    return [(i, i ^ (2 if i % 2 == 0 else 4)) for i in range(32)]


def parity_groups(count):
    return [list(range(0, count, 2)), list(range(1, count, 2))]


def peer_plan(device, count):
    if count != 32:
        return [device % 2 + 2 * i for i in range(count // 2)]
    core = device % 2
    first = jnp.where(core == 0, 4, 2)
    second = 6 - first
    return [device ^ (8 * z) ^ step for z in range(4) for step in (0, first, second, 6)]


def behind(value, *others):
    return lax.optimization_barrier((value,) + others)[0] if others else value


STEPS = {
    "z1": ("", swap_perm(8)),
    "z2": ("", swap_perm(16)),
    "z3": ("z2", swap_perm(8)),
    "first0": ("", first_perm()),
    "second0": ("", second_perm()),
    "across0": ("first0", second_perm()),
    "first1": ("first0", swap_perm(8)),
    "second1": ("z1", second_perm()),
    "across1": ("across0", swap_perm(8)),
    "first2": ("z2", first_perm()),
    "second2": ("z2", second_perm()),
    "across2": ("first2", second_perm()),
    "first3": ("z3", first_perm()),
    "second3": ("z3", second_perm()),
    "across3": ("first3", second_perm()),
}
class Graph:
    def __init__(self, gates):
        self.gates, self.steps, self.have = gates, {}, {}

    def put(self, name, function, *needs):
        self.steps[name] = (function, needs)

    def get(self, name):
        if name not in self.have:
            self.have[name] = None
            function, needs = self.steps[name]
            values = [self.get(n) for n in needs]
            gates = [jax.tree.leaves(self.get(g))[0] for g in self.gates.get(name, ())]
            if gates and values:
                values[0] = jax.tree.map(lambda v: behind(v, *gates), values[0])
            with jax.named_scope(name.replace(" ", "_")):
                self.have[name] = function(*values)
        return self.have[name]


def put_permute(graph, name, perm, source, make=None):
    graph.put(name, lambda *v: permute(make(*v) if make else v[0], perm), *([source] if isinstance(source, str) else source))


def put_gather(graph, tag, source):
    for step, (base, perm) in STEPS.items():
        put_permute(graph, tag + step, perm, tag + base if base else source)


def gathered(tag, source):
    names = [[base, f"{tag}first{p}", f"{tag}second{p}", f"{tag}across{p}"] for p, base in enumerate((source, tag + "z1", tag + "z2", tag + "z3"))]
    return [n for plane in names for n in plane]


def put_sum(graph, tag, terms):
    own, one, two, three = [terms[4 * p : 4 * (p + 1)] for p in range(4)]
    for p, plane in ((2, two), (3, three)):
        put_permute(graph, f"{tag}a{p}", second_perm(), plane[3])
        put_permute(graph, f"{tag}b{p}", second_perm(), plane[2])
        put_permute(graph, f"{tag}c{p}", first_perm(), (plane[1], f"{tag}a{p}"), add_round)
    put_permute(graph, f"{tag}z3", swap_perm(8), (three[0], f"{tag}b3", f"{tag}c3"), add_round)
    put_permute(graph, f"{tag}z2", swap_perm(16), (two[0], f"{tag}b2", f"{tag}c2", f"{tag}z3"), add_round)
    put_permute(graph, f"{tag}b1", second_perm(), one[2])
    put_permute(graph, f"{tag}f1", swap_perm(8), one[1])
    put_permute(graph, f"{tag}d1", swap_perm(8), one[3])
    put_permute(graph, f"{tag}z1", swap_perm(8), (one[0], f"{tag}b1"), add_round)
    put_permute(graph, f"{tag}a0", second_perm(), (own[3], f"{tag}d1"), add_round)
    put_permute(graph, f"{tag}b0", second_perm(), own[2])
    put_permute(graph, f"{tag}c0", first_perm(), (own[1], f"{tag}f1", f"{tag}a0"), add_round)
    return [own[0]] + [f"{tag}{n}" for n in ("c0", "b0", "z1", "z2")]


def gather_whole(shard, count):
    whole = lax.all_gather(shard, "fsdp", axis=0, axis_index_groups=parity_groups(count))
    return [whole[i] for i in range(count // 2)]


def add_wide(*terms):
    return sum(t.astype(F32) for t in terms)


def add_round(*terms):
    return add_wide(*terms).astype(BF)


def sum_whole(terms, count):
    stacked = jnp.concatenate([t.astype(F32) for t in terms], axis=0)
    return [
        lax.psum_scatter(
            stacked, "fsdp", scatter_dimension=0, tiled=True, axis_index_groups=parity_groups(count)
        )
    ]


def filled_rows(device, lengths, devices):
    return lax.fori_loop(
        0,
        lengths.shape[0],
        lambda i, rows: rows + jnp.where(devices[i] == device[0], lengths[i], 0),
        jnp.int32(0),
    )


def pack_kernel(with_weights, device, lengths, devices, ids, out_grad, *refs):
    packed = refs[-1]
    if with_weights:
        query, keyvalue, output, router, attn_gain, moe_gain = refs[:-1]
        square = jnp.zeros((128, 128), F32)
        row = lax.broadcasted_iota(jnp.int32, (128, 128), 0)
        for i, gain in enumerate((attn_gain, moe_gain)):
            wide = jnp.concatenate(
                [gain[...].astype(F32).reshape(1, PART), jnp.zeros((1, 128 - PART), F32)], axis=1
            )
            square = jnp.where(row == EXPERT_COUNT + i, wide, square)
        small = square.T[:PART]
        small = small + jnp.concatenate(
            [router[...].astype(F32), jnp.zeros((PART, 128 - EXPERT_COUNT), F32)], axis=1
        )
        small = small.astype(BF)
        packed[0:PART, :] = query[...]
        packed[PART : 2 * PART, :] = keyvalue[...]
        packed[2 * PART : 3 * PART, :] = output[...]
        packed[3 * PART : PACK, :] = jnp.zeros((EXTRA, MODEL), BF)
        packed[3 * PART : PACK, 0:128] = small[0:EXTRA, :]
        packed[3 * PART : PACK, 128:256] = small[EXTRA:, :]
    else:
        packed[0:EXTRA, :] = jnp.zeros((EXTRA, MODEL), BF)
    filled = filled_rows(device, lengths, devices)
    first = PACK if with_weights else EXTRA
    rows = lax.broadcasted_iota(jnp.int32, (ROWS, MODEL), 0)
    packed[first : first + ROWS, :] = jnp.where(
        rows < filled, out_grad[...].astype(F32), 0.0
    ).astype(BF)
    wide = ids[...].astype(F32)
    expert = lax.broadcasted_iota(jnp.int32, (EXPERT_COUNT, ROWS), 0).astype(F32)
    hit = jnp.zeros((EXPERT_COUNT, ROWS), F32)
    for k in range(TOPK):
        hit = hit + jnp.where(expert == wide[k : k + 1, :], 1.0, 0.0)
    row = lax.broadcasted_iota(jnp.int32, (ROWS, ROWS), 0)
    column = lax.broadcasted_iota(jnp.int32, (ROWS, ROWS), 1)
    before = jnp.where(row < column, 1.0, 0.0).astype(BF)
    rank = row_by_col(hit.astype(BF), before)
    table = jnp.where(hit > 0.0, rank, float(NOT_CHOSEN)).astype(BF)
    packed[first - EXTRA : first, 256:384] = table[:EXTRA]
    packed[first - EXTRA : first, 384:512] = table[EXTRA:]


def join_kernel(rows, *refs):
    parts, out, sems = refs[:-2], refs[-2], refs[-1]
    copies = [
        pltpu.make_async_copy(part.at[pl.ds(0, rows)], out.at[pl.ds(rows * i, rows)], sems.at[i])
        for i, part in enumerate(parts)
    ]
    for copy in copies:
        copy.start()
    for copy in copies:
        copy.wait()


def start_weights(place, buffers, weights, sems, first, last):
    copies = []
    for buffer in buffers:
        for j in range(buffer.shape[0] // PACK if buffer.shape[0] != WHOLE else 1):
            i = len(copies)
            copies.append(
                pltpu.make_async_copy(
                    buffer.at[pl.ds(j * PACK + first, last - first)], weights.at[place[i]], sems.at[i]
                )
            )
            copies[-1].start()
    return copies


def half_swap(chunk):
    lane = lax.broadcasted_iota(jnp.int32, chunk.shape, 1)
    half = HEAD_WIDTH // 2
    return jnp.where(
        lane % HEAD_WIDTH < half, pltpu.roll(chunk, 128 - half, 1), pltpu.roll(chunk, half, 1)
    )


def doubled(chunk, second):
    lane = lax.broadcasted_iota(jnp.int32, chunk.shape, 1)
    turned = pltpu.roll(chunk, HEAD_WIDTH, 1)
    keep = lane >= HEAD_WIDTH if second else lane < HEAD_WIDTH
    return jnp.where(keep, chunk, turned)


def split_pair(chunk):
    lane = lax.broadcasted_iota(jnp.int32, chunk.shape, 1)
    zero = jnp.zeros_like(chunk)
    return jnp.concatenate(
        [jnp.where(lane < HEAD_WIDTH, chunk, zero), jnp.where(lane < HEAD_WIDTH, zero, chunk)], axis=0
    )


def join_pair(stacked):
    lane = lax.broadcasted_iota(jnp.int32, (ROWS, 128), 1)
    return jnp.where(lane < HEAD_WIDTH, stacked[:ROWS], stacked[ROWS:])


def attention_kernel(buffers_count, *refs):
    place, buffers, refs = refs[0], refs[1 : 1 + buffers_count], refs[1 + buffers_count :]
    x_ref, cos_ref, sin_ref, allowed_ref = refs[:4]
    moe_ref, resid_ref, share_ref, query_ref, kv_ref, probs_ref, small_ref = refs[4:11]
    weights, columns, sems = refs[11:]
    copies = start_weights(place, buffers, weights, sems, 0, PACK)
    x = x_ref[...].astype(F32)
    unit = x * lax.rsqrt(jnp.mean(x * x, axis=-1, keepdims=True) + EPS)
    for copy in copies:
        copy.wait()
    for p in range(BLOCKS):
        for j in range(2):
            columns[pl.ds(p * PART + j * EXTRA, EXTRA), :] = weights[
                p, 3 * PART :, 128 * j : 128 * (j + 1)
            ].astype(F32)
    small = columns[...].T
    small_ref[...] = small.astype(BF)
    attn_in = (unit * small[EXPERT_COUNT : EXPERT_COUNT + 1, :]).astype(BF)
    share_ref[:ROWS, :] = attn_in
    cosine, sine = cos_ref[...], sin_ref[...]

    def weight_columns(which, chunk):
        lanes = slice(256 * chunk, 256 * (chunk + 1))
        return weights[:, PART * which : PART * (which + 1), lanes].reshape(MODEL, 256)

    for chunk in range(4):
        query_pre = row_by_col(attn_in, weight_columns(0, chunk))
        kv_pre = row_by_col(attn_in, weight_columns(1, chunk))
        for j in range(2):
            at = slice(256 * chunk + 128 * j, 256 * chunk + 128 * (j + 1))
            part = query_pre[:, 128 * j : 128 * (j + 1)]
            query_ref[:, at] = (part * cosine + half_swap(part) * sine).astype(BF)
            part = kv_pre[:, 128 * j : 128 * (j + 1)]
            if chunk < 2:
                part = part * cosine + half_swap(part) * sine
            kv_ref[:, at] = part.astype(BF)
    allowed = jnp.concatenate([allowed_ref[...], allowed_ref[...]], axis=0) > 0.0
    scale = HEAD_WIDTH ** (-0.5)
    for head in range(KEY_VALUE_HEADS):
        pair, second = head // 2, head % 2 == 1
        key = doubled(kv_ref[:, 128 * pair : 128 * (pair + 1)].astype(F32), second).astype(BF)
        value = doubled(
            kv_ref[:, 512 + 128 * pair : 512 + 128 * (pair + 1)].astype(F32), second
        ).astype(BF)
        at = slice(128 * head, 128 * (head + 1))
        scores = row_by_row(split_pair(query_ref[:, at]), key) * scale
        scores = jnp.where(allowed, scores, -jnp.inf)
        raised = jnp.exp(scores - jnp.max(scores, axis=-1, keepdims=True))
        probs = raised / jnp.sum(raised, axis=-1, keepdims=True)
        probs_ref[head] = probs
        share_ref[ROWS:, at] = join_pair(row_by_col(probs.astype(BF), value)).astype(BF)
    heads = share_ref[ROWS:, :]
    for chunk in range(4):
        at = slice(256 * chunk, 256 * (chunk + 1))
        resid_ref[:, at] = x_ref[:, at].astype(F32) + row_by_col(heads, weight_columns(2, chunk))
    residual = resid_ref[...]
    unit = residual * lax.rsqrt(jnp.mean(residual * residual, axis=-1, keepdims=True) + EPS)
    moe_ref[...] = (unit * small[EXPERT_COUNT + 1 : EXPERT_COUNT + 2, :]).astype(BF)


def route_table(extra):
    return jnp.concatenate([extra[:, 0:128], extra[:, 128:256]], axis=0).astype(F32)


def route_weights_of(table, small, rows):
    logits = row_by_row(small, rows)[:EXPERT_COUNT]
    raised = jnp.where(table < NOT_CHOSEN, jnp.exp(logits), 0.0)
    return raised / jnp.sum(raised, axis=0, keepdims=True)


def expert_kernel(sizes, *refs):
    x_sizes, c_first = sizes
    names, refs = refs[0], refs[1:]
    x_hbm, refs = refs[: len(x_sizes)], refs[len(x_sizes) :]
    c_hbm, refs = refs[:8], refs[8:]
    small_ref, tables_hbm, refs = refs[0], refs[1:7], refs[7:]
    p_hbm, g_hbm, saved_hbm, refs = refs[:4], refs[4:12], refs[12:22], refs[22:]
    xs_all, cs_all, tables, ps, gs, saved_wide, saved_thin, picks, cots, results, back, in_sems, out_sems = refs
    copies = []

    def fetch(source, target):
        copies.append(pltpu.make_async_copy(source, target, in_sems.at[len(copies)]))
        copies[-1].start()

    def send(source, target, number):
        copy = pltpu.make_async_copy(source, target, out_sems.at[number])
        copy.start()
        return copy

    at = 0
    for ref, size in zip(x_hbm, x_sizes):
        for j in range(size):
            fetch(ref.at[pl.ds(ROWS * j, ROWS)], xs_all.at[at])
            at += 1
    for i, ref in enumerate(c_hbm):
        fetch(ref.at[pl.ds(c_first, WIDE)], cs_all.at[i])
    for i, ref in enumerate(tables_hbm):
        fetch(ref, tables.at[i])
    slots = 4 * CAP
    small = small_ref[...]
    expert_row = lax.broadcasted_iota(jnp.int32, (EXPERT_COUNT, ROWS), 0)
    slot_row = lax.broadcasted_iota(jnp.int32, (slots, 4 * ROWS), 0).astype(F32)
    slot_weights = [[None, None], [None, None]]
    for copy in copies[:16]:
        copy.wait()
    for h in range(2):
        places, weights = [[], []], [[], []]
        for b in range(4):
            table = route_table(cs_all[4 * h + b, :EXTRA, 256:512])
            weight = route_weights_of(table, small, xs_all[4 * h + b])
            for l in range(2):
                here = expert_row == names[l]
                place = jnp.sum(jnp.where(here, table, 0.0), axis=0, keepdims=True)
                places[l].append(jnp.where(place < NOT_CHOSEN, place + b * CAP, 4096.0))
                weights[l].append(jnp.sum(jnp.where(here, weight, 0.0), axis=0, keepdims=True))
        for l in range(2):
            chosen = slot_row == jnp.concatenate(places[l], axis=1)
            weight = jnp.concatenate(weights[l], axis=1)
            slot_weights[l][h] = jnp.sum(jnp.where(chosen, weight, 0.0), axis=1, keepdims=True)
            picks[h, slots * l : slots * (l + 1), :] = chosen.astype(F32).astype(BF)
        pick = picks[h]
        rows = xs_all[4 * h : 4 * (h + 1)].reshape(4 * ROWS, MODEL)
        cot_rows = cs_all[4 * h : 4 * (h + 1), EXTRA:, :].reshape(4 * ROWS, MODEL)
        inputs = row_by_col(pick, rows).astype(BF)
        cot = row_by_col(pick, cot_rows).astype(BF)
        for l in range(2):
            saved_wide[2 * l, slots * h : slots * (h + 1), :] = inputs[slots * l : slots * (l + 1)]
            cots[l, slots * h : slots * (h + 1), :] = cot[slots * l : slots * (l + 1)]
    slot_routes, sends = [], []
    for l in range(2):
        gate, up, down = tables.at[3 * l], tables.at[3 * l + 1], tables.at[3 * l + 2]
        for copy in copies[16 + 3 * l : 19 + 3 * l]:
            copy.wait()
        weight = jnp.concatenate(slot_weights[l], axis=0)
        inputs = saved_wide[2 * l]
        gate_pre = row_by_row(inputs, gate[...])
        up_pre = row_by_row(inputs, up[...])
        sigma = jax.nn.sigmoid(gate_pre)
        acts = (gate_pre * sigma * up_pre).astype(BF)
        saved_thin[3 * l] = acts
        cot = cots[l].astype(F32)
        result = row_by_col(acts, down[...])
        slot_routes.append(jnp.sum(cot * result, axis=1, keepdims=True))
        results[l] = (weight * result).astype(BF)
        pair_cot = (weight * cot).astype(BF)
        saved_wide[2 * l + 1] = pair_cot
        act_grad = row_by_row(pair_cot, down[...])
        gate_grad = (act_grad * up_pre * sigma * (1.0 + gate_pre * (1.0 - sigma))).astype(BF)
        up_grad = (act_grad * gate_pre * sigma).astype(BF)
        saved_thin[3 * l + 1] = gate_grad
        saved_thin[3 * l + 2] = up_grad
        back[l] = (row_by_col(gate_grad, gate[...]) + row_by_col(up_grad, up[...])).astype(BF)
        for i in range(5):
            source = saved_wide.at[2 * l + i] if i < 2 else saved_thin.at[3 * l + i - 2]
            sends.append(send(source, saved_hbm[5 * l + i], 16 + 5 * l + i))
    for h in range(2):
        pick = picks[h]
        at = slice(slots * h, slots * (h + 1))
        grad = col_by_col(pick, jnp.concatenate([back[0, at], back[1, at]], axis=0)).astype(BF)
        routes = []
        for l in range(2):
            chosen = pick[slots * l : slots * (l + 1)].astype(F32)
            routes.append(jnp.sum(chosen * slot_routes[l][at], axis=0, keepdims=True))
        for b in range(4):
            i = 4 * h + b
            rows = slice(ROWS * b, ROWS * (b + 1))
            gs[i, :ROWS, :] = grad[rows]
            route = jnp.zeros((EXPERT_COUNT, ROWS), F32)
            for l in range(2):
                route = route + jnp.where(expert_row == names[l], routes[l][:, rows], 0.0)
            high = route.astype(BF)
            low = (route - high.astype(F32)).astype(BF)
            gs[i, ROWS:, 0:128] = high[:16]
            gs[i, ROWS:, 128:256] = high[16:]
            gs[i, ROWS:, 256:384] = low[:16]
            gs[i, ROWS:, 384:512] = low[16:]
            gs[i, ROWS:, 512:] = jnp.zeros((EXTRA, MODEL - 512), BF)
            sends.append(send(gs.at[i], g_hbm[i], 8 + i))
        out = col_by_col(pick, jnp.concatenate([results[0, at], results[1, at]], axis=0)).astype(BF)
        for b in range(4):
            i = 4 * h + b
            ps[i] = out[ROWS * b : ROWS * (b + 1)]
            sends.append(send(ps.at[i], p_hbm[i % 4].at[pl.ds(ROWS * (i // 4), ROWS)], i))
    for copy in sends:
        copy.wait()


def weight_grad_kernel(calls, added, *refs):
    saved, refs = refs[: 5 * calls], refs[5 * calls :]
    received, refs = refs[:added], refs[added:]
    outs, refs = refs[: 3 if added else 1], refs[3 if added else 1 :]
    wide, thin, extra, sums, in_sems, out_sems = refs
    hidden = thin.shape[2]
    copies = {}

    def fetch(name, source, target):
        copies[name] = pltpu.make_async_copy(source, target, in_sems.at[len(copies)])
        copies[name].start()

    order = ((3, 0), (4, 0), (2, 1))
    for o, pair in enumerate(order):
        for c in range(calls):
            for i in pair:
                if (c, i) not in copies:
                    target = wide.at[2 * c + i] if i < 2 else thin.at[3 * c + i - 2]
                    fetch((c, i), saved[5 * c + i], target)
        if added:
            fetch(o, received[0].at[pl.ds(hidden * o, hidden)], extra.at[o])
    waited, sends = set(), []
    for o, (left, right) in enumerate(order):
        total = None
        for c in range(calls):
            for i in (left, right):
                if (c, i) not in waited:
                    waited.add((c, i))
                    copies[c, i].wait()
            term = col_by_col(thin[3 * c + left - 2], wide[2 * c + right])
            total = term if total is None else total + term
        if added:
            copies[o].wait()
            total = total + extra[o]
        sums[o] = total
        target = outs[o] if added else outs[0].at[pl.ds(hidden * o, hidden)]
        sends.append(pltpu.make_async_copy(sums.at[o], target, out_sems.at[o]))
        sends[-1].start()
    for copy in sends:
        copy.wait()


def head_backward_kernel(buffers_count, pieces_count, *refs):
    place, buffers, refs = refs[0], refs[1 : 1 + buffers_count], refs[1 + buffers_count :]
    pieces, refs = refs[:pieces_count], refs[pieces_count:]
    moe_ref, resid_ref, cot_ref, small_ref, share_ref, query_ref, kv_ref, probs_ref = refs[:8]
    cos_ref, sin_ref = refs[8:10]
    resid_grad_ref, grads_ref = refs[10:12]
    weights, grads, sems = refs[12:]
    copies = start_weights(place, buffers, weights, sems, 2 * PART, 3 * PART)
    small = small_ref[...]
    total = pieces[0][...].astype(F32)
    for piece in pieces[1:]:
        total = total + piece[...].astype(F32)
    extra = total[ROWS:]
    route_grad = jnp.concatenate(
        [extra[:, 0:128] + extra[:, 256:384], extra[:, 128:256] + extra[:, 384:512]], axis=0
    )
    moe_in = moe_ref[...]
    first = cot_ref.shape[0] - WIDE
    table = route_table(cot_ref[first : first + EXTRA, 256:512])
    weight = route_weights_of(table, small, moe_in)
    logit_grad = weight * (route_grad - jnp.sum(weight * route_grad, axis=0, keepdims=True))
    logit_grad = jnp.concatenate(
        [logit_grad, jnp.zeros((ROWS - EXPERT_COUNT, ROWS), F32)], axis=0
    ).astype(BF)
    moe_in_grad = total[:ROWS] + col_by_col(logit_grad, small)
    router_grad = row_by_col(logit_grad, moe_in)[:SMALL]
    residual = resid_ref[...]
    inverse = lax.rsqrt(jnp.mean(residual * residual, axis=-1, keepdims=True) + EPS)
    unit = residual * inverse
    moe_gain_grad = jnp.sum(moe_in_grad * unit, axis=0, keepdims=True)
    row = lax.broadcasted_iota(jnp.int32, (SMALL, MODEL), 0)
    grads_ref[3 * ROWS :, :] = jnp.where(row == EXPERT_COUNT + 1, moe_gain_grad, router_grad).astype(BF)
    grad_unit = moe_in_grad * small[EXPERT_COUNT : EXPERT_COUNT + 8].astype(F32)[1:2]
    mean = jnp.mean(grad_unit * unit, axis=-1, keepdims=True)
    cot = cot_ref[first + EXTRA :, :]
    residual_grad = cot.astype(F32) + inverse * (grad_unit - unit * mean)
    resid_grad_ref[...] = residual_grad
    residual_bf = residual_grad.astype(BF)
    grads_ref[:ROWS, :] = residual_bf
    for copy in copies:
        copy.wait()
    for chunk in range(4):
        at = slice(256 * chunk, 256 * (chunk + 1))
        rows = weights[8 * chunk : 8 * (chunk + 1)].reshape(256, MODEL)
        grads[:, at] = row_by_row(residual_bf, rows).astype(BF)
    cosine, sine = cos_ref[...], sin_ref[...]
    scale = HEAD_WIDTH ** (-0.5)
    key_grads, value_grads = [], []
    for head in range(KEY_VALUE_HEADS):
        pair, second = head // 2, head % 2 == 1
        key = doubled(kv_ref[:, 128 * pair : 128 * (pair + 1)].astype(F32), second).astype(BF)
        value = doubled(
            kv_ref[:, 512 + 128 * pair : 512 + 128 * (pair + 1)].astype(F32), second
        ).astype(BF)
        at = slice(128 * head, 128 * (head + 1))
        query = split_pair(query_ref[:, at])
        head_grad = split_pair(grads[:, at])
        mixed = split_pair(share_ref[ROWS:, at])
        inner = jnp.sum(head_grad.astype(F32) * mixed.astype(F32), axis=-1, keepdims=True)
        probs = probs_ref[head]
        score_grad = (probs * (row_by_row(head_grad, value) - inner)).astype(BF)
        part = join_pair(row_by_col(score_grad, key)) * scale
        grads_ref[ROWS : 2 * ROWS, at] = (part * cosine - half_swap(part) * sine).astype(BF)
        part = col_by_col(score_grad, query) * scale
        key_grads.append(part + pltpu.roll(part, HEAD_WIDTH, 1))
        part = col_by_col(probs.astype(BF), head_grad)
        value_grads.append(part + pltpu.roll(part, HEAD_WIDTH, 1))
    lane = lax.broadcasted_iota(jnp.int32, (ROWS, 128), 1)
    for which, parts in enumerate((key_grads, value_grads)):
        for pair in range(KEY_VALUE_HEADS // 2):
            part = jnp.where(lane < HEAD_WIDTH, parts[2 * pair], parts[2 * pair + 1])
            if which == 0:
                part = part * cosine - half_swap(part) * sine
            at = slice(512 * which + 128 * pair, 512 * which + 128 * (pair + 1))
            grads_ref[2 * ROWS : 3 * ROWS, at] = part.astype(BF)


def input_grad_kernel(buffers_count, place, device, lengths, devices, *refs):
    buffers, refs = refs[:buffers_count], refs[buffers_count:]
    grads_ref, resid_grad_ref, small_ref, x_ref, in_ref = refs[:5]
    weights, sems = refs[5:]
    copies = start_weights(place, buffers, weights, sems, 0, 2 * PART)
    x = x_ref[...].astype(F32)
    inverse = lax.rsqrt(jnp.mean(x * x, axis=-1, keepdims=True) + EPS)
    unit = x * inverse
    query_grad, kv_grad = grads_ref[ROWS : 2 * ROWS, :], grads_ref[2 * ROWS : 3 * ROWS, :]
    for copy in copies:
        copy.wait()
    back = []
    for chunk in range(4):
        rows = weights[8 * chunk : 8 * (chunk + 1)]
        back.append(
            row_by_row(query_grad, rows[:, :PART].reshape(256, MODEL))
            + row_by_row(kv_grad, rows[:, PART:].reshape(256, MODEL))
        )
    attn_in_grad = jnp.concatenate(back, axis=1)
    grad_unit = attn_in_grad * small_ref[EXPERT_COUNT : EXPERT_COUNT + 8].astype(F32)[0:1]
    mean = jnp.mean(grad_unit * unit, axis=-1, keepdims=True)
    input_grad = resid_grad_ref[...] + inverse * (grad_unit - unit * mean)
    rows = lax.broadcasted_iota(jnp.int32, (ROWS, MODEL), 0)
    in_ref[...] = jnp.where(rows < filled_rows(device, lengths, devices), input_grad, 0.0)


def dense_grad_kernel(parties, blocks, *refs):
    place, refs = refs[0], refs[1:]
    results = refs[2 * parties : -blocks - 2]
    refs = refs[: 2 * parties] + refs[-blocks - 2 :]
    sems = refs[-1]
    shares, grads, refs = refs[:parties], refs[parties : 2 * parties], refs[2 * parties :]
    outs, terms = refs[:blocks], refs[blocks]
    copies = []
    for i in range(4 * len(results) // 2 if results else 0):
        source = results[4 * (i // 8) + i % 4].at[pl.ds(ROWS * (i // 4 % 2), ROWS)]
        copies.append(pltpu.make_async_copy(source, outs[i].at[pl.ds(PACK, ROWS)], sems.at[i]))
        copies[-1].start()
    attn_in = jnp.concatenate([r[:ROWS, :] for r in shares], axis=0)
    heads = jnp.concatenate([r[ROWS:, :] for r in shares], axis=0)
    residual, query, keyvalue = [
        jnp.concatenate([r[ROWS * i : ROWS * (i + 1), :] for r in grads], axis=0) for i in range(3)
    ]
    for chunk in range(4):
        at = slice(256 * chunk, 256 * (chunk + 1))
        for which, left, right in ((0, attn_in, query), (1, attn_in, keyvalue), (2, heads, residual)):
            term = col_by_col(left[:, at], right).astype(BF).reshape(8, PART, MODEL)
            terms[8 * chunk : 8 * (chunk + 1), PART * which : PART * (which + 1), :] = term
    columns = sum(r[3 * ROWS :, :].astype(F32) for r in grads)
    columns = jnp.concatenate([columns, jnp.zeros((128 - SMALL, MODEL), F32)], axis=0).T.astype(BF)
    for p in range(BLOCKS):
        for j in range(2):
            terms[p, 3 * PART :, 128 * j : 128 * (j + 1)] = columns[
                p * PART + j * EXTRA : p * PART + (j + 1) * EXTRA
            ]
        terms[p, 3 * PART :, 256:] = jnp.zeros((EXTRA, MODEL - 256), BF)
    for i in range(blocks):
        outs[i][:PACK, :] = terms[place[i]]
    for copy in copies:
        copy.wait()


def params():
    return pltpu.CompilerParams(vmem_limit_bytes=VMEM_LIMIT)


def shape(dims, dtype):
    return jax.ShapeDtypeStruct(dims, dtype)


def spec(space):
    return pl.BlockSpec(memory_space=space)


def pack_call(sequences, expert_ids, output_grad, *weights):
    smem, vmem = spec(pltpu.SMEM), spec(pltpu.VMEM)
    return pl.pallas_call(
        partial(pack_kernel, bool(weights)),
        out_shape=shape((WHOLE if weights else WIDE, MODEL), BF),
        in_specs=[smem] * 3 + [vmem] * (2 + len(weights)),
        out_specs=vmem,
        compiler_params=params(),
    )(*sequences, expert_ids.T, output_grad, *weights)


def join_call(rows, *parts):
    anywhere = spec(pl.ANY)
    return pl.pallas_call(
        partial(join_kernel, rows),
        out_shape=shape((rows * len(parts), MODEL), BF),
        in_specs=[anywhere] * len(parts),
        out_specs=spec(pltpu.VMEM),
        scratch_shapes=[pltpu.SemaphoreType.DMA((len(parts),))],
        compiler_params=params(),
    )(*parts)


def attention_call(place, block_input, cosine, sine, allowed, *dense):
    vmem = spec(pltpu.VMEM)
    return pl.pallas_call(
        partial(attention_kernel, len(dense)),
        out_shape=(
            shape((ROWS, MODEL), BF),
            shape((ROWS, MODEL), F32),
            shape((2 * ROWS, MODEL), BF),
            shape((ROWS, MODEL), BF),
            shape((ROWS, MODEL), BF),
            shape((KEY_VALUE_HEADS, 2 * ROWS, ROWS), F32),
            shape((128, MODEL), BF),
        ),
        in_specs=[spec(pltpu.SMEM)] + [spec(pl.ANY)] * len(dense) + [vmem] * 4,
        out_specs=(vmem,) * 7,
        scratch_shapes=[
            pltpu.VMEM((BLOCKS, PACK, MODEL), BF),
            pltpu.VMEM((MODEL, 128), F32),
            pltpu.SemaphoreType.DMA((BLOCKS,)),
        ],
        compiler_params=params(),
    )(place, *dense, block_input, cosine, sine, allowed)


def expert_call(first, small, tables, names, *rows_and_cots):
    hidden, slots = tables[0].shape[0], 8 * CAP
    anywhere = spec(pl.ANY)
    got = pl.pallas_call(
        partial(expert_kernel, ((1,) * 8, first)),
        out_shape=(shape((2 * ROWS, MODEL), BF),) * 4
        + (shape((WIDE, MODEL), BF),) * 8
        + ((shape((slots, MODEL), BF),) * 2 + (shape((slots, hidden), BF),) * 3) * 2,
        in_specs=[spec(pltpu.SMEM)] + [anywhere] * 16 + [spec(pltpu.VMEM)] + [anywhere] * 6,
        out_specs=(anywhere,) * 22,
        scratch_shapes=[
            pltpu.VMEM((8, ROWS, MODEL), BF),
            pltpu.VMEM((8, WIDE, MODEL), BF),
            pltpu.VMEM((6, hidden, MODEL), BF),
            pltpu.VMEM((8, ROWS, MODEL), BF),
            pltpu.VMEM((8, WIDE, MODEL), BF),
            pltpu.VMEM((4, slots, MODEL), BF),
            pltpu.VMEM((6, slots, hidden), BF),
            pltpu.VMEM((2, slots, 4 * ROWS), BF),
            pltpu.VMEM((2, slots, MODEL), BF),
            pltpu.VMEM((2, slots, MODEL), BF),
            pltpu.VMEM((2, slots, MODEL), BF),
            pltpu.SemaphoreType.DMA((22,)),
            pltpu.SemaphoreType.DMA((26,)),
        ],
        compiler_params=params(),
    )(names, *rows_and_cots, small, *tables)
    return got[:4], got[4:12], got[12:17], got[17:]


def weight_grad_call(calls, *added):
    saves = [v for saved in calls for v in saved]
    hidden, slots = saves[2].shape[1], saves[2].shape[0]
    table = shape((hidden, MODEL), F32)
    anywhere = spec(pl.ANY)
    number = len(calls)
    return pl.pallas_call(
        partial(weight_grad_kernel, number, len(added)),
        out_shape=(table,) * 3 if added else shape((3 * hidden, MODEL), F32),
        in_specs=[anywhere] * (len(saves) + len(added)),
        out_specs=(anywhere,) * 3 if added else anywhere,
        scratch_shapes=[
            pltpu.VMEM((2 * number, slots, MODEL), BF),
            pltpu.VMEM((3 * number, slots, hidden), BF),
            pltpu.VMEM((3, hidden, MODEL), F32),
            pltpu.VMEM((3, hidden, MODEL), F32),
            pltpu.SemaphoreType.DMA((5 * number + 3,)),
            pltpu.SemaphoreType.DMA((3,)),
        ],
        compiler_params=params(),
    )(*saves, *added)


def head_backward_call(place, dense, pieces, others):
    vmem = spec(pltpu.VMEM)
    return pl.pallas_call(
        partial(head_backward_kernel, len(dense), len(pieces)),
        out_shape=(shape((ROWS, MODEL), F32), shape((3 * ROWS + SMALL, MODEL), BF)),
        in_specs=[spec(pltpu.SMEM)] + [spec(pl.ANY)] * len(dense) + [vmem] * (len(pieces) + 10),
        out_specs=(vmem,) * 2,
        scratch_shapes=[
            pltpu.VMEM((BLOCKS, PART, MODEL), BF),
            pltpu.VMEM((ROWS, MODEL), BF),
            pltpu.SemaphoreType.DMA((BLOCKS,)),
        ],
        compiler_params=params(),
    )(place, *dense, *pieces, *others)


def dense_grad_call(blocks, place, parties, results=()):
    vmem = spec(pltpu.VMEM)
    rows = PACK + ROWS if results else PACK
    return pl.pallas_call(
        partial(dense_grad_kernel, len(parties) // 2, blocks),
        out_shape=(shape((rows, MODEL), BF),) * blocks,
        in_specs=[spec(pltpu.SMEM)] + [vmem] * len(parties) + [spec(pl.ANY)] * len(results),
        out_specs=(vmem,) * blocks,
        scratch_shapes=[
            pltpu.VMEM((BLOCKS, PACK, MODEL), BF),
            pltpu.SemaphoreType.DMA((BLOCKS // 2,)),
        ],
        compiler_params=params(),
    )(place, *parties, *results)


def input_grad_call(place, sequences, dense, *others):
    smem, vmem = spec(pltpu.SMEM), spec(pltpu.VMEM)
    return pl.pallas_call(
        partial(input_grad_kernel, len(dense)),
        out_shape=shape((ROWS, MODEL), F32),
        in_specs=[smem] * 4 + [spec(pl.ANY)] * len(dense) + [vmem] * 4,
        out_specs=vmem,
        scratch_shapes=[
            pltpu.VMEM((BLOCKS, 2 * PART, MODEL), BF),
            pltpu.SemaphoreType.DMA((BLOCKS,)),
        ],
        compiler_params=params(),
    )(place, *sequences, *dense, *others)


def attention_inputs(seq_lengths, seq_devices, device):
    live_rows, segment, position = layout(seq_lengths, seq_devices, device, ROWS)
    row_slots = jnp.arange(ROWS, dtype=jnp.int32)
    allowed = (segment[:, None] == segment[None, :]) & (row_slots[:, None] >= row_slots[None, :])
    return live_rows, (*rope_tables(position), allowed.astype(F32))


def finish(live_rows, residual, out_pieces, gain, weights, grads):
    block_output = jnp.where(live_rows[:, None], add_wide(residual, *out_pieces), 0.0).astype(BF)
    weighted = sum(w.astype(F32) * g for w, g in zip(weights, grads))
    return block_output, jnp.sum(weighted, axis=1) / gain.astype(F32)


def small_columns(rows):
    return jnp.concatenate([rows[..., 0:128], rows[..., 128:256]], axis=-2)


def graph_on_slice(device, inputs):
    (block_input, seq_lengths, seq_devices, expert_ids, attn_gain, query_weight, keyvalue_weight,
     output_weight, moe_gain, router_weight, gate_weight, up_weight, down_weight, output_grad) = inputs
    own_tables = (gate_weight, up_weight, down_weight)
    sequences = (device.reshape(1), seq_lengths, seq_devices)
    names = jnp.stack([device, device ^ 1])
    graph = Graph(GATES)
    put = graph.put

    weights = (query_weight, keyvalue_weight, output_weight, router_weight, attn_gain, moe_gain)
    put("packed", lambda: pack_call(sequences, expert_ids, output_grad, *weights))
    put_gather(graph, "d.", "packed")
    cots = gathered("d.", "packed")
    for i, table in enumerate(own_tables):
        put(f"tables {i}", lambda table=table: permute(table, swap_perm(1)))
    early = [n for n in cots if n not in ("d.across1", "d.across2", "d.first3", "d.second3", "d.across3")]
    late = ["d.across1", "d.across2", "d.first3", "d.second3"]
    for name, parts in (("early", early), ("late", late)):
        put("joined " + name, partial(join_call, PACK), *parts)
        put_permute(graph, "sibling " + name, swap_perm(1), "joined " + name)
    put_permute(graph, "sibling last", swap_perm(1), "d.across3")
    dense = cots + ["sibling early", "sibling late", "sibling last"]
    order = cots + early + late + ["d.across3"]
    at = {n: i for i, n in enumerate(cots)}
    plan = peer_plan(device, 32), peer_plan(device ^ 1, 32)
    place = jnp.stack([plan[i // 16][at[n]] for i, n in enumerate(order)])

    put("layout", lambda v: attention_inputs(behind(seq_lengths, v), seq_devices, device), "packed")
    put("attention", lambda l, *v: attention_call(place, block_input, *l[1], *v), "layout", *dense)
    for i, name in enumerate(("moe in", "residual", "share", "query", "keyvalue", "probs", "small")):
        put(name, lambda v, i=i: v[i], "attention")
    put_permute(graph, "share sibling", swap_perm(1), "share")

    put_gather(graph, "m.", "moe in")
    rows = gathered("m.", "moe in")
    for name, at in (("near", slice(0, 8)), ("far", slice(8, 16))):
        put(
            "experts " + name,
            lambda small, *v: expert_call(3 * PART, small, (*own_tables, *v[:3]), names, *v[3:]),
            "small", "tables 0", "tables 1", "tables 2", *rows[at], *cots[at],
        )
        for i in range(4):
            put(f"out {name} {i}", lambda v, i=i: v[0][i], "experts " + name)
        for i in range(8):
            put(f"back {name} {i}", lambda v, i=i: v[1][i], "experts " + name)
    put("sibling grads", lambda a, b: weight_grad_call((a[3], b[3])), "experts near", "experts far")
    put_permute(graph, "received grads", swap_perm(1), "sibling grads")
    put(
        "table grads", lambda r, a, b: weight_grad_call((a[2], b[2]), r),
        "received grads", "experts near", "experts far",
    )

    back_pieces = put_sum(graph, "g.", [f"back {n} {i}" for n in ("near", "far") for i in range(8)])
    others = ["moe in", "residual", "packed", "small", "share", "query", "keyvalue", "probs"]
    put(
        "heads back",
        lambda *v: head_backward_call(place, v[:19], v[19:24], (*v[24:32], *v[32][1][:2])),
        *dense, *back_pieces, *others, "layout",
    )
    put("grads", lambda v: v[1], "heads back")
    put_permute(graph, "grads sibling", swap_perm(1), "grads")
    put(
        "dense grads",
        lambda *v: dense_grad_call(BLOCKS // 2, place, v[:4], v[4:]),
        "share", "share sibling", "grads", "grads sibling",
        *[f"out {name} {i}" for name in ("near", "far") for i in range(4)],
    )
    for i in range(16):
        put(f"term {i}", lambda v, i=i: v[i], "dense grads")
    pieces = put_sum(graph, "s.", [f"term {i}" for i in range(16)])
    put("total", add_wide, *pieces)
    put(
        "input grad",
        lambda h, g, small, *v: input_grad_call(place, sequences, v, g, h[0], small, block_input),
        "heads back", "grads", "small", *dense,
    )

    return graph


def body_on_slice(device, inputs):
    attn_gain, query_weight, keyvalue_weight = inputs[4:7]
    graph = graph_on_slice(device, inputs)
    total = graph.get("total")
    query_grad, keyvalue_grad, output_weight_grad = [total[PART * i : PART * (i + 1)] for i in range(3)]
    small_grad = small_columns(total[3 * PART : PACK])
    block_output, attn_gain_grad = finish(
        graph.get("layout")[0],
        graph.get("residual"),
        (total[PACK:],),
        attn_gain,
        (query_weight, keyvalue_weight),
        (query_grad, keyvalue_grad),
    )
    return (
        block_output,
        graph.get("input grad"),
        attn_gain_grad,
        query_grad,
        keyvalue_grad,
        output_weight_grad,
        small_grad[:, EXPERT_COUNT + 1],
        small_grad[:, :EXPERT_COUNT],
        *graph.get("table grads"),
    )


def body_elsewhere(device, count, inputs):
    (block_input, seq_lengths, seq_devices, expert_ids, attn_gain, query_weight, keyvalue_weight,
     output_weight, moe_gain, router_weight, gate_weight, up_weight, down_weight, output_grad) = inputs
    own_tables = (gate_weight, up_weight, down_weight)
    sequences = (device.reshape(1), seq_lengths, seq_devices)
    hidden = gate_weight.shape[0]
    packed = pack_call(sequences, expert_ids, output_grad)
    small = jnp.concatenate([router_weight, attn_gain[:, None], moe_gain[:, None]], axis=1)
    small = jnp.pad(small, ((0, 0), (0, 128 - small.shape[1])))
    whole = [
        lax.all_gather(w, "fsdp", axis=0, tiled=True)
        for w in (query_weight, keyvalue_weight, output_weight, small)
    ]
    extra = whole[3].reshape(BLOCKS, 2, EXTRA, 128).transpose(0, 2, 1, 3).reshape(BLOCKS, EXTRA, 256)
    extra = jnp.pad(extra, ((0, 0), (0, 0), (0, MODEL - 256)))
    dense = jnp.concatenate([w.reshape(BLOCKS, PART, MODEL) for w in whole[:3]] + [extra], axis=1)
    dense = dense.reshape(BLOCKS * PACK, MODEL)
    place = jnp.arange(BLOCKS, dtype=jnp.int32)
    names = jnp.stack([device, device ^ 1]) * hidden // EXPERT_HIDDEN
    tables = (*own_tables, *(permute(t, swap_perm(1, count)) for t in own_tables))
    live_rows, others = attention_inputs(seq_lengths, seq_devices, device)
    moe_in, residual, share, query, keyvalue, probs, small = attention_call(
        place, block_input, *others, dense
    )
    rows, cots = gather_whole(moe_in, count), gather_whole(packed, count)
    calls = [
        expert_call(0, small, tables, names, *rows[i : i + 8], *cots[i : i + 8])
        for i in range(0, len(rows), 8)
    ]
    back_pieces = sum_whole([b for call in calls for b in call[1]], count)
    outs = [call[0][j][ROWS * h : ROWS * (h + 1)] for call in calls for h in range(2) for j in range(4)]
    out_pieces = sum_whole(outs, count)
    received = permute(weight_grad_call([call[3] for call in calls]), swap_perm(1, count))
    expert_grads = weight_grad_call([call[2] for call in calls], received)
    residual_grad, grads = head_backward_call(
        place, (dense,), back_pieces,
        (moe_in, residual, packed, small, share, query, keyvalue, probs, *others[:2]),
    )
    terms = jnp.stack(dense_grad_call(BLOCKS, place, (share, grads))).astype(F32)
    wholes = [terms[:, PART * i : PART * (i + 1)].reshape(MODEL, MODEL) for i in range(3)]
    wholes.append(small_columns(terms[:, 3 * PART :]).reshape(MODEL, 128))
    query_grad, keyvalue_grad, output_weight_grad, small_grad = [
        lax.psum_scatter(w, "fsdp", scatter_dimension=0, tiled=True) for w in wholes
    ]
    input_grad = input_grad_call(place, sequences, (dense,), grads, residual_grad, small, block_input)
    block_output, attn_gain_grad = finish(
        live_rows, residual, out_pieces, attn_gain, (query_weight, keyvalue_weight),
        (query_grad, keyvalue_grad),
    )
    return (
        block_output,
        input_grad,
        attn_gain_grad,
        query_grad,
        keyvalue_grad,
        output_weight_grad,
        small_grad[:, EXPERT_COUNT + 1],
        small_grad[:, :EXPERT_COUNT],
        *expert_grads,
    )


def body(*inputs):
    device = lax.axis_index("fsdp").astype(jnp.int32)
    count = lax.axis_size("fsdp")
    return body_on_slice(device, inputs) if count == 32 else body_elsewhere(device, count, inputs)


def solution(mesh):
    placed = (
        P("fsdp", None),
        P(),
        P(),
        P("fsdp", None),
        P("fsdp"),
        P("fsdp", None),
        P("fsdp", None),
        P("fsdp", None),
        P("fsdp"),
        P("fsdp", None),
        P("fsdp", None),
        P("fsdp", None),
        P("fsdp", None),
        P("fsdp", None),
    )
    return jax.shard_map(
        body,
        mesh=mesh,
        in_specs=placed,
        out_specs=(
            P("fsdp", None),
            P("fsdp", None),
            P("fsdp"),
            P("fsdp", None),
            P("fsdp", None),
            P("fsdp", None),
            P("fsdp"),
            P("fsdp", None),
            P("fsdp", None),
            P("fsdp", None),
            P("fsdp", None),
        ),
        check_vma=False,
    )
```
